32 devices in a mesh: seq: 2 (over x), fsdp: 16 (over z, y, core).
Axes of the slice: x: 2, y: 2, z: 4, core: 2. Of those that a mesh axis runs over, the one named last changes fastest.
Arguments:
- hidden_in: bfloat16 [16, 2, 192, 2560], P('fsdp', 'seq'), may hold values from -6 to 6
- cotangent: bfloat16 [16, 2, 192, 2560], P('fsdp', 'seq'), may hold values from -6 to 6
- lengths: int32 [2, 3], replicated, may hold values from 1 to 2560, 3072 in all within a row
- weight_qkv: float32 [2560, 3072], P('fsdp'), may hold values from -0.125 to 0.125
- first_qkv: float32 [2560, 3072], P('fsdp'), may hold values from -160 to 160
- second_qkv: float32 [2560, 3072], P('fsdp'), may hold values from 2764.8 to 11059.2
- weight_out: float32 [2560, 2560], P('fsdp'), may hold values from -2 to 2
- first_out: float32 [2560, 2560], P('fsdp'), may hold values from -6 to 6
- second_out: float32 [2560, 2560], P('fsdp'), may hold values from 1.50528 to 6.02112
- weight_mlp: float32 [2560, 3, 7680], P('fsdp'), may hold values from -0.125 to 0.125
- first_mlp: float32 [2560, 3, 7680], P('fsdp'), may hold values from -32 to 32
- second_mlp: float32 [2560, 3, 7680], P('fsdp'), may hold values from 110.592 to 442.368
- norm_gains: float32 [2560, 2], P('fsdp'), may hold values from 0.5 to 1.5
- first_gains: float32 [2560, 2], P('fsdp'), may hold values from -128 to 128
- second_gains: float32 [2560, 2], P('fsdp'), may hold values from 1904.64 to 7680
Outputs:
- hidden_out: bfloat16 [16, 2, 192, 2560], P('fsdp', 'seq')
- hidden_grad: float32 [16, 2, 192, 2560], P('fsdp', 'seq')
- grad_qkv: float32 [2560, 3072], P('fsdp')
- new_second_qkv: float32 [2560, 3072], P('fsdp')
- new_qkv: float32 [2560, 3072], P('fsdp')
- grad_out: float32 [2560, 2560], P('fsdp')
- new_second_out: float32 [2560, 2560], P('fsdp')
- new_out: float32 [2560, 2560], P('fsdp')
- grad_mlp: float32 [2560, 3, 7680], P('fsdp')
- new_second_mlp: float32 [2560, 3, 7680], P('fsdp')
- new_mlp: float32 [2560, 3, 7680], P('fsdp')
- grad_gains: float32 [2560, 2], P('fsdp')
- new_second_gains: float32 [2560, 2], P('fsdp')
- new_gains: float32 [2560, 2], P('fsdp')
The draws below stay inside these ranges and needn't reach their ends.
Inputs may be any that keep to these rules, and one draw needn't show every extreme that they name: Each row holds the lengths of 3 documents packed in order into one sequence of 3072 tokens; a row sums to 3072 and its longest document has exactly 2560 tokens.
All inputs are finite; a program needn't handle non-finite values.
Results may differ from the reference program's by a relative error of at most 0.02.
Values may be sent and summed in bfloat16 or wider, within the bound.
No kernel may reach another device: no remote copies, remote signals or barrier semaphores. Data moves between devices by JAX's collectives and lax.ppermute only.
A program may use at most 648 MiB of HBM per device.

```python
import math
import jax
import jax.numpy as jnp
import numpy as np
from jax import lax

D = 2560
HEADS = 10
HEAD_DIM = 256
FF = 7680
WINDOW = 2048
TOK_DEV = 192
DOCS = 3
STEP = 10
SEQ_LEN = 3072
LONGEST = 2560
SEQS = 2
TOKENS = 6144
N_SEQ = 2
N_FSDP = 16


def block_levels(key, dims, pieces, low, top_value):
    loudness, own = 1.0, jax.random.fold_in(key, 6)
    for position, blocks in pieces:
        heights = jnp.exp(jax.random.uniform(jax.random.fold_in(own, position), (blocks,), jnp.float32, low / len(pieces), top_value / len(pieces)))
        loudness = loudness * jnp.repeat(heights, dims[position] // blocks).reshape([-1 if axis == position else 1 for axis in range(len(dims))])
    return loudness


def split_up(count, total, limit, slope):
    portions = [(1 << 20) // math.isqrt(rank ** slope) + 1 for rank in range(2, count + 1)]
    surplus, counts = total - limit - (count - 1), [1] * (count - 1)
    while surplus > 0:
        candidates = [i for i in range(count - 1) if counts[i] < limit]
        mass, budget = sum([portions[i] for i in candidates]), surplus
        for i in candidates:
            more = min(limit - counts[i], max(1, budget * portions[i] // mass), surplus)
            counts[i] = counts[i] + more
            surplus = surplus - more
    return np.array([limit] + counts)


def uneven_parts(key, count, total, bound, lean):
    if count == 2:
        one = jax.random.randint(key, (), max(1, total - bound), min(bound, total - 1) + 1)
        return jnp.stack([one, total - one])
    sizes = jnp.asarray(split_up(count, total, bound, lean), jnp.int32)
    twos = (count - 1) // 2
    donor, sink = sizes[1:1 + 2 * twos:2], sizes[2:2 + 2 * twos:2]
    slack = jnp.minimum(donor - 1, bound - sink)
    shifted = jax.random.randint(jax.random.fold_in(key, 1), (twos,), 0, 1 << 20) % (slack + 1)
    sizes = sizes.at[1:1 + 2 * twos:2].set(donor - shifted).at[2:2 + 2 * twos:2].set(sink + shifted)
    return sizes[jax.random.permutation(jax.random.fold_in(key, 2), count)]


def scatter_about(key, extent, spread, most, pieces=(), held_as=jnp.bfloat16):
    drawn = spread * jax.random.normal(key, extent, jnp.float32)
    if pieces:
        drawn = drawn * block_levels(key, extent, pieces, -0.22, 0.18)
    return jnp.clip(drawn, -most, most).astype(held_as)


def setup_inputs(seed: int = 0) -> dict:
    streams_of = jax.random.split(jax.random.key(seed), 16)
    hidden_in = scatter_about(streams_of[0], (N_FSDP, N_SEQ, TOK_DEV, D), 1.0, 6.0, ((0, 16), (1, 2)))
    cotangent = scatter_about(streams_of[1], (N_FSDP, N_SEQ, TOK_DEV, D), 1.0, 6.0, ((0, 16), (1, 2)))
    lengths = jax.vmap(lambda own: uneven_parts(own, DOCS, SEQ_LEN, LONGEST, 2))(jax.random.split(streams_of[2], SEQS)).reshape((SEQS, DOCS)).astype(jnp.int32)
    weight_qkv = scatter_about(streams_of[3], (D, D + 2 * HEAD_DIM), D ** -0.5, 0.125, ((0, 16),), jnp.float32)
    first_qkv = scatter_about(streams_of[4], (D, D + 2 * HEAD_DIM), (0.33 * TOKENS ** 0.5), 160.0, ((0, 16),), jnp.float32)
    second_qkv = jnp.clip(jnp.exp(math.log(11059.2) - 1.3862944 * jax.random.uniform(streams_of[5], (D, D + 2 * HEAD_DIM), jnp.float32) ** block_levels(streams_of[5], (D, D + 2 * HEAD_DIM), ((0, 16),), -0.2, 0.2)), 2764.8, 11059.2)
    weight_out = scatter_about(streams_of[6], (D, D), (max(1, 6 * D // WINDOW)) ** -0.5, 2.0, ((0, 16),), jnp.float32)
    first_out = scatter_about(streams_of[7], (D, D), (0.0077 * TOKENS ** 0.5), 6.0, ((0, 16),), jnp.float32)
    second_out = jnp.clip(jnp.exp(math.log(6.02112) - 1.3862944 * jax.random.uniform(streams_of[8], (D, D), jnp.float32) ** block_levels(streams_of[8], (D, D), ((0, 16),), -0.2, 0.2)), 1.50528, 6.02112)
    weight_mlp = scatter_about(streams_of[9], (D, 3, FF), D ** -0.5, 0.125, ((0, 16),), jnp.float32)
    first_mlp = scatter_about(streams_of[10], (D, 3, FF), (0.066 * TOKENS ** 0.5), 32.0, ((0, 16),), jnp.float32)
    second_mlp = jnp.clip(jnp.exp(math.log(442.368) - 1.3862944 * jax.random.uniform(streams_of[11], (D, 3, FF), jnp.float32) ** block_levels(streams_of[11], (D, 3, FF), ((0, 16),), -0.2, 0.2)), 110.592, 442.368)
    norm_gains = jnp.clip(1.0 + 0.1 * jax.random.normal(streams_of[12], (D, 2), jnp.float32), 0.5, 1.5)
    first_gains = scatter_about(streams_of[13], (D, 2), (0.275 * TOKENS ** 0.5), 128.0, ((0, 16),), jnp.float32)
    second_gains = jnp.clip(jnp.exp(math.log(7680.0) - 1.39432653 * jax.random.uniform(streams_of[14], (D, 2), jnp.float32) ** block_levels(streams_of[14], (D, 2), ((0, 16),), -0.2, 0.2)), 1904.64, 7680.0)
    return {"hidden_in": hidden_in, "cotangent": cotangent, "lengths": lengths, "weight_qkv": weight_qkv, "first_qkv": first_qkv, "second_qkv": second_qkv, "weight_out": weight_out, "first_out": first_out, "second_out": second_out, "weight_mlp": weight_mlp, "first_mlp": first_mlp, "second_mlp": second_mlp, "norm_gains": norm_gains, "first_gains": first_gains, "second_gains": second_gains}


@jax.custom_vjp
def low(v):
    return lax.optimization_barrier(v.astype(jnp.bfloat16)).astype(jnp.float32)

@jax.custom_vjp
def low_back(v):
    return v

def low_keep(v):
    return (low(v), None)

def low_pass(kept, grad):
    return (grad,)

def back_keep(v):
    return (v, None)

def back_low(kept, grad):
    return (low(grad),)
low.defvjp(low_keep, low_pass)
low_back.defvjp(back_keep, back_low)
NORM_EPS = 1e-06
BETA_ONE = 0.9
BETA_TWO = 0.95
ADAM_EPS = 1e-08
DECAY_RATE = 0.1
MASKED_SCORE = -1e+30
HIGHEST = lax.Precision.HIGHEST

def rms_norm(values, gain):
    factor = lax.rsqrt(lax.optimization_barrier(jnp.mean(values * values, axis=-1, keepdims=True)) + NORM_EPS)
    return values * factor * gain

def rotate(values, cosine, sine):
    half_dim = values.shape[-1] // 2
    first_half = values[..., :half_dim]
    second_half = values[..., half_dim:]
    return jnp.concatenate([first_half * cosine - second_half * sine, second_half * cosine + first_half * sine], axis=-1)

def doc_places(lengths_row, offsets):
    doc_ends = jnp.cumsum(lengths_row).astype(jnp.int32)
    passed = (doc_ends[None, :] <= offsets[:, None]).astype(jnp.int32)
    document = lax.optimization_barrier(jnp.sum(passed, axis=1)).astype(jnp.int32)
    starts = lax.optimization_barrier(jnp.sum(passed * lengths_row[None, :], axis=1)).astype(jnp.int32)
    return (document, offsets - starts)

def rope_angles(places, head_dim):
    freq_index = jnp.arange(head_dim // 2, dtype=jnp.float32)
    inverse = jnp.exp(freq_index * (-2.0 * math.log(10000.0) / head_dim))
    angles = places.astype(jnp.float32)[:, None] * inverse[None, :]
    return (jnp.cos(angles), jnp.sin(angles))

def adam_step(weight, first, second, grad, rate):
    first_new = BETA_ONE * first + (1.0 - BETA_ONE) * grad
    second_new = BETA_TWO * second + (1.0 - BETA_TWO) * grad * grad
    first_hat = first_new / (1.0 - BETA_ONE ** STEP)
    second_hat = second_new / (1.0 - BETA_TWO ** STEP)
    update = first_hat / (jnp.sqrt(second_hat) + ADAM_EPS)
    return (second_new, weight - rate * (update + DECAY_RATE * weight))

def attend_packed(packed):
    queries, keys_rot, values_low, documents, places = packed
    block_rows = 512 if SEQ_LEN % 512 == 0 else SEQ_LEN
    block_count = SEQ_LEN // block_rows

    def attend_block(block):
        query_block, block_docs, block_places = block
        scores = low_back(jnp.einsum('thd,kd->thk', query_block, keys_rot, precision=HIGHEST))
        distance = block_places[:, None] - places[None, :]
        allowed = (block_docs[:, None] == documents[None, :]) & (distance >= 0) & (distance < WINDOW)
        scores = jnp.where(allowed[:, None, :], scores, MASKED_SCORE)
        probs = jax.nn.softmax(scores, axis=-1)
        mixed = jnp.einsum('thk,kd->thd', low(probs), values_low, precision=HIGHEST)
        return low_back(low(mixed))
    blocks = (queries.reshape(block_count, block_rows, HEADS, HEAD_DIM), documents.reshape(block_count, block_rows), places.reshape(block_count, block_rows))
    mixed_all = lax.map(jax.checkpoint(attend_block), blocks)
    return mixed_all.reshape(SEQ_LEN, HEADS, HEAD_DIM)

def forward(tokens, weight_qkv, weight_out, norm_gains, weight_mlp, cosine, sine, documents, places):
    gains_low = low(norm_gains)
    normed = low(rms_norm(tokens, gains_low[:, 0]))
    projected = jnp.dot(normed, low(weight_qkv), precision=HIGHEST)
    query_pre = low_back(projected[:, :D])
    key_pre = low_back(projected[:, D:D + HEAD_DIM])
    value_low = low_back(low(projected[:, D + HEAD_DIM:]))
    queries = low(rotate(query_pre.reshape(TOKENS, HEADS, HEAD_DIM), cosine[:, None, :], sine[:, None, :]) * HEAD_DIM ** (-0.5))
    keys_rot = low(rotate(key_pre, cosine, sine))
    packed = (queries.reshape(SEQS, SEQ_LEN, HEADS, HEAD_DIM), keys_rot.reshape(SEQS, SEQ_LEN, HEAD_DIM), value_low.reshape(SEQS, SEQ_LEN, HEAD_DIM), documents, places)
    mixed = lax.map(jax.checkpoint(attend_packed), packed)
    attn_low = mixed.reshape(TOKENS, D)
    branch = low_back(jnp.dot(attn_low, low(weight_out), precision=HIGHEST))
    middle = tokens + branch
    normed_two = low(rms_norm(middle, gains_low[:, 1]))
    mlp_low = low(weight_mlp)
    gate_pre = low_back(jnp.dot(normed_two, mlp_low[:, 0, :], precision=HIGHEST))
    upward = low_back(jnp.dot(normed_two, mlp_low[:, 1, :], precision=HIGHEST))
    activated = low_back(low(jax.nn.gelu(gate_pre, approximate=True) * upward))
    output_branch = low_back(jnp.dot(activated, mlp_low[:, 2, :].T, precision=HIGHEST))
    return middle + output_branch

def reference(hidden_in, cotangent, lengths, weight_qkv, first_qkv, second_qkv, weight_out, first_out, second_out, weight_mlp, first_mlp, second_mlp, norm_gains, first_gains, second_gains):
    tokens = hidden_in.reshape(TOKENS, D).astype(jnp.float32)
    incoming = cotangent.reshape(TOKENS, D).astype(jnp.float32)
    offsets = jnp.arange(SEQ_LEN, dtype=jnp.int32)
    documents, places = jax.vmap(lambda lengths_row: doc_places(lengths_row, offsets))(lengths)
    cosine, sine = rope_angles(places.reshape(TOKENS), HEAD_DIM)

    def closed(tokens_in, qkv_in, out_in, gains_in, mlp_in):
        return forward(tokens_in, qkv_in, out_in, gains_in, mlp_in, cosine, sine, documents, places)
    result, pullback = jax.vjp(closed, tokens, weight_qkv, weight_out, norm_gains, weight_mlp)
    grad_tokens, grad_qkv, grad_out, grad_gains, grad_mlp = pullback(incoming)
    rate_main = 2.0 * D ** (-0.5)
    rate_out = 2.0 * max(1, 6 * D // WINDOW) ** (-0.5)
    rate_gains = 0.4
    second_new_qkv, new_qkv = adam_step(weight_qkv, first_qkv, second_qkv, grad_qkv, rate_main)
    second_new_out, new_out = adam_step(weight_out, first_out, second_out, grad_out, rate_out)
    second_new_mlp, new_mlp = adam_step(weight_mlp, first_mlp, second_mlp, grad_mlp, rate_main)
    second_new_gains, new_gains = adam_step(norm_gains, first_gains, second_gains, grad_gains, rate_gains)
    hidden_out = result.astype(jnp.bfloat16).reshape(N_FSDP, N_SEQ, TOK_DEV, D)
    hidden_grad = grad_tokens.reshape(N_FSDP, N_SEQ, TOK_DEV, D)
    return (hidden_out, hidden_grad, grad_qkv, second_new_qkv, new_qkv, grad_out, second_new_out, new_out, grad_mlp, second_new_mlp, new_mlp, grad_gains, second_new_gains, new_gains)
```

```python
import math

import jax
import jax.numpy as jnp
from jax import lax
from jax.experimental import pallas as pl
from jax.experimental.pallas import tpu as pltpu
from jax.sharding import Mesh, PartitionSpec as P

D = 2560
HEAD_DIM = 256
WINDOW = 2048
STEP = 10
SEQ_LEN = 3072

NORM_EPS = 1e-06
BETA_ONE = 0.9
BETA_TWO = 0.95
ADAM_EPS = 1e-08
DECAY_RATE = 0.1
MASKED_SCORE = -1e30

LANES = 512
KEY_BLOCK = 768
PLANES = ("g", "h")
OWNERS = ("g", "h", "k", "c")
CHIPS = ("seq", "k")
GROUP = ("seq", "k", "c")
RING = ("seq", "h", "k")
EVERY = ("seq", "g", "h", "k", "c")


def rotate(values, cosine, sine):
    half_dim = values.shape[-1] // 2
    first_half = values[..., :half_dim]
    second_half = values[..., half_dim:]
    return jnp.concatenate(
        [first_half * cosine - second_half * sine, second_half * cosine + first_half * sine],
        axis=-1,
    )


def doc_places(lengths_row, offsets):
    doc_ends = jnp.cumsum(lengths_row)
    passed = (doc_ends[None, :] <= offsets[:, None]).astype(jnp.int32)
    document = jnp.sum(passed, axis=1)
    starts = jnp.sum(passed * lengths_row[None, :], axis=1)
    return (document, offsets - starts)


def rope_angles(places, head_dim):
    freq_index = jnp.arange(head_dim // 2, dtype=jnp.float32)
    inverse = jnp.exp(freq_index * (-2.0 * math.log(10000.0) / head_dim))
    angles = places.astype(jnp.float32)[:, None] * inverse[None, :]
    return (jnp.cos(angles), jnp.sin(angles))


def adam_step(weight, first, second, grad, rate):
    first_new = BETA_ONE * first + (1.0 - BETA_ONE) * grad
    second_new = BETA_TWO * second + (1.0 - BETA_TWO) * grad * grad
    first_hat = first_new / (1.0 - BETA_ONE**STEP)
    second_hat = second_new / (1.0 - BETA_TWO**STEP)
    update = first_hat / (jnp.sqrt(second_hat) + ADAM_EPS)
    return (second_new, weight - rate * (update + DECAY_RATE * weight))


def glu_values(gate_in, up_in):
    return jax.nn.gelu(gate_in, approximate=True) * up_in


def low(value):
    return value.astype(jnp.bfloat16)


def wide(value):
    return value.astype(jnp.float32)


def dot(left, right, contract):
    return lax.dot_general(
        left, right, ((contract[:1], contract[1:]), ((), ())), preferred_element_type=jnp.float32
    )


def traded(axes, step):
    count = math.prod(lax.axis_size(axis) for axis in axes)
    return [(source, source ^ step) for source in range(count)]


def swapped(value, axis):
    return lax.ppermute(value, axis, [(0, 1), (1, 0)])


def after(value, *others):
    return lax.optimization_barrier((value,) + others)[0]


def doubled(value, axis, step, place):
    other = lax.ppermute(value, axis, traded((axis,), step))
    first = (lax.axis_index(axis) & step) == 0
    return jnp.stack([jnp.where(first, value, other), jnp.where(first, other, value)], axis=place)


def next_plane(block):
    count = math.prod(lax.axis_size(axis) for axis in PLANES)
    return lax.ppermute(block, PLANES, [(one, (one + 1) % count) for one in range(count)])


def joined_planes(blocks):
    count, rows = len(blocks), blocks[0].shape[0]
    whole = jnp.zeros((count * rows, blocks[0].shape[1]), blocks[0].dtype)
    for step, block in enumerate(blocks):
        start = lax.rem(lax.axis_index(PLANES) + (count - step), count) * rows
        whole = lax.dynamic_update_slice_in_dim(whole, block, start, 0)
    return whole


def spread_ring(value):
    chips = math.prod(lax.axis_size(axis) for axis in RING)
    place = lax.axis_index(RING)
    whole = jnp.zeros((chips,) + value.shape, value.dtype)
    for step in range(chips):
        arrived = lax.ppermute(value, RING, traded(RING, step)) if step else value
        whole = lax.dynamic_update_index_in_dim(whole, arrived, place ^ step, 0)
    return whole


def ring_sum(terms):
    chips = terms.shape[0]
    place = lax.axis_index(CHIPS)
    total = 0.0
    for step in range(chips):
        term = lax.dynamic_index_in_dim(terms, place ^ step, 0, keepdims=False)
        if step:
            term = lax.ppermute(term, CHIPS, traded(CHIPS, step))
        total = total + wide(term)
    return total


def exchanged(value, axes):
    return lax.all_to_all(value, axes, split_axis=0, concat_axis=0, tiled=True)


def half_sum(terms, axis, place):
    here = lax.axis_index(axis)
    kept = lax.dynamic_index_in_dim(terms, here, place, keepdims=False)
    given = lax.dynamic_index_in_dim(terms, 1 - here, place, keepdims=False)
    return low(wide(kept) + wide(swapped(given, axis)))


def mlp_chunks_kernel(slices, side_ref, weight_ref, gain_ref, gate_up_ref, down_ref):
    per_piece = pl.num_programs(1)
    index = side_ref[0] * pl.num_programs(0) + pl.program_id(0)
    index = index * per_piece + pl.program_id(1)
    width = weight_ref.shape[2]
    lane = pl.program_id(1) * width
    gain = gain_ref[...]
    for part in range(3):
        weight = wide(low(weight_ref[part]))
        if part < 2:
            weight = weight * gain
        weight = low(jnp.where(index < slices, weight, 0.0))
        if part < 2:
            place = pl.multiple_of(part * per_piece * width + lane, width)
            gate_up_ref[0, :, pl.ds(place, width)] = weight
        else:
            down_ref[0, :, pl.ds(pl.multiple_of(lane, width), width)] = weight


def mlp_chunks(weight, gain, side, members, piece):
    parts, rows, ff_width = weight.shape
    slices = ff_width // LANES
    per_piece = piece // LANES

    def weight_block(m, b, side_ref):
        return (0, 0, jnp.minimum((side_ref[0] * members + m) * per_piece + b, slices - 1))

    def out_block(m, b, side_ref):
        return (m, 0, 0)

    return pl.pallas_call(
        lambda *refs: mlp_chunks_kernel(slices, *refs),
        grid_spec=pltpu.PrefetchScalarGridSpec(
            num_scalar_prefetch=1,
            grid=(members, per_piece),
            in_specs=[
                pl.BlockSpec((parts, rows, LANES), weight_block),
                pl.BlockSpec((rows, 1), lambda m, b, side_ref: (0, 0)),
            ],
            out_specs=[
                pl.BlockSpec((1, rows, 2 * piece), out_block),
                pl.BlockSpec((1, rows, piece), out_block),
            ],
        ),
        out_shape=[
            jax.ShapeDtypeStruct((members, rows, 2 * piece), jnp.bfloat16),
            jax.ShapeDtypeStruct((members, rows, piece), jnp.bfloat16),
        ],
        compiler_params=pltpu.CompilerParams(vmem_limit_bytes=48 * 1024 * 1024),
        cost_estimate=pl.CostEstimate(
            flops=weight.size, bytes_accessed=3 * weight.size, transcendentals=0
        ),
        name="mlp_chunks",
    )(jnp.full((1,), side, jnp.int32), weight, gain)


def mlp_adam_kernel(rate, per_side, scaled, side_ref, ours_ref, theirs_ref, weight_ref, first_ref,
                    second_ref, gain_ref, *refs):
    grad_out, second_out, weight_out, dot_out = refs[-4:]
    block = pl.program_id(0)
    ours = block // per_side == side_ref[0]
    grad = wide(jnp.where(ours, ours_ref[0], theirs_ref[0]))
    weight = weight_ref[0]
    dot_part = jnp.sum(wide(low(weight)) * grad, axis=1, keepdims=True)
    dot_out[...] = jnp.where(block == 0, dot_part, dot_out[...] + dot_part)
    if scaled:
        grad = grad * gain_ref[...]
    grad_out[0] = grad
    second_out[0], weight_out[0] = adam_step(weight, first_ref[0], second_ref[0], grad, rate)


def mlp_adam(part, side, pieces, states, gain, rate, outs):
    _, rows, ff_width = states[0].shape
    members, _, piece = pieces[0].shape
    per_piece = piece // LANES
    per_side = members * per_piece

    def grad_block(own):
        def place(b, side_ref):
            used = (b // per_side == side_ref[0]) == own
            inner = jnp.where(used, b % per_side, 0)
            return (inner // per_piece, 0, inner % per_piece)

        return pl.BlockSpec((1, rows, LANES), place)

    state = pl.BlockSpec((1, rows, LANES), lambda b, side_ref: (part, 0, b))
    gains = pl.BlockSpec((rows, 1), lambda b, side_ref: (0, 0))
    size = rows * ff_width
    return pl.pallas_call(
        lambda *refs: mlp_adam_kernel(rate, per_side, part < 2, *refs),
        grid_spec=pltpu.PrefetchScalarGridSpec(
            num_scalar_prefetch=1,
            grid=(ff_width // LANES,),
            in_specs=[grad_block(True), grad_block(False), state, state, state, gains]
            + [pl.BlockSpec(memory_space=pl.ANY)] * len(outs),
            out_specs=[state, state, state, gains],
        ),
        out_shape=[jax.ShapeDtypeStruct(states[0].shape, jnp.float32)] * 3
        + [jax.ShapeDtypeStruct((rows, 1), jnp.float32)],
        input_output_aliases={7 + index: index for index in range(len(outs))},
        compiler_params=pltpu.CompilerParams(vmem_limit_bytes=48 * 1024 * 1024),
        cost_estimate=pl.CostEstimate(
            flops=20 * size, bytes_accessed=26 * size, transcendentals=size
        ),
        name="mlp_adam",
    )(jnp.full((1,), side, jnp.int32), *pieces, *states, gain, *outs)


def stacked_heads(ref):
    return jnp.concatenate([ref[:, :HEAD_DIM], ref[:, HEAD_DIM:]], axis=0)


def attend_kernel(query_ref, key_ref, value_t_ref, bias_ref, out_ref, lse_ref, score_ref):
    rows = query_ref.shape[0]
    queries = stacked_heads(query_ref)
    blocks = key_ref.shape[0] // KEY_BLOCK

    def first(block, top):
        part = pl.ds(pl.multiple_of(block * KEY_BLOCK, KEY_BLOCK), KEY_BLOCK)
        scores = dot(key_ref[part, :], queries, (1, 1)) + bias_ref[part, :]
        score_ref[part, :] = scores
        return jnp.maximum(top, jnp.max(scores, axis=0, keepdims=True))

    top = jnp.full((1, 2 * rows), -jnp.inf, jnp.float32)
    top = lax.fori_loop(0, blocks, first, top, unroll=2)

    def second(block, carry):
        total, mixed = carry
        part = pl.ds(pl.multiple_of(block * KEY_BLOCK, KEY_BLOCK), KEY_BLOCK)
        exps = jnp.exp(score_ref[part, :] - top)
        total = total + jnp.sum(exps, axis=0, keepdims=True)
        return total, mixed + dot(value_t_ref[:, part], low(exps), (1, 0))

    total, mixed = lax.fori_loop(
        0,
        blocks,
        second,
        (jnp.zeros((1, 2 * rows), jnp.float32), jnp.zeros((HEAD_DIM, 2 * rows), jnp.float32)),
        unroll=2,
    )
    mixed = low((mixed / total).T)
    out_ref[:, :HEAD_DIM] = mixed[:rows]
    out_ref[:, HEAD_DIM:] = mixed[rows:]
    lse_ref[0] = top + jnp.log(total)


def attend(queries, keys, values, bias):
    rows, width = queries.shape
    pairs = width // (2 * HEAD_DIM)
    count = keys.shape[0]

    def whole(shape):
        return pl.BlockSpec(shape, lambda p: (0,) * len(shape))

    pair = pl.BlockSpec((rows, 2 * HEAD_DIM), lambda p: (0, p))
    return pl.pallas_call(
        attend_kernel,
        grid=(pairs,),
        in_specs=[pair, whole(keys.shape), whole((HEAD_DIM, count)), whole(bias.shape)],
        out_specs=[pair, pl.BlockSpec((1, 1, 2 * rows), lambda p: (p, 0, 0))],
        out_shape=[
            jax.ShapeDtypeStruct((rows, width), jnp.bfloat16),
            jax.ShapeDtypeStruct((pairs, 1, 2 * rows), jnp.float32),
        ],
        scratch_shapes=[pltpu.VMEM((count, 2 * rows), jnp.float32)],
        compiler_params=pltpu.CompilerParams(vmem_limit_bytes=48 * 1024 * 1024),
        cost_estimate=pl.CostEstimate(
            flops=4 * rows * width * count,
            bytes_accessed=8 * rows * width + 12 * bias.size,
            transcendentals=pairs * bias.size,
        ),
        name="attend",
    )(queries, keys, values.T, bias)


def attend_back_kernel(query_ref, grad_ref, key_ref, key_t_ref, value_ref, bias_ref, lse_ref,
                       delta_ref, grad_query_ref, grad_window_ref):
    rows = query_ref.shape[0]
    queries = stacked_heads(query_ref)
    grads = stacked_heads(grad_ref)
    blocks = key_ref.shape[0] // KEY_BLOCK

    @pl.when(pl.program_id(0) == 0)
    def _():
        grad_window_ref[...] = jnp.zeros_like(grad_window_ref)

    lse = lse_ref[0]
    delta = delta_ref[0]

    def body(block, grad_query):
        part = pl.ds(pl.multiple_of(block * KEY_BLOCK, KEY_BLOCK), KEY_BLOCK)
        probs = jnp.exp(dot(key_ref[part, :], queries, (1, 1)) + bias_ref[part, :] - lse)
        grad_probs = dot(value_ref[part, :], grads, (1, 1))
        grad_scores = low(probs * (grad_probs - delta))
        grad_window_ref[part, :HEAD_DIM] += dot(grad_scores, queries, (1, 0))
        grad_window_ref[part, HEAD_DIM:] += dot(low(probs), grads, (1, 0))
        return grad_query + dot(key_t_ref[:, part], grad_scores, (1, 0))

    grad_query = jnp.zeros((HEAD_DIM, 2 * rows), jnp.float32)
    grad_query = lax.fori_loop(0, blocks, body, grad_query, unroll=2).T
    grad_query_ref[:, :HEAD_DIM] = grad_query[:rows]
    grad_query_ref[:, HEAD_DIM:] = grad_query[rows:]


def attend_back(queries, grads, keys, values, bias, lse, delta):
    rows, width = queries.shape
    pairs = width // (2 * HEAD_DIM)
    count = keys.shape[0]

    def whole(shape):
        return pl.BlockSpec(shape, lambda p: (0,) * len(shape))

    pair = pl.BlockSpec((rows, 2 * HEAD_DIM), lambda p: (0, p))
    line = pl.BlockSpec((1, 1, 2 * rows), lambda p: (p, 0, 0))
    return pl.pallas_call(
        attend_back_kernel,
        grid=(pairs,),
        in_specs=[
            pair,
            pair,
            whole(keys.shape),
            whole((HEAD_DIM, count)),
            whole(values.shape),
            whole(bias.shape),
            line,
            line,
        ],
        out_specs=[pair, whole((count, 2 * HEAD_DIM))],
        out_shape=[
            jax.ShapeDtypeStruct((rows, width), jnp.float32),
            jax.ShapeDtypeStruct((count, 2 * HEAD_DIM), jnp.float32),
        ],
        compiler_params=pltpu.CompilerParams(vmem_limit_bytes=48 * 1024 * 1024),
        cost_estimate=pl.CostEstimate(
            flops=10 * rows * width * count,
            bytes_accessed=8 * rows * width + 16 * bias.size,
            transcendentals=pairs * bias.size,
        ),
        name="attend_back",
    )(queries, grads, keys, keys.T, values, bias, lse, delta)


def on_device(
    hidden_in,
    cotangent,
    lengths,
    weight_qkv,
    first_qkv,
    second_qkv,
    weight_out,
    first_out,
    second_out,
    weight_mlp,
    first_mlp,
    second_mlp,
    norm_gains,
    first_gains,
    second_gains,
):
    tok_rows = hidden_in.shape[2]
    width = hidden_in.shape[3]
    head_count = width // HEAD_DIM
    sides = lax.axis_size("seq")
    columns = lax.axis_size("k")
    members = columns * lax.axis_size("c")
    planes = lax.axis_size("g") * lax.axis_size("h")
    owner_count = planes * members
    blocks_in_side = lax.axis_size("h") * members
    side = lax.axis_index("seq")
    core = lax.axis_index("c")
    packed_index = lax.axis_index("g")
    place = lax.axis_index(("h", "k", "c"))
    own_rows = weight_mlp.shape[0]
    ff_width = weight_mlp.shape[2]
    piece = -(-ff_width // (sides * members * LANES)) * LANES

    gains_low = wide(low(norm_gains))
    gain_one = gains_low[:, :1]
    gain_two = gains_low[:, 1:]
    qkv_low = wide(low(weight_qkv))
    def gathered(weight):
        half = weight.shape[1] // sides
        weight = lax.dynamic_slice_in_dim(weight, side * half, half, 1)
        whole = lax.all_gather(weight, EVERY, axis=0, tiled=True)
        return whole.reshape(sides, owner_count * own_rows, half)

    qkv_halves = gathered(low(qkv_low * gain_one))
    out_halves = gathered(low(weight_out))
    mlp_planes = weight_mlp.transpose(1, 0, 2)
    gate_up_chunks, down_chunks = mlp_chunks(mlp_planes, gain_two, side, members, piece)

    def to_members(chunks):
        return exchanged(chunks, ("k", "c")).reshape(members * own_rows, chunks.shape[2])

    incoming = cotangent.reshape(tok_rows, width)
    gate_up_blocks = [to_members(gate_up_chunks)]
    gate_up_blocks.append(next_plane(gate_up_blocks[0]))
    down_blocks = [to_members(down_chunks)]
    incoming_columns = doubled(incoming, "k", 1, 0)

    tokens = wide(hidden_in.reshape(tok_rows, width))
    lengths_row = lax.dynamic_index_in_dim(lengths, packed_index, 0, keepdims=False)
    row_numbers = jnp.arange(tok_rows, dtype=jnp.int32)
    query_docs, query_places = doc_places(
        lengths_row, (place * sides + side) * tok_rows + row_numbers
    )
    blocks = jnp.arange(blocks_in_side, dtype=jnp.int32)[None, :] * sides
    blocks = blocks + jnp.arange(sides, dtype=jnp.int32)[:, None]
    key_offsets = (blocks[:, :, None] * tok_rows + row_numbers).reshape(-1)
    key_docs, key_places = doc_places(lengths_row, key_offsets)
    distance = query_places[:, None] - key_places[None, :]
    allowed = (query_docs[:, None] == key_docs[None, :]) & (distance >= 0) & (distance < WINDOW)
    cosine, sine = rope_angles(query_places, HEAD_DIM)
    query_scale = HEAD_DIM ** (-0.5)

    factor_one = lax.rsqrt(jnp.mean(tokens * tokens, axis=-1, keepdims=True) + NORM_EPS)
    normed_one = low(tokens * factor_one)
    normed_one = after(normed_one, incoming_columns, gate_up_blocks[1], down_blocks[0])
    projected = jnp.concatenate([dot(normed_one, half, (1, 0)) for half in qkv_halves], axis=1)
    key_pre = projected[:, width : width + HEAD_DIM]
    value_low = low(projected[:, width + HEAD_DIM :])
    key_low = low(rotate(key_pre, cosine, sine))
    window_kv = spread_ring(jnp.concatenate([key_low, value_low], axis=1))
    window_kv = doubled(window_kv, "c", 1, 1)
    window_kv = window_kv.reshape(SEQ_LEN, 2 * HEAD_DIM)
    gate_up_blocks.append(next_plane(after(gate_up_blocks[1], window_kv)))
    for _ in range(planes - 3):
        gate_up_blocks.append(next_plane(gate_up_blocks[-1]))
    down_blocks.append(next_plane(after(down_blocks[0], window_kv)))
    for _ in range(planes - 2):
        down_blocks.append(next_plane(down_blocks[-1]))
    gate_up_own = joined_planes(gate_up_blocks)
    down_own = joined_planes(down_blocks)
    incoming_sides = doubled(after(incoming_columns, window_kv), "seq", 1, 0)
    query_pre = projected[:, :width].reshape(tok_rows, head_count, HEAD_DIM)
    queries = low(rotate(query_pre, cosine[:, None, :], sine[:, None, :]) * query_scale)
    queries = queries.reshape(tok_rows, width)
    incoming_all = doubled(incoming_sides, "c", 1, incoming_sides.ndim - 2)
    incoming_all = incoming_all.reshape(sides * members * tok_rows, width)
    keys_win = window_kv[:, :HEAD_DIM]
    values_win = window_kv[:, HEAD_DIM:]
    bias = jnp.where(allowed.T, 0.0, MASKED_SCORE)
    bias = jnp.concatenate([bias, bias], axis=1)
    attn_low, log_total = attend(queries, keys_win, values_win, bias)
    attn_low = after(attn_low, gate_up_blocks[2], down_blocks[1], incoming_sides)
    branch = [dot(attn_low, half, (1, 0)) for half in out_halves]
    middle = tokens + jnp.concatenate(branch, axis=1)

    factor_two = lax.rsqrt(jnp.mean(middle * middle, axis=-1, keepdims=True) + NORM_EPS)
    normed_two = low(middle * factor_two)
    normed_two_all = lax.all_gather(normed_two, GROUP, axis=0, tiled=True)
    grad_act = low(dot(incoming_all, down_own, (1, 0)))
    gate_up = dot(normed_two_all, gate_up_own, (1, 0))
    activated, glu_back = jax.vjp(glu_values, gate_up[:, :piece], gate_up[:, piece:])
    activated_low = low(activated)
    attn_all = lax.all_gather(after(attn_low, normed_two_all), GROUP, axis=0, tiled=True)
    normed_one_all = lax.all_gather(after(normed_one, normed_two_all), GROUP, axis=0, tiled=True)
    grad_gate, grad_up = glu_back(wide(grad_act))
    grad_gate_up = low(jnp.concatenate([grad_gate, grad_up], axis=1))
    def to_owners(term):
        return lax.psum_scatter(term, PLANES, scatter_dimension=0, tiled=True)

    def in_plane(term, *others):
        term = term.reshape(members, own_rows, term.shape[1])
        ours = exchanged(after(term, *others), ("k", "c"))
        return (ours, swapped(ours, "seq"))

    by_core = grad_gate_up.reshape(sides * columns, 2, tok_rows, 2 * piece)

    def core_term(which):
        rows = lax.dynamic_index_in_dim(by_core, which, 1, keepdims=False)
        return dot(rows.reshape(-1, 2 * piece), gate_up_own, (1, 1))

    given = swapped(low(core_term(1 - core)), "c")
    terms = low(core_term(core) + wide(given)).reshape(sides * columns, tok_rows, width)
    half = width // sides
    first, second = terms[:, :, :half], terms[:, :, half:]
    down_term = low(dot(incoming_all, after(activated_low, terms), (0, 0)))
    down_term = after(down_term, attn_all, normed_one_all)
    first = exchanged(first, CHIPS)
    late = after(grad_gate_up, first)
    gate_term = low(dot(normed_two_all, late[:, :piece], (0, 0)))
    second = exchanged(after(second, first), CHIPS)
    up_term = low(dot(normed_two_all, late[:, piece:], (0, 0)))
    branch = low(dot(after(activated_low, first), down_own, (1, 1)))
    grad_normed_two = jnp.sum(wide(jnp.concatenate([first, second], axis=2)), axis=0)
    grad_normed_two = after(grad_normed_two, gate_term, up_term, branch)

    down_rows = to_owners(down_term)
    gate_rows = to_owners(gate_term)
    up_rows = to_owners(up_term)
    down_pieces = in_plane(down_rows)
    grad_middle = (
        wide(incoming)
        + factor_two * grad_normed_two
        - middle * factor_two**3 * jnp.mean(grad_normed_two * middle, axis=-1, keepdims=True)
    )

    grad_branch_low = low(grad_middle)
    half = width // sides
    grad_mixed = sum(
        dot(grad_branch_low[:, index * half : (index + 1) * half], out_halves[index], (1, 1))
        for index in range(sides)
    )
    grad_mixed_low = low(grad_mixed)
    delta = (wide(grad_mixed_low) * wide(attn_low)).reshape(tok_rows, head_count, HEAD_DIM)
    delta = jnp.sum(delta, axis=-1).T.reshape(log_total.shape)
    grad_query, grad_window = attend_back(
        queries, grad_mixed_low, keys_win, values_win, bias, log_total, delta
    )
    grad_window = after(low(grad_window), down_pieces[0])
    branch = lax.psum_scatter(
        after(branch, grad_window), GROUP, scatter_dimension=0, tiled=True
    )
    grad_window = half_sum(grad_window.reshape(-1, 2, tok_rows, 2 * HEAD_DIM), "c", 1)
    grad_window = grad_window.reshape(sides, -1, columns, tok_rows, 2 * HEAD_DIM)
    grad_window = half_sum(grad_window, "h", 1).reshape(-1, tok_rows, 2 * HEAD_DIM)
    grad_local = ring_sum(grad_window)
    grad_query = grad_query.reshape(tok_rows, head_count, HEAD_DIM)
    grad_query_pre = rotate(
        grad_query * query_scale, cosine[:, None, :], -sine[:, None, :]
    ).reshape(tok_rows, width)
    grad_key_pre = rotate(grad_local[:, :HEAD_DIM], cosine, -sine)
    grad_proj = low(
        jnp.concatenate([grad_query_pre, grad_key_pre, grad_local[:, HEAD_DIM:]], axis=1)
    )

    grad_proj = after(grad_proj, down_pieces[1])

    shares = sides * members

    def by_column(terms):
        terms = terms.reshape(tok_rows, shares, terms.shape[1] // shares).transpose(1, 0, 2)
        return exchanged(terms, GROUP).reshape(shares * tok_rows, -1)

    def to_rows(total):
        total = exchanged(total.reshape(owner_count, own_rows, -1), OWNERS)
        return low(jnp.sum(wide(total.reshape(planes, members, own_rows, -1)), axis=0))

    def joined(total):
        total = doubled(total, "seq", 1, 0).reshape(shares, own_rows, -1)
        return wide(total.transpose(1, 0, 2).reshape(own_rows, -1))

    out_columns = by_column(grad_branch_low)
    qkv_columns = by_column(grad_proj)
    out_total = after(low(dot(attn_all, out_columns, (0, 0))), qkv_columns)
    qkv_total = low(dot(normed_one_all, qkv_columns, (0, 0)))
    out_total = to_rows(out_total)
    gate_pieces = in_plane(gate_rows, qkv_columns)
    up_pieces = in_plane(up_rows, gate_pieces[0])
    grad_out = joined(out_total)
    qkv_total = to_rows(after(qkv_total, out_total, up_pieces[0]))

    mlp_states = (mlp_planes, first_mlp.transpose(1, 0, 2), second_mlp.transpose(1, 0, 2))
    mlp_outs = ()
    gain_dots = {}
    rate_main = 2.0 * D ** (-0.5)
    for part, pieces in ((2, down_pieces), (0, gate_pieces), (1, up_pieces)):
        if part == 1:
            qkv_total = after(qkv_total, *mlp_outs)
        *mlp_outs, gain_dots[part] = mlp_adam(
            part, side, pieces, mlp_states, gain_two, rate_main, mlp_outs
        )
    grad_mlp, second_new_mlp, new_mlp = mlp_outs
    grad_gain_two = gain_dots[0] + gain_dots[1]
    grad_qkv = joined(qkv_total)
    hidden_out = low(middle + wide(after(branch, grad_qkv))).reshape(1, 1, tok_rows, width)

    half = grad_proj.shape[1] // sides
    grad_normed = sum(
        dot(grad_proj[:, index * half : (index + 1) * half], qkv_halves[index], (1, 1))
        for index in range(sides)
    )
    hidden_grad = (
        grad_middle
        + factor_one * grad_normed
        - tokens * factor_one**3 * jnp.mean(grad_normed * tokens, axis=-1, keepdims=True)
    ).reshape(1, 1, tok_rows, width)

    rate_out = 2.0 * max(1, 6 * D // WINDOW) ** (-0.5)
    rate_gains = 0.4
    grad_gain_one = jnp.sum(qkv_low * grad_qkv, axis=1, keepdims=True)
    grad_qkv = grad_qkv * gain_one
    second_new_qkv, new_qkv = adam_step(weight_qkv, first_qkv, second_qkv, grad_qkv, rate_main)
    second_new_out, new_out = adam_step(weight_out, first_out, second_out, grad_out, rate_out)
    grad_gains = jnp.concatenate([grad_gain_one, grad_gain_two], axis=1)
    second_new_gains, new_gains = adam_step(
        norm_gains, first_gains, second_gains, grad_gains, rate_gains
    )
    return (
        hidden_out,
        hidden_grad,
        grad_qkv,
        second_new_qkv,
        new_qkv,
        grad_out,
        second_new_out,
        new_out,
        grad_mlp.transpose(1, 0, 2),
        second_new_mlp.transpose(1, 0, 2),
        new_mlp.transpose(1, 0, 2),
        grad_gains,
        second_new_gains,
        new_gains,
    )


def solution(mesh):
    seq_count, owner_count = mesh.devices.shape

    def whole(*arguments):
        members = SEQ_LEN // (seq_count * arguments[0].shape[2])
        shape = (seq_count, owner_count // members, members // 4, 2, 2)
        split = Mesh(mesh.devices.reshape(shape), ("seq", "g", "h", "k", "c"))
        acts = P(OWNERS, "seq", None, None)
        flat = P(OWNERS, None)
        planes = P(OWNERS, None, None)
        return jax.shard_map(
            on_device,
            mesh=split,
            in_specs=(acts, acts, P()) + (flat,) * 6 + (planes,) * 3 + (flat,) * 3,
            out_specs=(acts, acts) + (flat,) * 6 + (planes,) * 3 + (flat,) * 3,
            check_vma=False,
        )(*arguments)

    return whole
```

```python
import math

import jax
import jax.numpy as jnp
from jax import lax
from jax.experimental import pallas as pl
from jax.experimental.pallas import tpu as pltpu
from jax.sharding import Mesh, PartitionSpec as P

D = 2560
HEAD_DIM = 256
WINDOW = 2048
STEP = 10
SEQ_LEN = 3072

NORM_EPS = 1e-06
BETA_ONE = 0.9
BETA_TWO = 0.95
ADAM_EPS = 1e-08
DECAY_RATE = 0.1
MASKED_SCORE = -1e30

LANES = 512
KEY_BLOCK = 768
PLANES = ("g", "h")
OWNERS = ("g", "h", "k", "c")
CHIPS = ("seq", "k")
GROUP = ("seq", "k", "c")
RING = ("seq", "h", "k")
EVERY = ("seq", "g", "h", "k", "c")


def rotate(values, cosine, sine):
    half_dim = values.shape[-1] // 2
    first_half = values[..., :half_dim]
    second_half = values[..., half_dim:]
    return jnp.concatenate(
        [first_half * cosine - second_half * sine, second_half * cosine + first_half * sine],
        axis=-1,
    )


def doc_places(lengths_row, offsets):
    doc_ends = jnp.cumsum(lengths_row)
    passed = (doc_ends[None, :] <= offsets[:, None]).astype(jnp.int32)
    document = jnp.sum(passed, axis=1)
    starts = jnp.sum(passed * lengths_row[None, :], axis=1)
    return (document, offsets - starts)


def rope_angles(places, head_dim):
    freq_index = jnp.arange(head_dim // 2, dtype=jnp.float32)
    inverse = jnp.exp(freq_index * (-2.0 * math.log(10000.0) / head_dim))
    angles = places.astype(jnp.float32)[:, None] * inverse[None, :]
    return (jnp.cos(angles), jnp.sin(angles))


def adam_step(weight, first, second, grad, rate):
    first_new = BETA_ONE * first + (1.0 - BETA_ONE) * grad
    second_new = BETA_TWO * second + (1.0 - BETA_TWO) * grad * grad
    first_hat = first_new / (1.0 - BETA_ONE**STEP)
    second_hat = second_new / (1.0 - BETA_TWO**STEP)
    update = first_hat / (jnp.sqrt(second_hat) + ADAM_EPS)
    return (second_new, weight - rate * (update + DECAY_RATE * weight))


def glu_values(gate_in, up_in):
    return jax.nn.gelu(gate_in, approximate=True) * up_in


def low(value):
    return value.astype(jnp.bfloat16)


def wide(value):
    return value.astype(jnp.float32)


def dot(left, right, contract):
    return lax.dot_general(
        left, right, ((contract[:1], contract[1:]), ((), ())), preferred_element_type=jnp.float32
    )


def traded(axes, step):
    count = math.prod(lax.axis_size(axis) for axis in axes)
    return [(source, source ^ step) for source in range(count)]


def swapped(value, axis):
    return lax.ppermute(value, axis, [(0, 1), (1, 0)])


def after(value, *others):
    return lax.optimization_barrier((value,) + others)[0]


def doubled(value, axis, step, place):
    other = lax.ppermute(value, axis, traded((axis,), step))
    first = (lax.axis_index(axis) & step) == 0
    return jnp.stack([jnp.where(first, value, other), jnp.where(first, other, value)], axis=place)


def next_plane(block):
    count = math.prod(lax.axis_size(axis) for axis in PLANES)
    return lax.ppermute(block, PLANES, [(one, (one + 1) % count) for one in range(count)])


def joined_planes(blocks):
    count, rows = len(blocks), blocks[0].shape[0]
    whole = jnp.zeros((count * rows, blocks[0].shape[1]), blocks[0].dtype)
    for step, block in enumerate(blocks):
        start = lax.rem(lax.axis_index(PLANES) + (count - step), count) * rows
        whole = lax.dynamic_update_slice_in_dim(whole, block, start, 0)
    return whole


def spread_ring(value):
    chips = math.prod(lax.axis_size(axis) for axis in RING)
    place = lax.axis_index(RING)
    whole = jnp.zeros((chips,) + value.shape, value.dtype)
    for step in range(chips):
        arrived = lax.ppermute(value, RING, traded(RING, step)) if step else value
        whole = lax.dynamic_update_index_in_dim(whole, arrived, place ^ step, 0)
    return whole


def ring_sum(terms):
    chips = terms.shape[0]
    place = lax.axis_index(CHIPS)
    total = 0.0
    for step in range(chips):
        term = lax.dynamic_index_in_dim(terms, place ^ step, 0, keepdims=False)
        if step:
            term = lax.ppermute(term, CHIPS, traded(CHIPS, step))
        total = total + wide(term)
    return total


def exchanged(value, axes):
    return lax.all_to_all(value, axes, split_axis=0, concat_axis=0, tiled=True)


def half_sum(terms, axis, place):
    here = lax.axis_index(axis)
    kept = lax.dynamic_index_in_dim(terms, here, place, keepdims=False)
    given = lax.dynamic_index_in_dim(terms, 1 - here, place, keepdims=False)
    return low(wide(kept) + wide(swapped(given, axis)))


def mlp_chunks_kernel(slices, side_ref, weight_ref, gain_ref, gate_up_ref, down_ref):
    per_piece = pl.num_programs(1)
    index = side_ref[0] * pl.num_programs(0) + pl.program_id(0)
    index = index * per_piece + pl.program_id(1)
    width = weight_ref.shape[2]
    lane = pl.program_id(1) * width
    gain = gain_ref[...]
    for part in range(3):
        weight = wide(low(weight_ref[part]))
        if part < 2:
            weight = weight * gain
        weight = low(jnp.where(index < slices, weight, 0.0))
        if part < 2:
            place = pl.multiple_of(part * per_piece * width + lane, width)
            gate_up_ref[0, :, pl.ds(place, width)] = weight
        else:
            down_ref[0, :, pl.ds(pl.multiple_of(lane, width), width)] = weight


def mlp_chunks(weight, gain, side, members, piece):
    parts, rows, ff_width = weight.shape
    slices = ff_width // LANES
    per_piece = piece // LANES

    def weight_block(m, b, side_ref):
        return (0, 0, jnp.minimum((side_ref[0] * members + m) * per_piece + b, slices - 1))

    def out_block(m, b, side_ref):
        return (m, 0, 0)

    return pl.pallas_call(
        lambda *refs: mlp_chunks_kernel(slices, *refs),
        grid_spec=pltpu.PrefetchScalarGridSpec(
            num_scalar_prefetch=1,
            grid=(members, per_piece),
            in_specs=[
                pl.BlockSpec((parts, rows, LANES), weight_block),
                pl.BlockSpec((rows, 1), lambda m, b, side_ref: (0, 0)),
            ],
            out_specs=[
                pl.BlockSpec((1, rows, 2 * piece), out_block),
                pl.BlockSpec((1, rows, piece), out_block),
            ],
        ),
        out_shape=[
            jax.ShapeDtypeStruct((members, rows, 2 * piece), jnp.bfloat16),
            jax.ShapeDtypeStruct((members, rows, piece), jnp.bfloat16),
        ],
        compiler_params=pltpu.CompilerParams(vmem_limit_bytes=48 * 1024 * 1024),
        cost_estimate=pl.CostEstimate(
            flops=weight.size, bytes_accessed=3 * weight.size, transcendentals=0
        ),
        name="mlp_chunks",
    )(jnp.full((1,), side, jnp.int32), weight, gain)


def mlp_adam_kernel(rate, per_side, scaled, side_ref, ours_ref, theirs_ref, weight_ref, first_ref,
                    second_ref, gain_ref, *refs):
    grad_out, second_out, weight_out, dot_out = refs[-4:]
    block = pl.program_id(0)
    ours = block // per_side == side_ref[0]
    grad = wide(jnp.where(ours, ours_ref[0], theirs_ref[0]))
    weight = weight_ref[0]
    dot_part = jnp.sum(wide(low(weight)) * grad, axis=1, keepdims=True)
    dot_out[...] = jnp.where(block == 0, dot_part, dot_out[...] + dot_part)
    if scaled:
        grad = grad * gain_ref[...]
    grad_out[0] = grad
    second_out[0], weight_out[0] = adam_step(weight, first_ref[0], second_ref[0], grad, rate)


def mlp_adam(part, side, pieces, states, gain, rate, outs):
    _, rows, ff_width = states[0].shape
    members, _, piece = pieces[0].shape
    per_piece = piece // LANES
    per_side = members * per_piece

    def grad_block(own):
        def place(b, side_ref):
            used = (b // per_side == side_ref[0]) == own
            inner = jnp.where(used, b % per_side, 0)
            return (inner // per_piece, 0, inner % per_piece)

        return pl.BlockSpec((1, rows, LANES), place)

    state = pl.BlockSpec((1, rows, LANES), lambda b, side_ref: (part, 0, b))
    gains = pl.BlockSpec((rows, 1), lambda b, side_ref: (0, 0))
    size = rows * ff_width
    return pl.pallas_call(
        lambda *refs: mlp_adam_kernel(rate, per_side, part < 2, *refs),
        grid_spec=pltpu.PrefetchScalarGridSpec(
            num_scalar_prefetch=1,
            grid=(ff_width // LANES,),
            in_specs=[grad_block(True), grad_block(False), state, state, state, gains]
            + [pl.BlockSpec(memory_space=pl.ANY)] * len(outs),
            out_specs=[state, state, state, gains],
        ),
        out_shape=[jax.ShapeDtypeStruct(states[0].shape, jnp.float32)] * 3
        + [jax.ShapeDtypeStruct((rows, 1), jnp.float32)],
        input_output_aliases={7 + index: index for index in range(len(outs))},
        compiler_params=pltpu.CompilerParams(vmem_limit_bytes=48 * 1024 * 1024),
        cost_estimate=pl.CostEstimate(
            flops=20 * size, bytes_accessed=26 * size, transcendentals=size
        ),
        name="mlp_adam",
    )(jnp.full((1,), side, jnp.int32), *pieces, *states, gain, *outs)


def stacked_heads(ref):
    return jnp.concatenate([ref[:, :HEAD_DIM], ref[:, HEAD_DIM:]], axis=0)


def attend_kernel(query_ref, key_ref, value_t_ref, bias_ref, out_ref, lse_ref, score_ref):
    rows = query_ref.shape[0]
    queries = stacked_heads(query_ref)
    blocks = key_ref.shape[0] // KEY_BLOCK

    def first(block, top):
        part = pl.ds(pl.multiple_of(block * KEY_BLOCK, KEY_BLOCK), KEY_BLOCK)
        scores = dot(key_ref[part, :], queries, (1, 1)) + bias_ref[part, :]
        score_ref[part, :] = scores
        return jnp.maximum(top, jnp.max(scores, axis=0, keepdims=True))

    top = jnp.full((1, 2 * rows), -jnp.inf, jnp.float32)
    top = lax.fori_loop(0, blocks, first, top, unroll=2)

    def second(block, carry):
        total, mixed = carry
        part = pl.ds(pl.multiple_of(block * KEY_BLOCK, KEY_BLOCK), KEY_BLOCK)
        exps = jnp.exp(score_ref[part, :] - top)
        total = total + jnp.sum(exps, axis=0, keepdims=True)
        return total, mixed + dot(value_t_ref[:, part], low(exps), (1, 0))

    total, mixed = lax.fori_loop(
        0,
        blocks,
        second,
        (jnp.zeros((1, 2 * rows), jnp.float32), jnp.zeros((HEAD_DIM, 2 * rows), jnp.float32)),
        unroll=2,
    )
    mixed = low((mixed / total).T)
    out_ref[:, :HEAD_DIM] = mixed[:rows]
    out_ref[:, HEAD_DIM:] = mixed[rows:]
    lse_ref[0] = top + jnp.log(total)


def attend(queries, keys, values, bias):
    rows, width = queries.shape
    pairs = width // (2 * HEAD_DIM)
    count = keys.shape[0]

    def whole(shape):
        return pl.BlockSpec(shape, lambda p: (0,) * len(shape))

    pair = pl.BlockSpec((rows, 2 * HEAD_DIM), lambda p: (0, p))
    return pl.pallas_call(
        attend_kernel,
        grid=(pairs,),
        in_specs=[pair, whole(keys.shape), whole((HEAD_DIM, count)), whole(bias.shape)],
        out_specs=[pair, pl.BlockSpec((1, 1, 2 * rows), lambda p: (p, 0, 0))],
        out_shape=[
            jax.ShapeDtypeStruct((rows, width), jnp.bfloat16),
            jax.ShapeDtypeStruct((pairs, 1, 2 * rows), jnp.float32),
        ],
        scratch_shapes=[pltpu.VMEM((count, 2 * rows), jnp.float32)],
        compiler_params=pltpu.CompilerParams(vmem_limit_bytes=48 * 1024 * 1024),
        cost_estimate=pl.CostEstimate(
            flops=4 * rows * width * count,
            bytes_accessed=8 * rows * width + 12 * bias.size,
            transcendentals=pairs * bias.size,
        ),
        name="attend",
    )(queries, keys, values.T, bias)


def attend_back_kernel(query_ref, grad_ref, key_ref, key_t_ref, value_ref, bias_ref, lse_ref,
                       delta_ref, grad_query_ref, grad_window_ref):
    rows = query_ref.shape[0]
    queries = stacked_heads(query_ref)
    grads = stacked_heads(grad_ref)
    blocks = key_ref.shape[0] // KEY_BLOCK

    @pl.when(pl.program_id(0) == 0)
    def _():
        grad_window_ref[...] = jnp.zeros_like(grad_window_ref)

    lse = lse_ref[0]
    delta = delta_ref[0]

    def body(block, grad_query):
        part = pl.ds(pl.multiple_of(block * KEY_BLOCK, KEY_BLOCK), KEY_BLOCK)
        probs = jnp.exp(dot(key_ref[part, :], queries, (1, 1)) + bias_ref[part, :] - lse)
        grad_probs = dot(value_ref[part, :], grads, (1, 1))
        grad_scores = low(probs * (grad_probs - delta))
        grad_window_ref[part, :HEAD_DIM] += dot(grad_scores, queries, (1, 0))
        grad_window_ref[part, HEAD_DIM:] += dot(low(probs), grads, (1, 0))
        return grad_query + dot(key_t_ref[:, part], grad_scores, (1, 0))

    grad_query = jnp.zeros((HEAD_DIM, 2 * rows), jnp.float32)
    grad_query = lax.fori_loop(0, blocks, body, grad_query, unroll=2).T
    grad_query_ref[:, :HEAD_DIM] = grad_query[:rows]
    grad_query_ref[:, HEAD_DIM:] = grad_query[rows:]


def attend_back(queries, grads, keys, values, bias, lse, delta):
    rows, width = queries.shape
    pairs = width // (2 * HEAD_DIM)
    count = keys.shape[0]

    def whole(shape):
        return pl.BlockSpec(shape, lambda p: (0,) * len(shape))

    pair = pl.BlockSpec((rows, 2 * HEAD_DIM), lambda p: (0, p))
    line = pl.BlockSpec((1, 1, 2 * rows), lambda p: (p, 0, 0))
    return pl.pallas_call(
        attend_back_kernel,
        grid=(pairs,),
        in_specs=[
            pair,
            pair,
            whole(keys.shape),
            whole((HEAD_DIM, count)),
            whole(values.shape),
            whole(bias.shape),
            line,
            line,
        ],
        out_specs=[pair, whole((count, 2 * HEAD_DIM))],
        out_shape=[
            jax.ShapeDtypeStruct((rows, width), jnp.float32),
            jax.ShapeDtypeStruct((count, 2 * HEAD_DIM), jnp.float32),
        ],
        compiler_params=pltpu.CompilerParams(vmem_limit_bytes=48 * 1024 * 1024),
        cost_estimate=pl.CostEstimate(
            flops=10 * rows * width * count,
            bytes_accessed=8 * rows * width + 16 * bias.size,
            transcendentals=pairs * bias.size,
        ),
        name="attend_back",
    )(queries, grads, keys, keys.T, values, bias, lse, delta)


def on_device(
    hidden_in,
    cotangent,
    lengths,
    weight_qkv,
    first_qkv,
    second_qkv,
    weight_out,
    first_out,
    second_out,
    weight_mlp,
    first_mlp,
    second_mlp,
    norm_gains,
    first_gains,
    second_gains,
):
    tok_rows = hidden_in.shape[2]
    width = hidden_in.shape[3]
    head_count = width // HEAD_DIM
    sides = lax.axis_size("seq")
    columns = lax.axis_size("k")
    members = columns * lax.axis_size("c")
    planes = lax.axis_size("g") * lax.axis_size("h")
    owner_count = planes * members
    blocks_in_side = lax.axis_size("h") * members
    side = lax.axis_index("seq")
    core = lax.axis_index("c")
    packed_index = lax.axis_index("g")
    place = lax.axis_index(("h", "k", "c"))
    own_rows = weight_mlp.shape[0]
    ff_width = weight_mlp.shape[2]
    piece = -(-ff_width // (sides * members * LANES)) * LANES

    gains_low = wide(low(norm_gains))
    gain_one = gains_low[:, :1]
    gain_two = gains_low[:, 1:]
    qkv_low = wide(low(weight_qkv))
    def gathered(weight):
        half = weight.shape[1] // sides
        weight = lax.dynamic_slice_in_dim(weight, side * half, half, 1)
        whole = lax.all_gather(weight, EVERY, axis=0, tiled=True)
        return whole.reshape(sides, owner_count * own_rows, half)

    qkv_halves = gathered(low(qkv_low * gain_one))
    out_halves = gathered(low(weight_out))
    mlp_planes = weight_mlp.transpose(1, 0, 2)
    gate_up_chunks, down_chunks = mlp_chunks(mlp_planes, gain_two, side, members, piece)

    def to_members(chunks):
        return exchanged(chunks, ("k", "c")).reshape(members * own_rows, chunks.shape[2])

    incoming = cotangent.reshape(tok_rows, width)
    gate_up_blocks = [to_members(gate_up_chunks)]
    gate_up_blocks.append(next_plane(gate_up_blocks[0]))
    down_blocks = [to_members(down_chunks)]
    incoming_columns = doubled(incoming, "k", 1, 0)

    tokens = wide(hidden_in.reshape(tok_rows, width))
    lengths_row = lax.dynamic_index_in_dim(lengths, packed_index, 0, keepdims=False)
    row_numbers = jnp.arange(tok_rows, dtype=jnp.int32)
    query_docs, query_places = doc_places(
        lengths_row, (place * sides + side) * tok_rows + row_numbers
    )
    blocks = jnp.arange(blocks_in_side, dtype=jnp.int32)[None, :] * sides
    blocks = blocks + jnp.arange(sides, dtype=jnp.int32)[:, None]
    key_offsets = (blocks[:, :, None] * tok_rows + row_numbers).reshape(-1)
    key_docs, key_places = doc_places(lengths_row, key_offsets)
    distance = query_places[:, None] - key_places[None, :]
    allowed = (query_docs[:, None] == key_docs[None, :]) & (distance >= 0) & (distance < WINDOW)
    cosine, sine = rope_angles(query_places, HEAD_DIM)
    query_scale = HEAD_DIM ** (-0.5)

    factor_one = lax.rsqrt(jnp.mean(tokens * tokens, axis=-1, keepdims=True) + NORM_EPS)
    normed_one = low(tokens * factor_one)
    normed_one = after(normed_one, incoming_columns, gate_up_blocks[1], down_blocks[0])
    projected = jnp.concatenate([dot(normed_one, half, (1, 0)) for half in qkv_halves], axis=1)
    key_pre = projected[:, width : width + HEAD_DIM]
    value_low = low(projected[:, width + HEAD_DIM :])
    key_low = low(rotate(key_pre, cosine, sine))
    window_kv = spread_ring(jnp.concatenate([key_low, value_low], axis=1))
    window_kv = doubled(window_kv, "c", 1, 1)
    window_kv = window_kv.reshape(SEQ_LEN, 2 * HEAD_DIM)
    gate_up_blocks.append(next_plane(after(gate_up_blocks[1], projected)))
    for _ in range(planes - 3):
        gate_up_blocks.append(next_plane(gate_up_blocks[-1]))
    down_blocks.append(next_plane(after(down_blocks[0], projected)))
    for _ in range(planes - 2):
        down_blocks.append(next_plane(down_blocks[-1]))
    gate_up_own = joined_planes(gate_up_blocks)
    down_own = joined_planes(down_blocks)
    incoming_sides = doubled(after(incoming_columns, window_kv), "seq", 1, 0)
    query_pre = projected[:, :width].reshape(tok_rows, head_count, HEAD_DIM)
    queries = low(rotate(query_pre, cosine[:, None, :], sine[:, None, :]) * query_scale)
    queries = after(queries.reshape(tok_rows, width), gate_up_blocks[2], down_blocks[1])
    incoming_all = doubled(incoming_sides, "c", 1, incoming_sides.ndim - 2)
    incoming_all = incoming_all.reshape(sides * members * tok_rows, width)
    keys_win = window_kv[:, :HEAD_DIM]
    values_win = window_kv[:, HEAD_DIM:]
    bias = jnp.where(allowed.T, 0.0, MASKED_SCORE)
    bias = jnp.concatenate([bias, bias], axis=1)
    attn_low, log_total = attend(queries, keys_win, values_win, bias)
    attn_low = after(attn_low, incoming_sides)
    branch = [dot(attn_low, half, (1, 0)) for half in out_halves]
    middle = tokens + jnp.concatenate(branch, axis=1)

    factor_two = lax.rsqrt(jnp.mean(middle * middle, axis=-1, keepdims=True) + NORM_EPS)
    normed_two = after(low(middle * factor_two), gate_up_blocks[3], down_blocks[2])
    normed_two_all = lax.all_gather(normed_two, GROUP, axis=0, tiled=True)
    grad_act = low(dot(incoming_all, down_own, (1, 0)))
    gate_up = dot(normed_two_all, gate_up_own, (1, 0))
    activated, glu_back = jax.vjp(glu_values, gate_up[:, :piece], gate_up[:, piece:])
    activated_low = low(activated)
    attn_all = lax.all_gather(after(attn_low, normed_two_all), GROUP, axis=0, tiled=True)
    normed_one_all = lax.all_gather(after(normed_one, normed_two_all), GROUP, axis=0, tiled=True)
    grad_gate, grad_up = glu_back(wide(grad_act))
    grad_gate_up = low(jnp.concatenate([grad_gate, grad_up], axis=1))
    def to_owners(term):
        return lax.psum_scatter(term, PLANES, scatter_dimension=0, tiled=True)

    def in_plane(term, *others):
        term = term.reshape(members, own_rows, term.shape[1])
        ours = exchanged(after(term, *others), ("k", "c"))
        return (ours, swapped(ours, "seq"))

    def group_terms(hidden, weight):
        by_core = hidden.reshape(sides * columns, 2, tok_rows, hidden.shape[1])

        def one_core(which):
            rows = lax.dynamic_index_in_dim(by_core, which, 1, keepdims=False)
            return dot(rows.reshape(-1, hidden.shape[1]), weight, (1, 1))

        given = swapped(low(one_core(1 - core)), "c")
        return low(one_core(core) + wide(given)).reshape(sides * columns, tok_rows, width)

    terms = group_terms(grad_gate_up, gate_up_own)
    down_term = low(dot(incoming_all, after(activated_low, terms), (0, 0)))
    down_term = after(down_term, attn_all, normed_one_all)
    late = after(grad_gate_up[:, :piece], terms)
    gate_term = low(dot(normed_two_all, late, (0, 0)))
    grad_normed_two = after(ring_sum(terms), down_term, gate_term)

    down_rows = to_owners(down_term)
    gate_rows = to_owners(gate_term)
    down_pieces = in_plane(down_rows)
    grad_middle = (
        wide(incoming)
        + factor_two * grad_normed_two
        - middle * factor_two**3 * jnp.mean(grad_normed_two * middle, axis=-1, keepdims=True)
    )

    shares = sides * members

    def by_column(terms):
        terms = terms.reshape(tok_rows, shares, terms.shape[1] // shares).transpose(1, 0, 2)
        return exchanged(terms, GROUP).reshape(shares * tok_rows, -1)

    def to_rows(total):
        total = exchanged(total.reshape(owner_count, own_rows, -1), OWNERS)
        return low(jnp.sum(wide(total.reshape(planes, members, own_rows, -1)), axis=0))

    def joined(total):
        total = doubled(total, "seq", 1, 0).reshape(shares, own_rows, -1)
        return wide(total.transpose(1, 0, 2).reshape(own_rows, -1))

    grad_branch_low = low(grad_middle)
    out_columns = by_column(grad_branch_low)
    half = width // sides
    grad_mixed = sum(
        dot(grad_branch_low[:, index * half : (index + 1) * half], out_halves[index], (1, 1))
        for index in range(sides)
    )
    grad_mixed_low = low(grad_mixed)
    branch = ring_sum(group_terms(after(activated_low, grad_mixed_low), down_own))
    delta = (wide(grad_mixed_low) * wide(attn_low)).reshape(tok_rows, head_count, HEAD_DIM)
    delta = jnp.sum(delta, axis=-1).T.reshape(log_total.shape)
    grad_query, grad_window = attend_back(
        queries, grad_mixed_low, keys_win, values_win, bias, log_total, delta
    )
    grad_window = after(low(grad_window), down_pieces[0], out_columns)
    late = after(grad_gate_up[:, piece:], grad_window)
    up_term = low(dot(normed_two_all, late, (0, 0)))
    up_rows = to_owners(up_term)
    grad_window = half_sum(grad_window.reshape(-1, 2, tok_rows, 2 * HEAD_DIM), "c", 1)
    grad_window = grad_window.reshape(sides, -1, columns, tok_rows, 2 * HEAD_DIM)
    grad_window = half_sum(grad_window, "h", 1).reshape(-1, tok_rows, 2 * HEAD_DIM)
    grad_local = after(ring_sum(grad_window), up_term)
    grad_query = grad_query.reshape(tok_rows, head_count, HEAD_DIM)
    grad_query_pre = rotate(
        grad_query * query_scale, cosine[:, None, :], -sine[:, None, :]
    ).reshape(tok_rows, width)
    grad_key_pre = rotate(grad_local[:, :HEAD_DIM], cosine, -sine)
    grad_proj = low(
        jnp.concatenate([grad_query_pre, grad_key_pre, grad_local[:, HEAD_DIM:]], axis=1)
    )

    grad_proj = after(grad_proj, down_pieces[1])

    qkv_columns = by_column(grad_proj)
    qkv_total = low(dot(normed_one_all, qkv_columns, (0, 0)))
    out_total = low(dot(attn_all, after(out_columns, qkv_columns), (0, 0)))
    gate_pieces = in_plane(gate_rows, qkv_columns)
    qkv_total = to_rows(after(qkv_total, gate_pieces[0]))
    up_pieces = in_plane(up_rows, qkv_total)
    grad_out = joined(to_rows(after(out_total, up_pieces[0])))

    mlp_states = (mlp_planes, first_mlp.transpose(1, 0, 2), second_mlp.transpose(1, 0, 2))
    mlp_outs = ()
    gain_dots = {}
    rate_main = 2.0 * D ** (-0.5)
    for part, pieces in ((2, down_pieces), (0, gate_pieces), (1, up_pieces)):
        *mlp_outs, gain_dots[part] = mlp_adam(
            part, side, pieces, mlp_states, gain_two, rate_main, mlp_outs
        )
    grad_mlp, second_new_mlp, new_mlp = mlp_outs
    grad_gain_two = gain_dots[0] + gain_dots[1]
    grad_qkv = joined(qkv_total)
    hidden_out = low(middle + after(branch, grad_qkv)).reshape(1, 1, tok_rows, width)

    half = grad_proj.shape[1] // sides
    grad_normed = sum(
        dot(grad_proj[:, index * half : (index + 1) * half], qkv_halves[index], (1, 1))
        for index in range(sides)
    )
    hidden_grad = (
        grad_middle
        + factor_one * grad_normed
        - tokens * factor_one**3 * jnp.mean(grad_normed * tokens, axis=-1, keepdims=True)
    ).reshape(1, 1, tok_rows, width)

    rate_out = 2.0 * max(1, 6 * D // WINDOW) ** (-0.5)
    rate_gains = 0.4
    grad_gain_one = jnp.sum(qkv_low * grad_qkv, axis=1, keepdims=True)
    grad_qkv = grad_qkv * gain_one
    second_new_qkv, new_qkv = adam_step(weight_qkv, first_qkv, second_qkv, grad_qkv, rate_main)
    second_new_out, new_out = adam_step(weight_out, first_out, second_out, grad_out, rate_out)
    grad_gains = jnp.concatenate([grad_gain_one, grad_gain_two], axis=1)
    second_new_gains, new_gains = adam_step(
        norm_gains, first_gains, second_gains, grad_gains, rate_gains
    )
    return (
        hidden_out,
        hidden_grad,
        grad_qkv,
        second_new_qkv,
        new_qkv,
        grad_out,
        second_new_out,
        new_out,
        grad_mlp.transpose(1, 0, 2),
        second_new_mlp.transpose(1, 0, 2),
        new_mlp.transpose(1, 0, 2),
        grad_gains,
        second_new_gains,
        new_gains,
    )


def solution(mesh):
    seq_count, owner_count = mesh.devices.shape

    def whole(*arguments):
        members = SEQ_LEN // (seq_count * arguments[0].shape[2])
        shape = (seq_count, owner_count // members, members // 4, 2, 2)
        split = Mesh(mesh.devices.reshape(shape), ("seq", "g", "h", "k", "c"))
        acts = P(OWNERS, "seq", None, None)
        flat = P(OWNERS, None)
        planes = P(OWNERS, None, None)
        return jax.shard_map(
            on_device,
            mesh=split,
            in_specs=(acts, acts, P()) + (flat,) * 6 + (planes,) * 3 + (flat,) * 3,
            out_specs=(acts, acts) + (flat,) * 6 + (planes,) * 3 + (flat,) * 3,
            check_vma=False,
        )(*arguments)

    return whole
```

```python
import math

import jax
import jax.numpy as jnp
from jax import lax
from jax.experimental import pallas as pl
from jax.experimental.pallas import tpu as pltpu
from jax.sharding import Mesh, PartitionSpec as P

D = 2560
HEAD_DIM = 256
WINDOW = 2048
STEP = 10
SEQ_LEN = 3072

NORM_EPS = 1e-06
BETA_ONE = 0.9
BETA_TWO = 0.95
ADAM_EPS = 1e-08
DECAY_RATE = 0.1
MASKED_SCORE = -1e30

LANES = 512
KEY_BLOCK = 768
PLANES = ("g", "h")
OWNERS = ("g", "h", "k", "c")
CHIPS = ("seq", "k")
GROUP = ("seq", "k", "c")
RING = ("seq", "h", "k")


def rotate(values, cosine, sine):
    half_dim = values.shape[-1] // 2
    first_half = values[..., :half_dim]
    second_half = values[..., half_dim:]
    return jnp.concatenate(
        [first_half * cosine - second_half * sine, second_half * cosine + first_half * sine],
        axis=-1,
    )


def doc_places(lengths_row, offsets):
    doc_ends = jnp.cumsum(lengths_row)
    passed = (doc_ends[None, :] <= offsets[:, None]).astype(jnp.int32)
    document = jnp.sum(passed, axis=1)
    starts = jnp.sum(passed * lengths_row[None, :], axis=1)
    return (document, offsets - starts)


def rope_angles(places, head_dim):
    freq_index = jnp.arange(head_dim // 2, dtype=jnp.float32)
    inverse = jnp.exp(freq_index * (-2.0 * math.log(10000.0) / head_dim))
    angles = places.astype(jnp.float32)[:, None] * inverse[None, :]
    return (jnp.cos(angles), jnp.sin(angles))


def adam_step(weight, first, second, grad, rate):
    first_new = BETA_ONE * first + (1.0 - BETA_ONE) * grad
    second_new = BETA_TWO * second + (1.0 - BETA_TWO) * grad * grad
    first_hat = first_new / (1.0 - BETA_ONE**STEP)
    second_hat = second_new / (1.0 - BETA_TWO**STEP)
    update = first_hat / (jnp.sqrt(second_hat) + ADAM_EPS)
    return (second_new, weight - rate * (update + DECAY_RATE * weight))


def glu_values(gate_in, up_in):
    return jax.nn.gelu(gate_in, approximate=True) * up_in


def low(value):
    return value.astype(jnp.bfloat16)


def wide(value):
    return value.astype(jnp.float32)


def dot(left, right, contract):
    return lax.dot_general(
        left, right, ((contract[:1], contract[1:]), ((), ())), preferred_element_type=jnp.float32
    )


def traded(axes, step):
    count = math.prod(lax.axis_size(axis) for axis in axes)
    return [(source, source ^ step) for source in range(count)]


def swapped(value, axis):
    return lax.ppermute(value, axis, [(0, 1), (1, 0)])


def after(value, *others):
    return lax.optimization_barrier((value,) + others)[0]


def doubled(value, axis, step, place):
    other = lax.ppermute(value, axis, traded((axis,), step))
    first = (lax.axis_index(axis) & step) == 0
    return jnp.stack([jnp.where(first, value, other), jnp.where(first, other, value)], axis=place)


def next_plane(block):
    count = math.prod(lax.axis_size(axis) for axis in PLANES)
    return lax.ppermute(block, PLANES, [(one, (one + 1) % count) for one in range(count)])


def joined_planes(blocks):
    count, rows = len(blocks), blocks[0].shape[0]
    whole = jnp.zeros((count * rows, blocks[0].shape[1]), blocks[0].dtype)
    for step, block in enumerate(blocks):
        start = lax.rem(lax.axis_index(PLANES) + (count - step), count) * rows
        whole = lax.dynamic_update_slice_in_dim(whole, block, start, 0)
    return whole


def spread_ring(value):
    chips = math.prod(lax.axis_size(axis) for axis in RING)
    place = lax.axis_index(RING)
    whole = jnp.zeros((chips,) + value.shape, value.dtype)
    for step in range(chips):
        arrived = lax.ppermute(value, RING, traded(RING, step)) if step else value
        whole = lax.dynamic_update_index_in_dim(whole, arrived, place ^ step, 0)
    return whole


def ring_sum(terms, first=None):
    chips = terms.shape[0]
    place = lax.axis_index(CHIPS)
    total = 0.0
    for step in range(chips):
        term = lax.dynamic_index_in_dim(terms, place ^ step, 0, keepdims=False)
        if step == 1 and first is not None:
            term = first
        elif step:
            term = lax.ppermute(term, CHIPS, traded(CHIPS, step))
        total = total + wide(term)
    return total


def exchanged(value, axes):
    return lax.all_to_all(value, axes, split_axis=0, concat_axis=0, tiled=True)


def half_sum(terms, axis, place):
    here = lax.axis_index(axis)
    kept = lax.dynamic_index_in_dim(terms, here, place, keepdims=False)
    given = lax.dynamic_index_in_dim(terms, 1 - here, place, keepdims=False)
    return low(wide(kept) + wide(swapped(given, axis)))


def mlp_chunks_kernel(slices, side_ref, weight_ref, gain_ref, gate_up_ref, down_ref):
    per_piece = pl.num_programs(1)
    index = side_ref[0] * pl.num_programs(0) + pl.program_id(0)
    index = index * per_piece + pl.program_id(1)
    width = weight_ref.shape[2]
    lane = pl.program_id(1) * width
    gain = gain_ref[...]
    for part in range(3):
        weight = wide(low(weight_ref[part]))
        if part < 2:
            weight = weight * gain
        weight = low(jnp.where(index < slices, weight, 0.0))
        if part < 2:
            place = pl.multiple_of(part * per_piece * width + lane, width)
            gate_up_ref[0, :, pl.ds(place, width)] = weight
        else:
            down_ref[0, :, pl.ds(pl.multiple_of(lane, width), width)] = weight


def mlp_chunks(weight, gain, side, members, piece):
    parts, rows, ff_width = weight.shape
    slices = ff_width // LANES
    per_piece = piece // LANES

    def weight_block(m, b, side_ref):
        return (0, 0, jnp.minimum((side_ref[0] * members + m) * per_piece + b, slices - 1))

    def out_block(m, b, side_ref):
        return (m, 0, 0)

    return pl.pallas_call(
        lambda *refs: mlp_chunks_kernel(slices, *refs),
        grid_spec=pltpu.PrefetchScalarGridSpec(
            num_scalar_prefetch=1,
            grid=(members, per_piece),
            in_specs=[
                pl.BlockSpec((parts, rows, LANES), weight_block),
                pl.BlockSpec((rows, 1), lambda m, b, side_ref: (0, 0)),
            ],
            out_specs=[
                pl.BlockSpec((1, rows, 2 * piece), out_block),
                pl.BlockSpec((1, rows, piece), out_block),
            ],
        ),
        out_shape=[
            jax.ShapeDtypeStruct((members, rows, 2 * piece), jnp.bfloat16),
            jax.ShapeDtypeStruct((members, rows, piece), jnp.bfloat16),
        ],
        compiler_params=pltpu.CompilerParams(vmem_limit_bytes=48 * 1024 * 1024),
        cost_estimate=pl.CostEstimate(
            flops=weight.size, bytes_accessed=3 * weight.size, transcendentals=0
        ),
        name="mlp_chunks",
    )(jnp.full((1,), side, jnp.int32), weight, gain)


def mlp_adam_kernel(rate, per_side, scaled, side_ref, ours_ref, theirs_ref, weight_ref, first_ref,
                    second_ref, gain_ref, *refs):
    grad_out, second_out, weight_out, dot_out = refs[-4:]
    block = pl.program_id(0)
    ours = block // per_side == side_ref[0]
    grad = wide(jnp.where(ours, ours_ref[0], theirs_ref[0]))
    weight = weight_ref[0]
    dot_part = jnp.sum(wide(low(weight)) * grad, axis=1, keepdims=True)
    dot_out[...] = jnp.where(block == 0, dot_part, dot_out[...] + dot_part)
    if scaled:
        grad = grad * gain_ref[...]
    grad_out[0] = grad
    second_out[0], weight_out[0] = adam_step(weight, first_ref[0], second_ref[0], grad, rate)


def mlp_adam(part, side, pieces, states, gain, rate, outs):
    _, rows, ff_width = states[0].shape
    members, _, piece = pieces[0].shape
    per_piece = piece // LANES
    per_side = members * per_piece

    def grad_block(own):
        def place(b, side_ref):
            used = (b // per_side == side_ref[0]) == own
            inner = jnp.where(used, b % per_side, 0)
            return (inner // per_piece, 0, inner % per_piece)

        return pl.BlockSpec((1, rows, LANES), place)

    state = pl.BlockSpec((1, rows, LANES), lambda b, side_ref: (part, 0, b))
    gains = pl.BlockSpec((rows, 1), lambda b, side_ref: (0, 0))
    size = rows * ff_width
    return pl.pallas_call(
        lambda *refs: mlp_adam_kernel(rate, per_side, part < 2, *refs),
        grid_spec=pltpu.PrefetchScalarGridSpec(
            num_scalar_prefetch=1,
            grid=(ff_width // LANES,),
            in_specs=[grad_block(True), grad_block(False), state, state, state, gains]
            + [pl.BlockSpec(memory_space=pl.ANY)] * len(outs),
            out_specs=[state, state, state, gains],
        ),
        out_shape=[jax.ShapeDtypeStruct(states[0].shape, jnp.float32)] * 3
        + [jax.ShapeDtypeStruct((rows, 1), jnp.float32)],
        input_output_aliases={7 + index: index for index in range(len(outs))},
        compiler_params=pltpu.CompilerParams(vmem_limit_bytes=48 * 1024 * 1024),
        cost_estimate=pl.CostEstimate(
            flops=20 * size, bytes_accessed=26 * size, transcendentals=size
        ),
        name="mlp_adam",
    )(jnp.full((1,), side, jnp.int32), *pieces, *states, gain, *outs)


def stacked_heads(ref):
    return jnp.concatenate([ref[:, :HEAD_DIM], ref[:, HEAD_DIM:]], axis=0)


def attend_kernel(query_ref, key_ref, value_t_ref, bias_ref, out_ref, lse_ref, score_ref):
    rows = query_ref.shape[0]
    queries = stacked_heads(query_ref)
    blocks = key_ref.shape[0] // KEY_BLOCK

    def first(block, top):
        part = pl.ds(pl.multiple_of(block * KEY_BLOCK, KEY_BLOCK), KEY_BLOCK)
        scores = dot(key_ref[part, :], queries, (1, 1)) + bias_ref[part, :]
        score_ref[part, :] = scores
        return jnp.maximum(top, jnp.max(scores, axis=0, keepdims=True))

    top = jnp.full((1, 2 * rows), -jnp.inf, jnp.float32)
    top = lax.fori_loop(0, blocks, first, top, unroll=2)

    def second(block, carry):
        total, mixed = carry
        part = pl.ds(pl.multiple_of(block * KEY_BLOCK, KEY_BLOCK), KEY_BLOCK)
        exps = jnp.exp(score_ref[part, :] - top)
        total = total + jnp.sum(exps, axis=0, keepdims=True)
        return total, mixed + dot(value_t_ref[:, part], low(exps), (1, 0))

    total, mixed = lax.fori_loop(
        0,
        blocks,
        second,
        (jnp.zeros((1, 2 * rows), jnp.float32), jnp.zeros((HEAD_DIM, 2 * rows), jnp.float32)),
        unroll=2,
    )
    mixed = low((mixed / total).T)
    out_ref[:, :HEAD_DIM] = mixed[:rows]
    out_ref[:, HEAD_DIM:] = mixed[rows:]
    lse_ref[0] = top + jnp.log(total)


def attend(queries, keys, values, bias):
    rows, width = queries.shape
    pairs = width // (2 * HEAD_DIM)
    count = keys.shape[0]

    def whole(shape):
        return pl.BlockSpec(shape, lambda p: (0,) * len(shape))

    pair = pl.BlockSpec((rows, 2 * HEAD_DIM), lambda p: (0, p))
    return pl.pallas_call(
        attend_kernel,
        grid=(pairs,),
        in_specs=[pair, whole(keys.shape), whole((HEAD_DIM, count)), whole(bias.shape)],
        out_specs=[pair, pl.BlockSpec((1, 1, 2 * rows), lambda p: (p, 0, 0))],
        out_shape=[
            jax.ShapeDtypeStruct((rows, width), jnp.bfloat16),
            jax.ShapeDtypeStruct((pairs, 1, 2 * rows), jnp.float32),
        ],
        scratch_shapes=[pltpu.VMEM((count, 2 * rows), jnp.float32)],
        compiler_params=pltpu.CompilerParams(vmem_limit_bytes=48 * 1024 * 1024),
        cost_estimate=pl.CostEstimate(
            flops=4 * rows * width * count,
            bytes_accessed=8 * rows * width + 12 * bias.size,
            transcendentals=pairs * bias.size,
        ),
        name="attend",
    )(queries, keys, values.T, bias)


def attend_back_kernel(query_ref, grad_ref, key_ref, key_t_ref, value_ref, bias_ref, lse_ref,
                       delta_ref, grad_query_ref, grad_window_ref):
    rows = query_ref.shape[0]
    queries = stacked_heads(query_ref)
    grads = stacked_heads(grad_ref)
    blocks = key_ref.shape[0] // KEY_BLOCK

    @pl.when(pl.program_id(0) == 0)
    def _():
        grad_window_ref[...] = jnp.zeros_like(grad_window_ref)

    lse = lse_ref[0]
    delta = delta_ref[0]

    def body(block, grad_query):
        part = pl.ds(pl.multiple_of(block * KEY_BLOCK, KEY_BLOCK), KEY_BLOCK)
        probs = jnp.exp(dot(key_ref[part, :], queries, (1, 1)) + bias_ref[part, :] - lse)
        grad_probs = dot(value_ref[part, :], grads, (1, 1))
        grad_scores = low(probs * (grad_probs - delta))
        grad_window_ref[part, :HEAD_DIM] += dot(grad_scores, queries, (1, 0))
        grad_window_ref[part, HEAD_DIM:] += dot(low(probs), grads, (1, 0))
        return grad_query + dot(key_t_ref[:, part], grad_scores, (1, 0))

    grad_query = jnp.zeros((HEAD_DIM, 2 * rows), jnp.float32)
    grad_query = lax.fori_loop(0, blocks, body, grad_query, unroll=2).T
    grad_query_ref[:, :HEAD_DIM] = grad_query[:rows]
    grad_query_ref[:, HEAD_DIM:] = grad_query[rows:]


def attend_back(queries, grads, keys, values, bias, lse, delta):
    rows, width = queries.shape
    pairs = width // (2 * HEAD_DIM)
    count = keys.shape[0]

    def whole(shape):
        return pl.BlockSpec(shape, lambda p: (0,) * len(shape))

    pair = pl.BlockSpec((rows, 2 * HEAD_DIM), lambda p: (0, p))
    line = pl.BlockSpec((1, 1, 2 * rows), lambda p: (p, 0, 0))
    return pl.pallas_call(
        attend_back_kernel,
        grid=(pairs,),
        in_specs=[
            pair,
            pair,
            whole(keys.shape),
            whole((HEAD_DIM, count)),
            whole(values.shape),
            whole(bias.shape),
            line,
            line,
        ],
        out_specs=[pair, whole((count, 2 * HEAD_DIM))],
        out_shape=[
            jax.ShapeDtypeStruct((rows, width), jnp.float32),
            jax.ShapeDtypeStruct((count, 2 * HEAD_DIM), jnp.float32),
        ],
        compiler_params=pltpu.CompilerParams(vmem_limit_bytes=48 * 1024 * 1024),
        cost_estimate=pl.CostEstimate(
            flops=10 * rows * width * count,
            bytes_accessed=8 * rows * width + 16 * bias.size,
            transcendentals=pairs * bias.size,
        ),
        name="attend_back",
    )(queries, grads, keys, keys.T, values, bias, lse, delta)


def on_device(
    hidden_in,
    cotangent,
    lengths,
    weight_qkv,
    first_qkv,
    second_qkv,
    weight_out,
    first_out,
    second_out,
    weight_mlp,
    first_mlp,
    second_mlp,
    norm_gains,
    first_gains,
    second_gains,
):
    tok_rows = hidden_in.shape[2]
    width = hidden_in.shape[3]
    head_count = width // HEAD_DIM
    sides = lax.axis_size("seq")
    columns = lax.axis_size("k")
    members = columns * lax.axis_size("c")
    planes = lax.axis_size("g") * lax.axis_size("h")
    owner_count = planes * members
    blocks_in_side = lax.axis_size("h") * members
    side = lax.axis_index("seq")
    core = lax.axis_index("c")
    packed_index = lax.axis_index("g")
    place = lax.axis_index(("h", "k", "c"))
    own_rows = weight_mlp.shape[0]
    ff_width = weight_mlp.shape[2]
    piece = -(-ff_width // (sides * members * LANES)) * LANES

    gains_low = wide(low(norm_gains))
    gain_one = gains_low[:, :1]
    gain_two = gains_low[:, 1:]
    qkv_low = wide(low(weight_qkv))
    def regrouped(value, outer, inner):
        value = value.reshape(value.shape[0], outer, inner, own_rows).transpose(0, 2, 1, 3)
        return value.reshape(value.shape[0], outer * inner * own_rows)

    mlp_planes = weight_mlp.transpose(1, 0, 2)
    gate_up_chunks, down_chunks = mlp_chunks(mlp_planes, gain_two, side, members, piece)

    def to_members(chunks):
        return exchanged(chunks, ("k", "c")).reshape(members * own_rows, chunks.shape[2])

    incoming = cotangent.reshape(tok_rows, width)
    def gathered(weight, *others):
        half = weight.shape[1] // sides
        weight = lax.dynamic_slice_in_dim(weight, side * half, half, 1)
        weight = after(lax.all_gather(weight, PLANES, axis=0, tiled=True), *others)
        weight = lax.all_gather(weight, GROUP, axis=0, tiled=True)
        return weight.reshape(sides, owner_count * own_rows, half)

    gate_up_blocks = [to_members(gate_up_chunks)]
    qkv_halves = gathered(low(qkv_low * gain_one), gate_up_chunks)
    out_halves = gathered(after(low(weight_out), gate_up_blocks[0]))
    gate_up_blocks.append(next_plane(gate_up_blocks[0]))
    down_blocks = [to_members(down_chunks)]
    incoming_columns = doubled(incoming, "k", 1, 0)

    tokens = wide(hidden_in.reshape(tok_rows, width))
    lengths_row = lax.dynamic_index_in_dim(lengths, packed_index, 0, keepdims=False)
    row_numbers = jnp.arange(tok_rows, dtype=jnp.int32)
    query_docs, query_places = doc_places(
        lengths_row, (place * sides + side) * tok_rows + row_numbers
    )
    blocks = jnp.arange(blocks_in_side, dtype=jnp.int32)[None, :] * sides
    blocks = blocks + jnp.arange(sides, dtype=jnp.int32)[:, None]
    key_offsets = (blocks[:, :, None] * tok_rows + row_numbers).reshape(-1)
    key_docs, key_places = doc_places(lengths_row, key_offsets)
    distance = query_places[:, None] - key_places[None, :]
    allowed = (query_docs[:, None] == key_docs[None, :]) & (distance >= 0) & (distance < WINDOW)
    cosine, sine = rope_angles(query_places, HEAD_DIM)
    query_scale = HEAD_DIM ** (-0.5)

    factor_one = lax.rsqrt(jnp.mean(tokens * tokens, axis=-1, keepdims=True) + NORM_EPS)
    normed_one = low(tokens * factor_one)
    normed_one = after(normed_one, incoming_columns, gate_up_blocks[1], down_blocks[0])
    rows = regrouped(normed_one, planes, members)
    projected = jnp.concatenate([dot(rows, half, (1, 0)) for half in qkv_halves], axis=1)
    key_pre = projected[:, width : width + HEAD_DIM]
    value_low = low(projected[:, width + HEAD_DIM :])
    key_low = low(rotate(key_pre, cosine, sine))
    window_kv = spread_ring(jnp.concatenate([key_low, value_low], axis=1))
    window_kv = doubled(window_kv, "c", 1, 1)
    window_kv = window_kv.reshape(SEQ_LEN, 2 * HEAD_DIM)
    gate_up_blocks.append(next_plane(after(gate_up_blocks[1], projected)))
    for _ in range(planes - 3):
        gate_up_blocks.append(next_plane(gate_up_blocks[-1]))
    down_blocks.append(next_plane(after(down_blocks[0], projected)))
    for _ in range(planes - 2):
        down_blocks.append(next_plane(down_blocks[-1]))
    gate_up_own = joined_planes(gate_up_blocks)
    down_own = joined_planes(down_blocks)
    incoming_sides = doubled(after(incoming_columns, window_kv), "seq", 1, 0)
    query_pre = projected[:, :width].reshape(tok_rows, head_count, HEAD_DIM)
    queries = low(rotate(query_pre, cosine[:, None, :], sine[:, None, :]) * query_scale)
    queries = after(queries.reshape(tok_rows, width), gate_up_blocks[2], down_blocks[1])
    incoming_all = doubled(incoming_sides, "c", 1, incoming_sides.ndim - 2)
    incoming_all = incoming_all.reshape(sides * members * tok_rows, width)
    keys_win = window_kv[:, :HEAD_DIM]
    values_win = window_kv[:, HEAD_DIM:]
    bias = jnp.where(allowed.T, 0.0, MASKED_SCORE)
    bias = jnp.concatenate([bias, bias], axis=1)
    attn_low, log_total = attend(queries, keys_win, values_win, bias)
    attn_low = after(attn_low, incoming_sides)
    rows = regrouped(attn_low, planes, members)
    branch = [dot(rows, half, (1, 0)) for half in out_halves]
    middle = tokens + jnp.concatenate(branch, axis=1)

    factor_two = lax.rsqrt(jnp.mean(middle * middle, axis=-1, keepdims=True) + NORM_EPS)
    normed_two = low(middle * factor_two)
    normed_two_all = lax.all_gather(normed_two, GROUP, axis=0, tiled=True)
    grad_act = low(dot(incoming_all, down_own, (1, 0)))
    gate_up = dot(after(normed_two_all, down_blocks[2]), gate_up_own, (1, 0))
    activated, glu_back = jax.vjp(glu_values, gate_up[:, :piece], gate_up[:, piece:])
    activated_low = low(activated)
    def to_owners(term):
        return lax.psum_scatter(term, PLANES, scatter_dimension=0, tiled=True)

    attn_all = lax.all_gather(after(attn_low, gate_up), GROUP, axis=0, tiled=True)
    down_term = after(low(dot(incoming_all, activated_low, (0, 0))), attn_all)
    down_rows = to_owners(down_term)
    grad_gate, grad_up = glu_back(wide(after(grad_act, down_term)))
    grad_gate_up = low(jnp.concatenate([grad_gate, grad_up], axis=1))

    def in_plane(term, *others):
        term = term.reshape(members, own_rows, term.shape[1])
        ours = exchanged(after(term, *others), ("k", "c"))
        return (ours, swapped(ours, "seq"))

    def group_terms(hidden, weight):
        by_core = hidden.reshape(sides * columns, 2, tok_rows, hidden.shape[1])

        def one_core(which):
            rows = lax.dynamic_index_in_dim(by_core, which, 1, keepdims=False)
            return dot(rows.reshape(-1, hidden.shape[1]), weight, (1, 1))

        given = swapped(low(one_core(1 - core)), "c")
        return low(one_core(core) + wide(given)).reshape(sides * columns, tok_rows, width)

    terms = group_terms(grad_gate_up, gate_up_own)
    first = lax.ppermute(
        lax.dynamic_index_in_dim(terms, lax.axis_index(CHIPS) ^ 1, 0, keepdims=False),
        CHIPS,
        traded(CHIPS, 1),
    )
    late = after(grad_gate_up, first)
    gate_term = low(dot(normed_two_all, late[:, :piece], (0, 0)))
    up_term = low(dot(normed_two_all, late[:, piece:], (0, 0)))
    grad_normed_two = after(ring_sum(terms, first), gate_term, up_term)

    gate_rows = to_owners(gate_term)
    up_rows = to_owners(up_term)
    grad_middle = (
        wide(incoming)
        + factor_two * grad_normed_two
        - middle * factor_two**3 * jnp.mean(grad_normed_two * middle, axis=-1, keepdims=True)
    )

    shares = sides * members

    def by_column(terms):
        terms = terms.reshape(tok_rows, shares, terms.shape[1] // shares).transpose(1, 0, 2)
        return exchanged(terms, GROUP).reshape(shares * tok_rows, -1)

    def to_rows(total):
        total = exchanged(total.reshape(owner_count, own_rows, -1), OWNERS)
        return low(jnp.sum(wide(total.reshape(planes, members, own_rows, -1)), axis=0))

    def joined(total):
        total = doubled(total, "seq", 1, 0).reshape(shares, own_rows, -1)
        return wide(total.transpose(1, 0, 2).reshape(own_rows, -1))

    grad_branch_low = low(grad_middle)
    out_columns = by_column(grad_branch_low)
    half = width // sides
    grad_mixed = sum(
        dot(grad_branch_low[:, index * half : (index + 1) * half], out_halves[index], (1, 1))
        for index in range(sides)
    )
    grad_mixed_low = regrouped(low(grad_mixed), members, planes)
    branch_terms = group_terms(after(activated_low, grad_mixed_low), down_own)
    delta = (wide(grad_mixed_low) * wide(attn_low)).reshape(tok_rows, head_count, HEAD_DIM)
    delta = jnp.sum(delta, axis=-1).T.reshape(log_total.shape)
    grad_query, grad_window = attend_back(
        queries, grad_mixed_low, keys_win, values_win, bias, log_total, delta
    )
    out_total = to_rows(low(dot(attn_all, out_columns, (0, 0))))
    normed_one_columns = doubled(after(normed_one, grad_normed_two), "k", 1, 0)
    normed_one_sides = doubled(normed_one_columns, "seq", 1, 0)
    grad_window = after(low(grad_window), out_total, normed_one_sides)
    down_pieces = in_plane(down_rows, out_total)
    grad_window = half_sum(grad_window.reshape(-1, 2, tok_rows, 2 * HEAD_DIM), "c", 1)
    grad_window = grad_window.reshape(sides, -1, columns, tok_rows, 2 * HEAD_DIM)
    grad_window = grad_window.swapaxes(1, 2).reshape(sides * columns, -1, tok_rows, 2 * HEAD_DIM)
    grad_local = wide(half_sum(low(ring_sum(grad_window)), "h", 0))
    grad_local = after(grad_local, down_pieces[0])
    normed_one_all = doubled(normed_one_sides, "c", 1, normed_one_sides.ndim - 2)
    normed_one_all = normed_one_all.reshape(-1, width)
    grad_query = grad_query.reshape(tok_rows, head_count, HEAD_DIM)
    grad_query_pre = rotate(
        grad_query * query_scale, cosine[:, None, :], -sine[:, None, :]
    ).reshape(tok_rows, width)
    grad_key_pre = rotate(grad_local[:, :HEAD_DIM], cosine, -sine)
    grad_proj = low(
        jnp.concatenate([grad_query_pre, grad_key_pre, grad_local[:, HEAD_DIM:]], axis=1)
    )

    mlp_states = (mlp_planes, first_mlp.transpose(1, 0, 2), second_mlp.transpose(1, 0, 2))
    rate_main = 2.0 * D ** (-0.5)

    def mlp_updated(part, pieces, outs):
        *outs, gain_dot = mlp_adam(part, side, pieces, mlp_states, gain_two, rate_main, outs)
        return outs, gain_dot

    gate_pieces = in_plane(gate_rows, down_pieces[0])
    qkv_columns = by_column(after(grad_proj, normed_one_all, gate_pieces[0]))
    branch = ring_sum(after(branch_terms, qkv_columns))
    mlp_outs, _ = mlp_updated(2, down_pieces, ())
    qkv_total = low(dot(normed_one_all, qkv_columns, (0, 0)))
    qkv_total = to_rows(qkv_total)
    mlp_outs, gate_dot = mlp_updated(0, gate_pieces, mlp_outs)
    up_pieces = in_plane(up_rows, qkv_total, gate_dot, branch)
    (grad_mlp, second_new_mlp, new_mlp), up_dot = mlp_updated(1, up_pieces, mlp_outs)
    grad_gain_two = gate_dot + up_dot
    grad_out = joined(out_total)

    grad_qkv = joined(qkv_total)
    hidden_out = low(middle + branch).reshape(1, 1, tok_rows, width)

    half = grad_proj.shape[1] // sides
    grad_normed = sum(
        dot(grad_proj[:, index * half : (index + 1) * half], qkv_halves[index], (1, 1))
        for index in range(sides)
    )
    grad_normed = regrouped(grad_normed, members, planes)
    hidden_grad = (
        grad_middle
        + factor_one * grad_normed
        - tokens * factor_one**3 * jnp.mean(grad_normed * tokens, axis=-1, keepdims=True)
    ).reshape(1, 1, tok_rows, width)

    rate_out = 2.0 * max(1, 6 * D // WINDOW) ** (-0.5)
    rate_gains = 0.4
    grad_gain_one = jnp.sum(qkv_low * grad_qkv, axis=1, keepdims=True)
    grad_qkv = grad_qkv * gain_one
    second_new_qkv, new_qkv = adam_step(weight_qkv, first_qkv, second_qkv, grad_qkv, rate_main)
    second_new_out, new_out = adam_step(weight_out, first_out, second_out, grad_out, rate_out)
    grad_gains = jnp.concatenate([grad_gain_one, grad_gain_two], axis=1)
    second_new_gains, new_gains = adam_step(
        norm_gains, first_gains, second_gains, grad_gains, rate_gains
    )
    return (
        hidden_out,
        hidden_grad,
        grad_qkv,
        second_new_qkv,
        new_qkv,
        grad_out,
        second_new_out,
        new_out,
        grad_mlp.transpose(1, 0, 2),
        second_new_mlp.transpose(1, 0, 2),
        new_mlp.transpose(1, 0, 2),
        grad_gains,
        second_new_gains,
        new_gains,
    )


def solution(mesh):
    seq_count, owner_count = mesh.devices.shape

    def whole(*arguments):
        members = SEQ_LEN // (seq_count * arguments[0].shape[2])
        shape = (seq_count, owner_count // members, members // 4, 2, 2)
        split = Mesh(mesh.devices.reshape(shape), ("seq", "g", "h", "k", "c"))
        acts = P(OWNERS, "seq", None, None)
        flat = P(OWNERS, None)
        planes = P(OWNERS, None, None)
        return jax.shard_map(
            on_device,
            mesh=split,
            in_specs=(acts, acts, P()) + (flat,) * 6 + (planes,) * 3 + (flat,) * 3,
            out_specs=(acts, acts) + (flat,) * 6 + (planes,) * 3 + (flat,) * 3,
            check_vma=False,
        )(*arguments)

    return whole
```

```python
import math

import jax
import jax.numpy as jnp
from jax import lax
from jax.experimental import pallas as pl
from jax.experimental.pallas import tpu as pltpu
from jax.sharding import Mesh, PartitionSpec as P

D = 2560
HEAD_DIM = 256
WINDOW = 2048
STEP = 10
SEQ_LEN = 3072

NORM_EPS = 1e-06
BETA_ONE = 0.9
BETA_TWO = 0.95
ADAM_EPS = 1e-08
DECAY_RATE = 0.1
MASKED_SCORE = -1e30

LANES = 512
KEY_BLOCK = 768
PLANES = ("g", "h")
OWNERS = ("g", "h", "k", "c")
CHIPS = ("seq", "k")
GROUP = ("seq", "k", "c")
RING = ("seq", "h", "k")


def rotate(values, cosine, sine):
    half_dim = values.shape[-1] // 2
    first_half = values[..., :half_dim]
    second_half = values[..., half_dim:]
    return jnp.concatenate(
        [first_half * cosine - second_half * sine, second_half * cosine + first_half * sine],
        axis=-1,
    )


def doc_places(lengths_row, offsets):
    doc_ends = jnp.cumsum(lengths_row)
    passed = (doc_ends[None, :] <= offsets[:, None]).astype(jnp.int32)
    document = jnp.sum(passed, axis=1)
    starts = jnp.sum(passed * lengths_row[None, :], axis=1)
    return (document, offsets - starts)


def rope_angles(places, head_dim):
    freq_index = jnp.arange(head_dim // 2, dtype=jnp.float32)
    inverse = jnp.exp(freq_index * (-2.0 * math.log(10000.0) / head_dim))
    angles = places.astype(jnp.float32)[:, None] * inverse[None, :]
    return (jnp.cos(angles), jnp.sin(angles))


def adam_step(weight, first, second, grad, rate):
    first_new = BETA_ONE * first + (1.0 - BETA_ONE) * grad
    second_new = BETA_TWO * second + (1.0 - BETA_TWO) * grad * grad
    first_hat = first_new / (1.0 - BETA_ONE**STEP)
    second_hat = second_new / (1.0 - BETA_TWO**STEP)
    update = first_hat / (jnp.sqrt(second_hat) + ADAM_EPS)
    return (second_new, weight - rate * (update + DECAY_RATE * weight))


def glu_values(gate_in, up_in):
    return jax.nn.gelu(gate_in, approximate=True) * up_in


def low(value):
    return value.astype(jnp.bfloat16)


def wide(value):
    return value.astype(jnp.float32)


def dot(left, right, contract):
    return lax.dot_general(
        left, right, ((contract[:1], contract[1:]), ((), ())), preferred_element_type=jnp.float32
    )


def traded(axes, step):
    count = math.prod(lax.axis_size(axis) for axis in axes)
    return [(source, source ^ step) for source in range(count)]


def swapped(value, axis):
    return lax.ppermute(value, axis, [(0, 1), (1, 0)])


def after(value, *others):
    return lax.optimization_barrier((value,) + others)[0]


def doubled(value, axis, step, place):
    other = lax.ppermute(value, axis, traded((axis,), step))
    first = (lax.axis_index(axis) & step) == 0
    return jnp.stack([jnp.where(first, value, other), jnp.where(first, other, value)], axis=place)


def next_plane(block):
    count = math.prod(lax.axis_size(axis) for axis in PLANES)
    return lax.ppermute(block, PLANES, [(one, (one + 1) % count) for one in range(count)])


def joined_planes(blocks):
    count, rows = len(blocks), blocks[0].shape[0]
    whole = jnp.zeros((count * rows, blocks[0].shape[1]), blocks[0].dtype)
    for step, block in enumerate(blocks):
        start = lax.rem(lax.axis_index(PLANES) + (count - step), count) * rows
        whole = lax.dynamic_update_slice_in_dim(whole, block, start, 0)
    return whole


def spread_ring(value):
    chips = math.prod(lax.axis_size(axis) for axis in RING)
    place = lax.axis_index(RING)
    whole = jnp.zeros((chips,) + value.shape, value.dtype)
    for step in range(chips):
        arrived = lax.ppermute(value, RING, traded(RING, step)) if step else value
        whole = lax.dynamic_update_index_in_dim(whole, arrived, place ^ step, 0)
    return whole


def ring_sum(terms):
    chips = terms.shape[0]
    place = lax.axis_index(CHIPS)
    total = 0.0
    for step in range(chips):
        term = lax.dynamic_index_in_dim(terms, place ^ step, 0, keepdims=False)
        if step:
            term = lax.ppermute(term, CHIPS, traded(CHIPS, step))
        total = total + wide(term)
    return total


def exchanged(value, axes):
    return lax.all_to_all(value, axes, split_axis=0, concat_axis=0, tiled=True)


def half_sum(terms, axis, place):
    here = lax.axis_index(axis)
    kept = lax.dynamic_index_in_dim(terms, here, place, keepdims=False)
    given = lax.dynamic_index_in_dim(terms, 1 - here, place, keepdims=False)
    return low(wide(kept) + wide(swapped(given, axis)))


def mlp_chunks_kernel(slices, side_ref, weight_ref, gain_ref, gate_up_ref, down_ref):
    per_piece = pl.num_programs(1)
    index = side_ref[0] * pl.num_programs(0) + pl.program_id(0)
    index = index * per_piece + pl.program_id(1)
    width = weight_ref.shape[2]
    lane = pl.program_id(1) * width
    gain = gain_ref[...]
    for part in range(3):
        weight = wide(low(weight_ref[part]))
        if part < 2:
            weight = weight * gain
        weight = low(jnp.where(index < slices, weight, 0.0))
        if part < 2:
            place = pl.multiple_of(part * per_piece * width + lane, width)
            gate_up_ref[0, :, pl.ds(place, width)] = weight
        else:
            down_ref[0, :, pl.ds(pl.multiple_of(lane, width), width)] = weight


def mlp_chunks(weight, gain, side, members, piece):
    parts, rows, ff_width = weight.shape
    slices = ff_width // LANES
    per_piece = piece // LANES

    def weight_block(m, b, side_ref):
        return (0, 0, jnp.minimum((side_ref[0] * members + m) * per_piece + b, slices - 1))

    def out_block(m, b, side_ref):
        return (m, 0, 0)

    return pl.pallas_call(
        lambda *refs: mlp_chunks_kernel(slices, *refs),
        grid_spec=pltpu.PrefetchScalarGridSpec(
            num_scalar_prefetch=1,
            grid=(members, per_piece),
            in_specs=[
                pl.BlockSpec((parts, rows, LANES), weight_block),
                pl.BlockSpec((rows, 1), lambda m, b, side_ref: (0, 0)),
            ],
            out_specs=[
                pl.BlockSpec((1, rows, 2 * piece), out_block),
                pl.BlockSpec((1, rows, piece), out_block),
            ],
        ),
        out_shape=[
            jax.ShapeDtypeStruct((members, rows, 2 * piece), jnp.bfloat16),
            jax.ShapeDtypeStruct((members, rows, piece), jnp.bfloat16),
        ],
        compiler_params=pltpu.CompilerParams(vmem_limit_bytes=48 * 1024 * 1024),
        cost_estimate=pl.CostEstimate(
            flops=weight.size, bytes_accessed=3 * weight.size, transcendentals=0
        ),
        name="mlp_chunks",
    )(jnp.full((1,), side, jnp.int32), weight, gain)


def mlp_adam_kernel(rate, per_side, scaled, side_ref, ours_ref, theirs_ref, weight_ref, first_ref,
                    second_ref, gain_ref, *refs):
    grad_out, second_out, weight_out, dot_out = refs[-4:]
    block = pl.program_id(0)
    ours = block // per_side == side_ref[0]
    grad = wide(jnp.where(ours, ours_ref[0], theirs_ref[0]))
    weight = weight_ref[0]
    dot_part = jnp.sum(wide(low(weight)) * grad, axis=1, keepdims=True)
    dot_out[...] = jnp.where(block == 0, dot_part, dot_out[...] + dot_part)
    if scaled:
        grad = grad * gain_ref[...]
    grad_out[0] = grad
    second_out[0], weight_out[0] = adam_step(weight, first_ref[0], second_ref[0], grad, rate)


def mlp_adam(part, side, pieces, states, gain, rate, outs):
    _, rows, ff_width = states[0].shape
    members, _, piece = pieces[0].shape
    per_piece = piece // LANES
    per_side = members * per_piece

    def grad_block(own):
        def place(b, side_ref):
            used = (b // per_side == side_ref[0]) == own
            inner = jnp.where(used, b % per_side, 0)
            return (inner // per_piece, 0, inner % per_piece)

        return pl.BlockSpec((1, rows, LANES), place)

    state = pl.BlockSpec((1, rows, LANES), lambda b, side_ref: (part, 0, b))
    gains = pl.BlockSpec((rows, 1), lambda b, side_ref: (0, 0))
    size = rows * ff_width
    return pl.pallas_call(
        lambda *refs: mlp_adam_kernel(rate, per_side, part < 2, *refs),
        grid_spec=pltpu.PrefetchScalarGridSpec(
            num_scalar_prefetch=1,
            grid=(ff_width // LANES,),
            in_specs=[grad_block(True), grad_block(False), state, state, state, gains]
            + [pl.BlockSpec(memory_space=pl.ANY)] * len(outs),
            out_specs=[state, state, state, gains],
        ),
        out_shape=[jax.ShapeDtypeStruct(states[0].shape, jnp.float32)] * 3
        + [jax.ShapeDtypeStruct((rows, 1), jnp.float32)],
        input_output_aliases={7 + index: index for index in range(len(outs))},
        compiler_params=pltpu.CompilerParams(vmem_limit_bytes=48 * 1024 * 1024),
        cost_estimate=pl.CostEstimate(
            flops=20 * size, bytes_accessed=26 * size, transcendentals=size
        ),
        name="mlp_adam",
    )(jnp.full((1,), side, jnp.int32), *pieces, *states, gain, *outs)


def stacked_heads(ref):
    return jnp.concatenate([ref[:, :HEAD_DIM], ref[:, HEAD_DIM:]], axis=0)


def attend_kernel(query_ref, key_ref, value_t_ref, bias_ref, out_ref, lse_ref, score_ref):
    rows = query_ref.shape[0]
    queries = stacked_heads(query_ref)
    blocks = key_ref.shape[0] // KEY_BLOCK

    def first(block, top):
        part = pl.ds(pl.multiple_of(block * KEY_BLOCK, KEY_BLOCK), KEY_BLOCK)
        scores = dot(key_ref[part, :], queries, (1, 1)) + bias_ref[part, :]
        score_ref[part, :] = scores
        return jnp.maximum(top, jnp.max(scores, axis=0, keepdims=True))

    top = jnp.full((1, 2 * rows), -jnp.inf, jnp.float32)
    top = lax.fori_loop(0, blocks, first, top, unroll=2)

    def second(block, carry):
        total, mixed = carry
        part = pl.ds(pl.multiple_of(block * KEY_BLOCK, KEY_BLOCK), KEY_BLOCK)
        exps = jnp.exp(score_ref[part, :] - top)
        total = total + jnp.sum(exps, axis=0, keepdims=True)
        return total, mixed + dot(value_t_ref[:, part], low(exps), (1, 0))

    total, mixed = lax.fori_loop(
        0,
        blocks,
        second,
        (jnp.zeros((1, 2 * rows), jnp.float32), jnp.zeros((HEAD_DIM, 2 * rows), jnp.float32)),
        unroll=2,
    )
    mixed = low((mixed / total).T)
    out_ref[:, :HEAD_DIM] = mixed[:rows]
    out_ref[:, HEAD_DIM:] = mixed[rows:]
    lse_ref[0] = top + jnp.log(total)


def attend(queries, keys, values, bias):
    rows, width = queries.shape
    pairs = width // (2 * HEAD_DIM)
    count = keys.shape[0]

    def whole(shape):
        return pl.BlockSpec(shape, lambda p: (0,) * len(shape))

    pair = pl.BlockSpec((rows, 2 * HEAD_DIM), lambda p: (0, p))
    return pl.pallas_call(
        attend_kernel,
        grid=(pairs,),
        in_specs=[pair, whole(keys.shape), whole((HEAD_DIM, count)), whole(bias.shape)],
        out_specs=[pair, pl.BlockSpec((1, 1, 2 * rows), lambda p: (p, 0, 0))],
        out_shape=[
            jax.ShapeDtypeStruct((rows, width), jnp.bfloat16),
            jax.ShapeDtypeStruct((pairs, 1, 2 * rows), jnp.float32),
        ],
        scratch_shapes=[pltpu.VMEM((count, 2 * rows), jnp.float32)],
        compiler_params=pltpu.CompilerParams(vmem_limit_bytes=48 * 1024 * 1024),
        cost_estimate=pl.CostEstimate(
            flops=4 * rows * width * count,
            bytes_accessed=8 * rows * width + 12 * bias.size,
            transcendentals=pairs * bias.size,
        ),
        name="attend",
    )(queries, keys, values.T, bias)


def attend_back_kernel(query_ref, grad_ref, key_ref, key_t_ref, value_ref, bias_ref, lse_ref,
                       delta_ref, grad_query_ref, grad_window_ref):
    rows = query_ref.shape[0]
    queries = stacked_heads(query_ref)
    grads = stacked_heads(grad_ref)
    blocks = key_ref.shape[0] // KEY_BLOCK

    @pl.when(pl.program_id(0) == 0)
    def _():
        grad_window_ref[...] = jnp.zeros_like(grad_window_ref)

    lse = lse_ref[0]
    delta = delta_ref[0]

    def body(block, grad_query):
        part = pl.ds(pl.multiple_of(block * KEY_BLOCK, KEY_BLOCK), KEY_BLOCK)
        probs = jnp.exp(dot(key_ref[part, :], queries, (1, 1)) + bias_ref[part, :] - lse)
        grad_probs = dot(value_ref[part, :], grads, (1, 1))
        grad_scores = low(probs * (grad_probs - delta))
        grad_window_ref[part, :HEAD_DIM] += dot(grad_scores, queries, (1, 0))
        grad_window_ref[part, HEAD_DIM:] += dot(low(probs), grads, (1, 0))
        return grad_query + dot(key_t_ref[:, part], grad_scores, (1, 0))

    grad_query = jnp.zeros((HEAD_DIM, 2 * rows), jnp.float32)
    grad_query = lax.fori_loop(0, blocks, body, grad_query, unroll=2).T
    grad_query_ref[:, :HEAD_DIM] = grad_query[:rows]
    grad_query_ref[:, HEAD_DIM:] = grad_query[rows:]


def attend_back(queries, grads, keys, values, bias, lse, delta):
    rows, width = queries.shape
    pairs = width // (2 * HEAD_DIM)
    count = keys.shape[0]

    def whole(shape):
        return pl.BlockSpec(shape, lambda p: (0,) * len(shape))

    pair = pl.BlockSpec((rows, 2 * HEAD_DIM), lambda p: (0, p))
    line = pl.BlockSpec((1, 1, 2 * rows), lambda p: (p, 0, 0))
    return pl.pallas_call(
        attend_back_kernel,
        grid=(pairs,),
        in_specs=[
            pair,
            pair,
            whole(keys.shape),
            whole((HEAD_DIM, count)),
            whole(values.shape),
            whole(bias.shape),
            line,
            line,
        ],
        out_specs=[pair, whole((count, 2 * HEAD_DIM))],
        out_shape=[
            jax.ShapeDtypeStruct((rows, width), jnp.float32),
            jax.ShapeDtypeStruct((count, 2 * HEAD_DIM), jnp.float32),
        ],
        compiler_params=pltpu.CompilerParams(vmem_limit_bytes=48 * 1024 * 1024),
        cost_estimate=pl.CostEstimate(
            flops=10 * rows * width * count,
            bytes_accessed=8 * rows * width + 16 * bias.size,
            transcendentals=pairs * bias.size,
        ),
        name="attend_back",
    )(queries, grads, keys, keys.T, values, bias, lse, delta)


def on_device(
    hidden_in,
    cotangent,
    lengths,
    weight_qkv,
    first_qkv,
    second_qkv,
    weight_out,
    first_out,
    second_out,
    weight_mlp,
    first_mlp,
    second_mlp,
    norm_gains,
    first_gains,
    second_gains,
):
    tok_rows = hidden_in.shape[2]
    width = hidden_in.shape[3]
    head_count = width // HEAD_DIM
    sides = lax.axis_size("seq")
    columns = lax.axis_size("k")
    members = columns * lax.axis_size("c")
    planes = lax.axis_size("g") * lax.axis_size("h")
    owner_count = planes * members
    blocks_in_side = lax.axis_size("h") * members
    side = lax.axis_index("seq")
    core = lax.axis_index("c")
    packed_index = lax.axis_index("g")
    place = lax.axis_index(("h", "k", "c"))
    own_rows = weight_mlp.shape[0]
    ff_width = weight_mlp.shape[2]
    piece = -(-ff_width // (sides * members * LANES)) * LANES

    gains_low = wide(low(norm_gains))
    gain_one = gains_low[:, :1]
    gain_two = gains_low[:, 1:]
    qkv_low = wide(low(weight_qkv))
    def regrouped(value, outer, inner):
        value = value.reshape(value.shape[0], outer, inner, own_rows).transpose(0, 2, 1, 3)
        return value.reshape(value.shape[0], outer * inner * own_rows)

    mlp_planes = weight_mlp.transpose(1, 0, 2)
    gate_up_chunks, down_chunks = mlp_chunks(mlp_planes, gain_two, side, members, piece)

    def to_members(chunks):
        return exchanged(chunks, ("k", "c")).reshape(members * own_rows, chunks.shape[2])

    incoming = cotangent.reshape(tok_rows, width)
    def gathered(weight, *others):
        half = weight.shape[1] // sides
        weight = lax.dynamic_slice_in_dim(weight, side * half, half, 1)
        weight = after(lax.all_gather(weight, PLANES, axis=0, tiled=True), *others)
        weight = lax.all_gather(weight, GROUP, axis=0, tiled=True)
        return weight.reshape(sides, owner_count * own_rows, half)

    gate_up_blocks = [to_members(gate_up_chunks)]
    qkv_halves = gathered(low(qkv_low * gain_one), gate_up_chunks)
    gate_up_blocks.append(next_plane(gate_up_blocks[0]))
    down_blocks = [to_members(down_chunks)]
    out_halves = gathered(after(low(weight_out), gate_up_blocks[1]))
    incoming_columns = doubled(incoming, "k", 1, 0)

    tokens = wide(hidden_in.reshape(tok_rows, width))
    lengths_row = lax.dynamic_index_in_dim(lengths, packed_index, 0, keepdims=False)
    row_numbers = jnp.arange(tok_rows, dtype=jnp.int32)
    query_docs, query_places = doc_places(
        lengths_row, (place * sides + side) * tok_rows + row_numbers
    )
    blocks = jnp.arange(blocks_in_side, dtype=jnp.int32)[None, :] * sides
    blocks = blocks + jnp.arange(sides, dtype=jnp.int32)[:, None]
    key_offsets = (blocks[:, :, None] * tok_rows + row_numbers).reshape(-1)
    key_docs, key_places = doc_places(lengths_row, key_offsets)
    distance = query_places[:, None] - key_places[None, :]
    allowed = (query_docs[:, None] == key_docs[None, :]) & (distance >= 0) & (distance < WINDOW)
    cosine, sine = rope_angles(query_places, HEAD_DIM)
    query_scale = HEAD_DIM ** (-0.5)

    factor_one = lax.rsqrt(jnp.mean(tokens * tokens, axis=-1, keepdims=True) + NORM_EPS)
    normed_one = low(tokens * factor_one)
    normed_one = after(normed_one, incoming_columns, gate_up_blocks[1], down_blocks[0])
    rows = regrouped(normed_one, planes, members)
    projected = jnp.concatenate([dot(rows, half, (1, 0)) for half in qkv_halves], axis=1)
    key_pre = projected[:, width : width + HEAD_DIM]
    value_low = low(projected[:, width + HEAD_DIM :])
    key_low = low(rotate(key_pre, cosine, sine))
    window_kv = spread_ring(jnp.concatenate([key_low, value_low], axis=1))
    window_kv = doubled(window_kv, "c", 1, 1)
    window_kv = window_kv.reshape(SEQ_LEN, 2 * HEAD_DIM)
    gate_up_blocks.append(next_plane(after(gate_up_blocks[1], projected)))
    for _ in range(planes - 3):
        gate_up_blocks.append(next_plane(gate_up_blocks[-1]))
    down_blocks.append(next_plane(after(down_blocks[0], projected)))
    for _ in range(planes - 2):
        down_blocks.append(next_plane(down_blocks[-1]))
    gate_up_own = joined_planes(gate_up_blocks)
    down_own = joined_planes(down_blocks)
    incoming_sides = doubled(after(incoming_columns, window_kv), "seq", 1, 0)
    query_pre = projected[:, :width].reshape(tok_rows, head_count, HEAD_DIM)
    queries = low(rotate(query_pre, cosine[:, None, :], sine[:, None, :]) * query_scale)
    queries = after(queries.reshape(tok_rows, width), gate_up_blocks[2], down_blocks[1])
    incoming_all = doubled(incoming_sides, "c", 1, incoming_sides.ndim - 2)
    incoming_all = incoming_all.reshape(sides * members * tok_rows, width)
    keys_win = window_kv[:, :HEAD_DIM]
    values_win = window_kv[:, HEAD_DIM:]
    bias = jnp.where(allowed.T, 0.0, MASKED_SCORE)
    bias = jnp.concatenate([bias, bias], axis=1)
    attn_low, log_total = attend(queries, keys_win, values_win, bias)
    attn_low = after(attn_low, incoming_sides)
    rows = regrouped(attn_low, planes, members)
    branch = [dot(rows, half, (1, 0)) for half in out_halves]
    middle = tokens + jnp.concatenate(branch, axis=1)

    factor_two = lax.rsqrt(jnp.mean(middle * middle, axis=-1, keepdims=True) + NORM_EPS)
    normed_two = low(middle * factor_two)
    normed_two_all = lax.all_gather(normed_two, GROUP, axis=0, tiled=True)
    grad_act = low(dot(incoming_all, down_own, (1, 0)))
    gate_up = dot(after(normed_two_all, down_blocks[2], incoming_all), gate_up_own, (1, 0))
    activated, glu_back = jax.vjp(glu_values, gate_up[:, :piece], gate_up[:, piece:])
    activated_low = low(activated)
    def to_owners(term):
        return lax.psum_scatter(term, PLANES, scatter_dimension=0, tiled=True)

    attn_all = lax.all_gather(after(attn_low, gate_up), GROUP, axis=0, tiled=True)
    down_term = after(low(dot(incoming_all, activated_low, (0, 0))), attn_all)
    down_rows = to_owners(down_term)
    grad_gate, grad_up = glu_back(wide(after(grad_act, down_term)))
    grad_gate_up = low(jnp.concatenate([grad_gate, grad_up], axis=1))

    def in_plane(term, *others):
        term = term.reshape(members, own_rows, term.shape[1])
        ours = exchanged(after(term, *others), ("k", "c"))
        return (ours, swapped(ours, "seq"))

    def group_terms(hidden, weight):
        by_core = hidden.reshape(sides * columns, 2, tok_rows, hidden.shape[1])

        def one_core(which):
            rows = lax.dynamic_index_in_dim(by_core, which, 1, keepdims=False)
            return dot(rows.reshape(-1, hidden.shape[1]), weight, (1, 1))

        given = swapped(low(one_core(1 - core)), "c")
        return low(one_core(core) + wide(given)).reshape(sides * columns, tok_rows, width)

    terms = group_terms(grad_gate_up, gate_up_own)
    place = lax.axis_index(CHIPS)
    grad_normed_two = wide(lax.dynamic_index_in_dim(terms, place, 0, keepdims=False))
    arrived = []
    for step in range(1, sides * columns):
        term = lax.dynamic_index_in_dim(terms, place ^ step, 0, keepdims=False)
        if step == sides * columns - 1:
            term = after(term, *arrived)
        arrived.append(lax.ppermute(term, CHIPS, traded(CHIPS, step)))
    late = after(grad_gate_up, *arrived[:-1])
    gate_term = low(dot(normed_two_all, late[:, :piece], (0, 0)))
    up_term = low(dot(normed_two_all, late[:, piece:], (0, 0)))
    grad_normed_two = grad_normed_two + sum(wide(term) for term in arrived)
    grad_normed_two = after(grad_normed_two, gate_term, up_term)

    gate_rows = to_owners(gate_term)
    up_rows = to_owners(up_term)
    grad_middle = (
        wide(incoming)
        + factor_two * grad_normed_two
        - middle * factor_two**3 * jnp.mean(grad_normed_two * middle, axis=-1, keepdims=True)
    )

    shares = sides * members

    def by_column(terms):
        terms = terms.reshape(tok_rows, shares, terms.shape[1] // shares).transpose(1, 0, 2)
        return exchanged(terms, GROUP).reshape(shares * tok_rows, -1)

    def to_rows(total):
        total = exchanged(total.reshape(owner_count, own_rows, -1), OWNERS)
        return low(jnp.sum(wide(total.reshape(planes, members, own_rows, -1)), axis=0))

    def joined(total):
        total = doubled(total, "seq", 1, 0).reshape(shares, own_rows, -1)
        return wide(total.transpose(1, 0, 2).reshape(own_rows, -1))

    grad_branch_low = low(grad_middle)
    out_columns = by_column(grad_branch_low)
    half = width // sides
    grad_mixed = sum(
        dot(grad_branch_low[:, index * half : (index + 1) * half], out_halves[index], (1, 1))
        for index in range(sides)
    )
    grad_mixed_low = regrouped(low(grad_mixed), members, planes)
    delta = (wide(grad_mixed_low) * wide(attn_low)).reshape(tok_rows, head_count, HEAD_DIM)
    delta = jnp.sum(delta, axis=-1).T.reshape(log_total.shape)
    grad_query, grad_window = attend_back(
        queries, grad_mixed_low, keys_win, values_win, bias, log_total, delta
    )
    normed_one_columns = doubled(after(normed_one, grad_normed_two), "k", 1, 0)
    normed_one_sides = doubled(normed_one_columns, "seq", 1, 0)
    branch_terms = group_terms(after(activated_low, grad_window), down_own)
    down_pieces = in_plane(down_rows, out_columns)
    grad_window = after(low(grad_window), normed_one_sides, down_pieces[1])
    out_total = to_rows(low(dot(attn_all, after(out_columns, grad_window), (0, 0))))
    normed_one_others = swapped(normed_one_sides, "c")
    gate_pieces = in_plane(gate_rows, out_total)
    grad_window = half_sum(grad_window.reshape(-1, 2, tok_rows, 2 * HEAD_DIM), "c", 1)
    grad_window = grad_window.reshape(sides, -1, columns, tok_rows, 2 * HEAD_DIM)
    grad_window = grad_window.swapaxes(1, 2).reshape(sides * columns, -1, tok_rows, 2 * HEAD_DIM)
    grad_local = wide(half_sum(low(ring_sum(grad_window)), "h", 0))
    grad_query = grad_query.reshape(tok_rows, head_count, HEAD_DIM)
    grad_query_pre = rotate(
        grad_query * query_scale, cosine[:, None, :], -sine[:, None, :]
    ).reshape(tok_rows, width)
    grad_key_pre = rotate(grad_local[:, :HEAD_DIM], cosine, -sine)
    grad_proj = low(
        jnp.concatenate([grad_query_pre, grad_key_pre, grad_local[:, HEAD_DIM:]], axis=1)
    )

    mlp_states = (mlp_planes, first_mlp.transpose(1, 0, 2), second_mlp.transpose(1, 0, 2))
    rate_main = 2.0 * D ** (-0.5)

    def mlp_updated(part, pieces, outs):
        *outs, gain_dot = mlp_adam(part, side, pieces, mlp_states, gain_two, rate_main, outs)
        return outs, gain_dot

    qkv_columns = by_column(after(grad_proj, gate_pieces[0], normed_one_others))
    mlp_outs, _ = mlp_updated(2, down_pieces, ())
    by_core = after(qkv_columns, *mlp_outs).reshape(sides * columns, 2, tok_rows, -1)

    def one_core_total(rows, which):
        columns_there = lax.dynamic_index_in_dim(by_core, which, 1, keepdims=False)
        return dot(rows.reshape(-1, width), columns_there.reshape(-1, by_core.shape[3]), (0, 0))

    qkv_total = one_core_total(normed_one_sides, core)
    qkv_total = low(qkv_total + one_core_total(normed_one_others, 1 - core))
    up_pieces = in_plane(up_rows, qkv_columns, gate_pieces[1])
    mlp_outs, gate_dot = mlp_updated(0, gate_pieces, mlp_outs)
    qkv_total = to_rows(after(qkv_total, up_pieces[0], gate_dot))
    branch = ring_sum(after(branch_terms, up_pieces[0]))
    (grad_mlp, second_new_mlp, new_mlp), up_dot = mlp_updated(1, up_pieces, mlp_outs)
    grad_gain_two = gate_dot + up_dot
    qkv_total = after(qkv_total, up_dot)
    grad_out = joined(out_total)

    grad_qkv = joined(qkv_total)
    hidden_out = low(middle + branch).reshape(1, 1, tok_rows, width)

    half = grad_proj.shape[1] // sides
    grad_normed = sum(
        dot(grad_proj[:, index * half : (index + 1) * half], qkv_halves[index], (1, 1))
        for index in range(sides)
    )
    grad_normed = regrouped(grad_normed, members, planes)
    hidden_grad = (
        grad_middle
        + factor_one * grad_normed
        - tokens * factor_one**3 * jnp.mean(grad_normed * tokens, axis=-1, keepdims=True)
    ).reshape(1, 1, tok_rows, width)

    rate_out = 2.0 * max(1, 6 * D // WINDOW) ** (-0.5)
    rate_gains = 0.4
    grad_gain_one = jnp.sum(qkv_low * grad_qkv, axis=1, keepdims=True)
    grad_qkv = grad_qkv * gain_one
    second_new_qkv, new_qkv = adam_step(weight_qkv, first_qkv, second_qkv, grad_qkv, rate_main)
    second_new_out, new_out = adam_step(weight_out, first_out, second_out, grad_out, rate_out)
    grad_gains = jnp.concatenate([grad_gain_one, grad_gain_two], axis=1)
    second_new_gains, new_gains = adam_step(
        norm_gains, first_gains, second_gains, grad_gains, rate_gains
    )
    return (
        hidden_out,
        hidden_grad,
        grad_qkv,
        second_new_qkv,
        new_qkv,
        grad_out,
        second_new_out,
        new_out,
        grad_mlp.transpose(1, 0, 2),
        second_new_mlp.transpose(1, 0, 2),
        new_mlp.transpose(1, 0, 2),
        grad_gains,
        second_new_gains,
        new_gains,
    )


def solution(mesh):
    seq_count, owner_count = mesh.devices.shape

    def whole(*arguments):
        members = SEQ_LEN // (seq_count * arguments[0].shape[2])
        shape = (seq_count, owner_count // members, members // 4, 2, 2)
        split = Mesh(mesh.devices.reshape(shape), ("seq", "g", "h", "k", "c"))
        acts = P(OWNERS, "seq", None, None)
        flat = P(OWNERS, None)
        planes = P(OWNERS, None, None)
        return jax.shard_map(
            on_device,
            mesh=split,
            in_specs=(acts, acts, P()) + (flat,) * 6 + (planes,) * 3 + (flat,) * 3,
            out_specs=(acts, acts) + (flat,) * 6 + (planes,) * 3 + (flat,) * 3,
            check_vma=False,
        )(*arguments)

    return whole
```

```python
import math

import jax
import jax.numpy as jnp
from jax import lax
from jax.experimental import pallas as pl
from jax.experimental.pallas import tpu as pltpu
from jax.sharding import Mesh, PartitionSpec as P

D = 2560
HEAD_DIM = 256
WINDOW = 2048
STEP = 10
SEQ_LEN = 3072

NORM_EPS = 1e-06
BETA_ONE = 0.9
BETA_TWO = 0.95
ADAM_EPS = 1e-08
DECAY_RATE = 0.1
MASKED_SCORE = -1e30

LANES = 512
KEY_BLOCK = 768
PLANES = ("g", "h")
OWNERS = ("g", "h", "k", "c")
CHIPS = ("seq", "k")
GROUP = ("seq", "k", "c")
RING = ("seq", "h", "k")


def rotate(values, cosine, sine):
    half_dim = values.shape[-1] // 2
    first_half = values[..., :half_dim]
    second_half = values[..., half_dim:]
    return jnp.concatenate(
        [first_half * cosine - second_half * sine, second_half * cosine + first_half * sine],
        axis=-1,
    )


def doc_places(lengths_row, offsets):
    doc_ends = jnp.cumsum(lengths_row)
    passed = (doc_ends[None, :] <= offsets[:, None]).astype(jnp.int32)
    document = jnp.sum(passed, axis=1)
    starts = jnp.sum(passed * lengths_row[None, :], axis=1)
    return (document, offsets - starts)


def rope_angles(places, head_dim):
    freq_index = jnp.arange(head_dim // 2, dtype=jnp.float32)
    inverse = jnp.exp(freq_index * (-2.0 * math.log(10000.0) / head_dim))
    angles = places.astype(jnp.float32)[:, None] * inverse[None, :]
    return (jnp.cos(angles), jnp.sin(angles))


def adam_step(weight, first, second, grad, rate):
    first_new = BETA_ONE * first + (1.0 - BETA_ONE) * grad
    second_new = BETA_TWO * second + (1.0 - BETA_TWO) * grad * grad
    first_hat = first_new / (1.0 - BETA_ONE**STEP)
    second_hat = second_new / (1.0 - BETA_TWO**STEP)
    update = first_hat / (jnp.sqrt(second_hat) + ADAM_EPS)
    return (second_new, weight - rate * (update + DECAY_RATE * weight))


def glu_values(gate_in, up_in):
    return jax.nn.gelu(gate_in, approximate=True) * up_in


def low(value):
    return value.astype(jnp.bfloat16)


def wide(value):
    return value.astype(jnp.float32)


def dot(left, right, contract):
    return lax.dot_general(
        left, right, ((contract[:1], contract[1:]), ((), ())), preferred_element_type=jnp.float32
    )


def traded(axes, step):
    count = math.prod(lax.axis_size(axis) for axis in axes)
    return [(source, source ^ step) for source in range(count)]


def swapped(value, axis):
    return lax.ppermute(value, axis, [(0, 1), (1, 0)])


def after(value, *others):
    return lax.optimization_barrier((value,) + others)[0]


def doubled(value, axis, step, place):
    other = lax.ppermute(value, axis, traded((axis,), step))
    first = (lax.axis_index(axis) & step) == 0
    return jnp.stack([jnp.where(first, value, other), jnp.where(first, other, value)], axis=place)


def next_plane(block):
    count = math.prod(lax.axis_size(axis) for axis in PLANES)
    return lax.ppermute(block, PLANES, [(one, (one + 1) % count) for one in range(count)])


def joined_planes(blocks):
    count, rows = len(blocks), blocks[0].shape[0]
    whole = jnp.zeros((count * rows, blocks[0].shape[1]), blocks[0].dtype)
    for step, block in enumerate(blocks):
        start = lax.rem(lax.axis_index(PLANES) + (count - step), count) * rows
        whole = lax.dynamic_update_slice_in_dim(whole, block, start, 0)
    return whole


def spread_ring(value):
    chips = math.prod(lax.axis_size(axis) for axis in RING)
    place = lax.axis_index(RING)
    whole = jnp.zeros((chips,) + value.shape, value.dtype)
    for step in range(chips):
        arrived = lax.ppermute(value, RING, traded(RING, step)) if step else value
        whole = lax.dynamic_update_index_in_dim(whole, arrived, place ^ step, 0)
    return whole


def ring_sum(terms):
    chips = terms.shape[0]
    place = lax.axis_index(CHIPS)
    total = 0.0
    for step in range(chips):
        term = lax.dynamic_index_in_dim(terms, place ^ step, 0, keepdims=False)
        if step:
            term = lax.ppermute(term, CHIPS, traded(CHIPS, step))
        total = total + wide(term)
    return total


def exchanged(value, axes):
    return lax.all_to_all(value, axes, split_axis=0, concat_axis=0, tiled=True)


def half_sum(terms, axis, place):
    here = lax.axis_index(axis)
    kept = lax.dynamic_index_in_dim(terms, here, place, keepdims=False)
    given = lax.dynamic_index_in_dim(terms, 1 - here, place, keepdims=False)
    return low(wide(kept) + wide(swapped(given, axis)))


def mlp_chunks_kernel(slices, side_ref, weight_ref, gain_ref, gate_up_ref, down_ref):
    per_piece = pl.num_programs(1)
    index = side_ref[0] * pl.num_programs(0) + pl.program_id(0)
    index = index * per_piece + pl.program_id(1)
    width = weight_ref.shape[2]
    lane = pl.program_id(1) * width
    gain = gain_ref[...]
    for part in range(3):
        weight = wide(low(weight_ref[part]))
        if part < 2:
            weight = weight * gain
        weight = low(jnp.where(index < slices, weight, 0.0))
        if part < 2:
            place = pl.multiple_of(part * per_piece * width + lane, width)
            gate_up_ref[0, :, pl.ds(place, width)] = weight
        else:
            down_ref[0, :, pl.ds(pl.multiple_of(lane, width), width)] = weight


def mlp_chunks(weight, gain, side, members, piece):
    parts, rows, ff_width = weight.shape
    slices = ff_width // LANES
    per_piece = piece // LANES

    def weight_block(m, b, side_ref):
        return (0, 0, jnp.minimum((side_ref[0] * members + m) * per_piece + b, slices - 1))

    def out_block(m, b, side_ref):
        return (m, 0, 0)

    return pl.pallas_call(
        lambda *refs: mlp_chunks_kernel(slices, *refs),
        grid_spec=pltpu.PrefetchScalarGridSpec(
            num_scalar_prefetch=1,
            grid=(members, per_piece),
            in_specs=[
                pl.BlockSpec((parts, rows, LANES), weight_block),
                pl.BlockSpec((rows, 1), lambda m, b, side_ref: (0, 0)),
            ],
            out_specs=[
                pl.BlockSpec((1, rows, 2 * piece), out_block),
                pl.BlockSpec((1, rows, piece), out_block),
            ],
        ),
        out_shape=[
            jax.ShapeDtypeStruct((members, rows, 2 * piece), jnp.bfloat16),
            jax.ShapeDtypeStruct((members, rows, piece), jnp.bfloat16),
        ],
        compiler_params=pltpu.CompilerParams(vmem_limit_bytes=48 * 1024 * 1024),
        cost_estimate=pl.CostEstimate(
            flops=weight.size, bytes_accessed=3 * weight.size, transcendentals=0
        ),
        name="mlp_chunks",
    )(jnp.full((1,), side, jnp.int32), weight, gain)


def mlp_adam_kernel(rate, per_side, scaled, side_ref, ours_ref, theirs_ref, weight_ref, first_ref,
                    second_ref, gain_ref, *refs):
    grad_out, second_out, weight_out, dot_out = refs[-4:]
    block = pl.program_id(0)
    ours = block // per_side == side_ref[0]
    grad = wide(jnp.where(ours, ours_ref[0], theirs_ref[0]))
    weight = weight_ref[0]
    dot_part = jnp.sum(wide(low(weight)) * grad, axis=1, keepdims=True)
    dot_out[...] = jnp.where(block == 0, dot_part, dot_out[...] + dot_part)
    if scaled:
        grad = grad * gain_ref[...]
    grad_out[0] = grad
    second_out[0], weight_out[0] = adam_step(weight, first_ref[0], second_ref[0], grad, rate)


def mlp_adam(part, side, pieces, states, gain, rate, outs):
    _, rows, ff_width = states[0].shape
    members, _, piece = pieces[0].shape
    per_piece = piece // LANES
    per_side = members * per_piece

    def grad_block(own):
        def place(b, side_ref):
            used = (b // per_side == side_ref[0]) == own
            inner = jnp.where(used, b % per_side, 0)
            return (inner // per_piece, 0, inner % per_piece)

        return pl.BlockSpec((1, rows, LANES), place)

    state = pl.BlockSpec((1, rows, LANES), lambda b, side_ref: (part, 0, b))
    gains = pl.BlockSpec((rows, 1), lambda b, side_ref: (0, 0))
    size = rows * ff_width
    return pl.pallas_call(
        lambda *refs: mlp_adam_kernel(rate, per_side, part < 2, *refs),
        grid_spec=pltpu.PrefetchScalarGridSpec(
            num_scalar_prefetch=1,
            grid=(ff_width // LANES,),
            in_specs=[grad_block(True), grad_block(False), state, state, state, gains]
            + [pl.BlockSpec(memory_space=pl.ANY)] * len(outs),
            out_specs=[state, state, state, gains],
        ),
        out_shape=[jax.ShapeDtypeStruct(states[0].shape, jnp.float32)] * 3
        + [jax.ShapeDtypeStruct((rows, 1), jnp.float32)],
        input_output_aliases={7 + index: index for index in range(len(outs))},
        compiler_params=pltpu.CompilerParams(vmem_limit_bytes=48 * 1024 * 1024),
        cost_estimate=pl.CostEstimate(
            flops=20 * size, bytes_accessed=26 * size, transcendentals=size
        ),
        name="mlp_adam",
    )(jnp.full((1,), side, jnp.int32), *pieces, *states, gain, *outs)


def stacked_heads(ref):
    return jnp.concatenate([ref[:, :HEAD_DIM], ref[:, HEAD_DIM:]], axis=0)


def attend_kernel(query_ref, key_ref, value_t_ref, bias_ref, out_ref, lse_ref, score_ref):
    rows = query_ref.shape[0]
    queries = stacked_heads(query_ref)
    blocks = key_ref.shape[0] // KEY_BLOCK

    def first(block, top):
        part = pl.ds(pl.multiple_of(block * KEY_BLOCK, KEY_BLOCK), KEY_BLOCK)
        scores = dot(key_ref[part, :], queries, (1, 1)) + bias_ref[part, :]
        score_ref[part, :] = scores
        return jnp.maximum(top, jnp.max(scores, axis=0, keepdims=True))

    top = jnp.full((1, 2 * rows), -jnp.inf, jnp.float32)
    top = lax.fori_loop(0, blocks, first, top, unroll=2)

    def second(block, carry):
        total, mixed = carry
        part = pl.ds(pl.multiple_of(block * KEY_BLOCK, KEY_BLOCK), KEY_BLOCK)
        exps = jnp.exp(score_ref[part, :] - top)
        total = total + jnp.sum(exps, axis=0, keepdims=True)
        return total, mixed + dot(value_t_ref[:, part], low(exps), (1, 0))

    total, mixed = lax.fori_loop(
        0,
        blocks,
        second,
        (jnp.zeros((1, 2 * rows), jnp.float32), jnp.zeros((HEAD_DIM, 2 * rows), jnp.float32)),
        unroll=2,
    )
    mixed = low((mixed / total).T)
    out_ref[:, :HEAD_DIM] = mixed[:rows]
    out_ref[:, HEAD_DIM:] = mixed[rows:]
    lse_ref[0] = top + jnp.log(total)


def attend(queries, keys, values, bias):
    rows, width = queries.shape
    pairs = width // (2 * HEAD_DIM)
    count = keys.shape[0]

    def whole(shape):
        return pl.BlockSpec(shape, lambda p: (0,) * len(shape))

    pair = pl.BlockSpec((rows, 2 * HEAD_DIM), lambda p: (0, p))
    return pl.pallas_call(
        attend_kernel,
        grid=(pairs,),
        in_specs=[pair, whole(keys.shape), whole((HEAD_DIM, count)), whole(bias.shape)],
        out_specs=[pair, pl.BlockSpec((1, 1, 2 * rows), lambda p: (p, 0, 0))],
        out_shape=[
            jax.ShapeDtypeStruct((rows, width), jnp.bfloat16),
            jax.ShapeDtypeStruct((pairs, 1, 2 * rows), jnp.float32),
        ],
        scratch_shapes=[pltpu.VMEM((count, 2 * rows), jnp.float32)],
        compiler_params=pltpu.CompilerParams(vmem_limit_bytes=48 * 1024 * 1024),
        cost_estimate=pl.CostEstimate(
            flops=4 * rows * width * count,
            bytes_accessed=8 * rows * width + 12 * bias.size,
            transcendentals=pairs * bias.size,
        ),
        name="attend",
    )(queries, keys, values.T, bias)


def attend_back_kernel(query_ref, grad_ref, key_ref, key_t_ref, value_ref, bias_ref, lse_ref,
                       delta_ref, grad_query_ref, grad_window_ref):
    rows = query_ref.shape[0]
    queries = stacked_heads(query_ref)
    grads = stacked_heads(grad_ref)
    blocks = key_ref.shape[0] // KEY_BLOCK

    @pl.when(pl.program_id(0) == 0)
    def _():
        grad_window_ref[...] = jnp.zeros_like(grad_window_ref)

    lse = lse_ref[0]
    delta = delta_ref[0]

    def body(block, grad_query):
        part = pl.ds(pl.multiple_of(block * KEY_BLOCK, KEY_BLOCK), KEY_BLOCK)
        probs = jnp.exp(dot(key_ref[part, :], queries, (1, 1)) + bias_ref[part, :] - lse)
        grad_probs = dot(value_ref[part, :], grads, (1, 1))
        grad_scores = low(probs * (grad_probs - delta))
        grad_window_ref[part, :HEAD_DIM] += dot(grad_scores, queries, (1, 0))
        grad_window_ref[part, HEAD_DIM:] += dot(low(probs), grads, (1, 0))
        return grad_query + dot(key_t_ref[:, part], grad_scores, (1, 0))

    grad_query = jnp.zeros((HEAD_DIM, 2 * rows), jnp.float32)
    grad_query = lax.fori_loop(0, blocks, body, grad_query, unroll=2).T
    grad_query_ref[:, :HEAD_DIM] = grad_query[:rows]
    grad_query_ref[:, HEAD_DIM:] = grad_query[rows:]


def attend_back(queries, grads, keys, values, bias, lse, delta):
    rows, width = queries.shape
    pairs = width // (2 * HEAD_DIM)
    count = keys.shape[0]

    def whole(shape):
        return pl.BlockSpec(shape, lambda p: (0,) * len(shape))

    pair = pl.BlockSpec((rows, 2 * HEAD_DIM), lambda p: (0, p))
    line = pl.BlockSpec((1, 1, 2 * rows), lambda p: (p, 0, 0))
    return pl.pallas_call(
        attend_back_kernel,
        grid=(pairs,),
        in_specs=[
            pair,
            pair,
            whole(keys.shape),
            whole((HEAD_DIM, count)),
            whole(values.shape),
            whole(bias.shape),
            line,
            line,
        ],
        out_specs=[pair, whole((count, 2 * HEAD_DIM))],
        out_shape=[
            jax.ShapeDtypeStruct((rows, width), jnp.float32),
            jax.ShapeDtypeStruct((count, 2 * HEAD_DIM), jnp.float32),
        ],
        compiler_params=pltpu.CompilerParams(vmem_limit_bytes=48 * 1024 * 1024),
        cost_estimate=pl.CostEstimate(
            flops=10 * rows * width * count,
            bytes_accessed=8 * rows * width + 16 * bias.size,
            transcendentals=pairs * bias.size,
        ),
        name="attend_back",
    )(queries, grads, keys, keys.T, values, bias, lse, delta)


def on_device(
    hidden_in,
    cotangent,
    lengths,
    weight_qkv,
    first_qkv,
    second_qkv,
    weight_out,
    first_out,
    second_out,
    weight_mlp,
    first_mlp,
    second_mlp,
    norm_gains,
    first_gains,
    second_gains,
):
    tok_rows = hidden_in.shape[2]
    width = hidden_in.shape[3]
    head_count = width // HEAD_DIM
    sides = lax.axis_size("seq")
    columns = lax.axis_size("k")
    members = columns * lax.axis_size("c")
    planes = lax.axis_size("g") * lax.axis_size("h")
    owner_count = planes * members
    blocks_in_side = lax.axis_size("h") * members
    side = lax.axis_index("seq")
    core = lax.axis_index("c")
    packed_index = lax.axis_index("g")
    place = lax.axis_index(("h", "k", "c"))
    own_rows = weight_mlp.shape[0]
    ff_width = weight_mlp.shape[2]
    piece = -(-ff_width // (sides * members * LANES)) * LANES

    gains_low = wide(low(norm_gains))
    gain_one = gains_low[:, :1]
    gain_two = gains_low[:, 1:]
    qkv_low = wide(low(weight_qkv))
    def regrouped(value, outer, inner):
        value = value.reshape(value.shape[0], outer, inner, own_rows).transpose(0, 2, 1, 3)
        return value.reshape(value.shape[0], outer * inner * own_rows)

    mlp_planes = weight_mlp.transpose(1, 0, 2)
    gate_up_chunks, down_chunks = mlp_chunks(mlp_planes, gain_two, side, members, piece)

    def to_members(chunks):
        return exchanged(chunks, ("k", "c")).reshape(members * own_rows, chunks.shape[2])

    incoming = cotangent.reshape(tok_rows, width)
    def own_half(weight):
        half = weight.shape[1] // sides
        return lax.dynamic_slice_in_dim(weight, side * half, half, 1)

    def gathered_group(weight):
        half = weight.shape[1]
        weight = lax.all_gather(weight, GROUP, axis=0, tiled=True)
        return weight.reshape(sides, owner_count * own_rows, half)

    gate_up_blocks = [to_members(gate_up_chunks)]
    qkv_rows = lax.all_gather(own_half(low(qkv_low * gain_one)), PLANES, axis=0, tiled=True)
    qkv_halves = gathered_group(after(qkv_rows, gate_up_chunks))
    gate_up_blocks.append(next_plane(after(gate_up_blocks[0], qkv_rows)))
    down_blocks = [to_members(down_chunks)]
    down_blocks.append(next_plane(down_blocks[0]))
    out_rows = own_half(after(low(weight_out), qkv_halves))
    out_halves = gathered_group(lax.all_gather(out_rows, PLANES, axis=0, tiled=True))
    incoming_columns = doubled(incoming, "k", 1, 0)

    tokens = wide(hidden_in.reshape(tok_rows, width))
    lengths_row = lax.dynamic_index_in_dim(lengths, packed_index, 0, keepdims=False)
    row_numbers = jnp.arange(tok_rows, dtype=jnp.int32)
    query_docs, query_places = doc_places(
        lengths_row, (place * sides + side) * tok_rows + row_numbers
    )
    blocks = jnp.arange(blocks_in_side, dtype=jnp.int32)[None, :] * sides
    blocks = blocks + jnp.arange(sides, dtype=jnp.int32)[:, None]
    key_offsets = (blocks[:, :, None] * tok_rows + row_numbers).reshape(-1)
    key_docs, key_places = doc_places(lengths_row, key_offsets)
    distance = query_places[:, None] - key_places[None, :]
    allowed = (query_docs[:, None] == key_docs[None, :]) & (distance >= 0) & (distance < WINDOW)
    cosine, sine = rope_angles(query_places, HEAD_DIM)
    query_scale = HEAD_DIM ** (-0.5)

    factor_one = lax.rsqrt(jnp.mean(tokens * tokens, axis=-1, keepdims=True) + NORM_EPS)
    normed_one = low(tokens * factor_one)
    normed_one = after(normed_one, incoming_columns, gate_up_blocks[1], down_blocks[1])
    rows = regrouped(normed_one, planes, members)
    projected = jnp.concatenate([dot(rows, half, (1, 0)) for half in qkv_halves], axis=1)
    key_pre = projected[:, width : width + HEAD_DIM]
    value_low = low(projected[:, width + HEAD_DIM :])
    key_low = low(rotate(key_pre, cosine, sine))
    window_kv = spread_ring(jnp.concatenate([key_low, value_low], axis=1))
    window_kv = doubled(window_kv, "c", 1, 1)
    window_kv = window_kv.reshape(SEQ_LEN, 2 * HEAD_DIM)
    gate_up_blocks.append(next_plane(after(gate_up_blocks[1], projected)))
    for _ in range(planes - 3):
        gate_up_blocks.append(next_plane(gate_up_blocks[-1]))
    down_blocks.append(next_plane(after(down_blocks[1], projected)))
    for _ in range(planes - 3):
        down_blocks.append(next_plane(down_blocks[-1]))
    gate_up_own = joined_planes(gate_up_blocks)
    down_own = joined_planes(down_blocks)
    incoming_sides = doubled(after(incoming_columns, window_kv), "seq", 1, 0)
    query_pre = projected[:, :width].reshape(tok_rows, head_count, HEAD_DIM)
    queries = low(rotate(query_pre, cosine[:, None, :], sine[:, None, :]) * query_scale)
    queries = after(queries.reshape(tok_rows, width), gate_up_blocks[2], down_blocks[2])
    incoming_all = doubled(incoming_sides, "c", 1, incoming_sides.ndim - 2)
    incoming_all = incoming_all.reshape(sides * members * tok_rows, width)
    keys_win = window_kv[:, :HEAD_DIM]
    values_win = window_kv[:, HEAD_DIM:]
    bias = jnp.where(allowed.T, 0.0, MASKED_SCORE)
    bias = jnp.concatenate([bias, bias], axis=1)
    attn_low, log_total = attend(queries, keys_win, values_win, bias)
    attn_low = after(attn_low, incoming_sides)
    rows = regrouped(attn_low, planes, members)
    branch = [dot(rows, half, (1, 0)) for half in out_halves]
    middle = tokens + jnp.concatenate(branch, axis=1)

    factor_two = lax.rsqrt(jnp.mean(middle * middle, axis=-1, keepdims=True) + NORM_EPS)
    normed_two = low(middle * factor_two)
    normed_two_all = lax.all_gather(normed_two, GROUP, axis=0, tiled=True)
    grad_act = low(dot(incoming_all, down_own, (1, 0)))
    gate_up = dot(after(normed_two_all, down_own, incoming_all), gate_up_own, (1, 0))
    activated, glu_back = jax.vjp(glu_values, gate_up[:, :piece], gate_up[:, piece:])
    activated_low = low(activated)
    def to_owners(term):
        return lax.psum_scatter(term, PLANES, scatter_dimension=0, tiled=True)

    attn_all = lax.all_gather(after(attn_low, gate_up), GROUP, axis=0, tiled=True)
    down_term = after(low(dot(incoming_all, activated_low, (0, 0))), attn_all)
    down_rows = to_owners(down_term)
    grad_gate, grad_up = glu_back(wide(after(grad_act, down_term)))
    grad_gate_up = low(jnp.concatenate([grad_gate, grad_up], axis=1))

    def in_plane(term, *others):
        term = term.reshape(members, own_rows, term.shape[1])
        ours = exchanged(after(term, *others), ("k", "c"))
        return (ours, swapped(ours, "seq"))

    def group_terms(hidden, weight):
        by_core = hidden.reshape(sides * columns, 2, tok_rows, hidden.shape[1])

        def one_core(which):
            rows = lax.dynamic_index_in_dim(by_core, which, 1, keepdims=False)
            return dot(rows.reshape(-1, hidden.shape[1]), weight, (1, 1))

        given = swapped(low(one_core(1 - core)), "c")
        return low(one_core(core) + wide(given)).reshape(sides * columns, tok_rows, width)

    terms = group_terms(grad_gate_up, gate_up_own)
    place = lax.axis_index(CHIPS)
    grad_normed_two = wide(lax.dynamic_index_in_dim(terms, place, 0, keepdims=False))
    arrived = []
    for step in range(1, sides * columns):
        term = lax.dynamic_index_in_dim(terms, place ^ step, 0, keepdims=False)
        if step == sides * columns - 1:
            term = after(term, *arrived)
        arrived.append(lax.ppermute(term, CHIPS, traded(CHIPS, step)))
    late = after(grad_gate_up, *arrived[:-1])
    gate_term = low(dot(normed_two_all, late[:, :piece], (0, 0)))
    up_term = low(dot(normed_two_all, late[:, piece:], (0, 0)))
    grad_normed_two = grad_normed_two + sum(wide(term) for term in arrived)
    grad_normed_two = after(grad_normed_two, gate_term, up_term)

    gate_rows = to_owners(gate_term)
    up_rows = to_owners(up_term)
    grad_middle = (
        wide(incoming)
        + factor_two * grad_normed_two
        - middle * factor_two**3 * jnp.mean(grad_normed_two * middle, axis=-1, keepdims=True)
    )

    shares = sides * members

    def by_column(terms):
        terms = terms.reshape(tok_rows, shares, terms.shape[1] // shares).transpose(1, 0, 2)
        return exchanged(terms, GROUP).reshape(shares * tok_rows, -1)

    def to_rows(total):
        total = exchanged(total.reshape(owner_count, own_rows, -1), OWNERS)
        return low(jnp.sum(wide(total.reshape(planes, members, own_rows, -1)), axis=0))

    def joined(total):
        total = doubled(total, "seq", 1, 0).reshape(shares, own_rows, -1)
        return wide(total.transpose(1, 0, 2).reshape(own_rows, -1))

    grad_branch_low = low(grad_middle)
    out_columns = by_column(grad_branch_low)
    half = width // sides
    grad_mixed = sum(
        dot(grad_branch_low[:, index * half : (index + 1) * half], out_halves[index], (1, 1))
        for index in range(sides)
    )
    grad_mixed_low = regrouped(low(grad_mixed), members, planes)
    delta = (wide(grad_mixed_low) * wide(attn_low)).reshape(tok_rows, head_count, HEAD_DIM)
    delta = jnp.sum(delta, axis=-1).T.reshape(log_total.shape)
    grad_query, grad_window = attend_back(
        queries, grad_mixed_low, keys_win, values_win, bias, log_total, delta
    )
    normed_one_columns = doubled(after(normed_one, grad_normed_two), "k", 1, 0)
    normed_one_sides = doubled(normed_one_columns, "seq", 1, 0)
    branch_terms = group_terms(after(activated_low, grad_window), down_own)
    down_pieces = in_plane(down_rows, grad_window)
    out_total = to_rows(low(dot(attn_all, out_columns, (0, 0))))
    grad_window = after(low(grad_window), normed_one_sides, out_total)
    normed_one_others = swapped(normed_one_sides, "c")
    grad_window = half_sum(grad_window.reshape(-1, 2, tok_rows, 2 * HEAD_DIM), "c", 1)
    grad_window = grad_window.reshape(sides, -1, columns, tok_rows, 2 * HEAD_DIM)
    grad_window = grad_window.swapaxes(1, 2).reshape(sides * columns, -1, tok_rows, 2 * HEAD_DIM)
    grad_local = wide(half_sum(low(ring_sum(grad_window)), "h", 0))
    grad_query = grad_query.reshape(tok_rows, head_count, HEAD_DIM)
    grad_query_pre = rotate(
        grad_query * query_scale, cosine[:, None, :], -sine[:, None, :]
    ).reshape(tok_rows, width)
    grad_key_pre = rotate(grad_local[:, :HEAD_DIM], cosine, -sine)
    grad_proj = low(
        jnp.concatenate([grad_query_pre, grad_key_pre, grad_local[:, HEAD_DIM:]], axis=1)
    )

    mlp_states = (mlp_planes, first_mlp.transpose(1, 0, 2), second_mlp.transpose(1, 0, 2))
    rate_main = 2.0 * D ** (-0.5)

    def mlp_updated(part, pieces, outs):
        *outs, gain_dot = mlp_adam(part, side, pieces, mlp_states, gain_two, rate_main, outs)
        return outs, gain_dot

    qkv_columns = by_column(after(grad_proj, down_pieces[0], normed_one_others))
    mlp_outs, _ = mlp_updated(2, down_pieces, ())
    by_core = after(qkv_columns, *mlp_outs).reshape(sides * columns, 2, tok_rows, -1)

    def one_core_total(rows, which):
        columns_there = lax.dynamic_index_in_dim(by_core, which, 1, keepdims=False)
        return dot(rows.reshape(-1, width), columns_there.reshape(-1, by_core.shape[3]), (0, 0))

    qkv_total = one_core_total(normed_one_sides, core)
    qkv_total = low(qkv_total + one_core_total(normed_one_others, 1 - core))
    branch = ring_sum(after(branch_terms, qkv_columns))
    gate_pieces = in_plane(gate_rows, qkv_columns)
    up_pieces = in_plane(up_rows, gate_pieces[0])
    qkv_total = to_rows(after(qkv_total, up_pieces[0], gate_pieces[1]))
    gate_pieces = lax.optimization_barrier((*gate_pieces, branch))[:2]
    mlp_outs, gate_dot = mlp_updated(0, gate_pieces, mlp_outs)
    (grad_mlp, second_new_mlp, new_mlp), up_dot = mlp_updated(1, up_pieces, mlp_outs)
    grad_gain_two = gate_dot + up_dot
    qkv_total = after(qkv_total, up_dot)
    grad_out = joined(out_total)

    grad_qkv = joined(qkv_total)
    hidden_out = low(middle + branch).reshape(1, 1, tok_rows, width)

    half = grad_proj.shape[1] // sides
    grad_normed = sum(
        dot(grad_proj[:, index * half : (index + 1) * half], qkv_halves[index], (1, 1))
        for index in range(sides)
    )
    grad_normed = regrouped(grad_normed, members, planes)
    hidden_grad = (
        grad_middle
        + factor_one * grad_normed
        - tokens * factor_one**3 * jnp.mean(grad_normed * tokens, axis=-1, keepdims=True)
    ).reshape(1, 1, tok_rows, width)

    rate_out = 2.0 * max(1, 6 * D // WINDOW) ** (-0.5)
    rate_gains = 0.4
    grad_gain_one = jnp.sum(qkv_low * grad_qkv, axis=1, keepdims=True)
    grad_qkv = grad_qkv * gain_one
    second_new_qkv, new_qkv = adam_step(weight_qkv, first_qkv, second_qkv, grad_qkv, rate_main)
    second_new_out, new_out = adam_step(weight_out, first_out, second_out, grad_out, rate_out)
    grad_gains = jnp.concatenate([grad_gain_one, grad_gain_two], axis=1)
    second_new_gains, new_gains = adam_step(
        norm_gains, first_gains, second_gains, grad_gains, rate_gains
    )
    return (
        hidden_out,
        hidden_grad,
        grad_qkv,
        second_new_qkv,
        new_qkv,
        grad_out,
        second_new_out,
        new_out,
        grad_mlp.transpose(1, 0, 2),
        second_new_mlp.transpose(1, 0, 2),
        new_mlp.transpose(1, 0, 2),
        grad_gains,
        second_new_gains,
        new_gains,
    )


def solution(mesh):
    seq_count, owner_count = mesh.devices.shape

    def whole(*arguments):
        members = SEQ_LEN // (seq_count * arguments[0].shape[2])
        shape = (seq_count, owner_count // members, members // 4, 2, 2)
        split = Mesh(mesh.devices.reshape(shape), ("seq", "g", "h", "k", "c"))
        acts = P(OWNERS, "seq", None, None)
        flat = P(OWNERS, None)
        planes = P(OWNERS, None, None)
        return jax.shard_map(
            on_device,
            mesh=split,
            in_specs=(acts, acts, P()) + (flat,) * 6 + (planes,) * 3 + (flat,) * 3,
            out_specs=(acts, acts) + (flat,) * 6 + (planes,) * 3 + (flat,) * 3,
            check_vma=False,
        )(*arguments)

    return whole
```

```python
import math

import jax
import jax.numpy as jnp
from jax import lax
from jax.experimental import pallas as pl
from jax.experimental.pallas import tpu as pltpu
from jax.sharding import Mesh, PartitionSpec as P

D = 2560
HEAD_DIM = 256
WINDOW = 2048
STEP = 10
SEQ_LEN = 3072

NORM_EPS = 1e-06
BETA_ONE = 0.9
BETA_TWO = 0.95
ADAM_EPS = 1e-08
DECAY_RATE = 0.1
MASKED_SCORE = -1e30

LANES = 512
KEY_BLOCK = 768
PLANES = ("g", "h")
OWNERS = ("g", "h", "k", "c")
CHIPS = ("seq", "k")
GROUP = ("seq", "k", "c")
RING = ("seq", "h", "k")


def rotate(values, cosine, sine):
    half_dim = values.shape[-1] // 2
    first_half = values[..., :half_dim]
    second_half = values[..., half_dim:]
    return jnp.concatenate(
        [first_half * cosine - second_half * sine, second_half * cosine + first_half * sine],
        axis=-1,
    )


def doc_places(lengths_row, offsets):
    doc_ends = jnp.cumsum(lengths_row)
    passed = (doc_ends[None, :] <= offsets[:, None]).astype(jnp.int32)
    document = jnp.sum(passed, axis=1)
    starts = jnp.sum(passed * lengths_row[None, :], axis=1)
    return (document, offsets - starts)


def rope_angles(places, head_dim):
    freq_index = jnp.arange(head_dim // 2, dtype=jnp.float32)
    inverse = jnp.exp(freq_index * (-2.0 * math.log(10000.0) / head_dim))
    angles = places.astype(jnp.float32)[:, None] * inverse[None, :]
    return (jnp.cos(angles), jnp.sin(angles))


def adam_step(weight, first, second, grad, rate):
    first_new = BETA_ONE * first + (1.0 - BETA_ONE) * grad
    second_new = BETA_TWO * second + (1.0 - BETA_TWO) * grad * grad
    first_hat = first_new / (1.0 - BETA_ONE**STEP)
    second_hat = second_new / (1.0 - BETA_TWO**STEP)
    update = first_hat / (jnp.sqrt(second_hat) + ADAM_EPS)
    return (second_new, weight - rate * (update + DECAY_RATE * weight))


def glu_values(gate_in, up_in):
    return jax.nn.gelu(gate_in, approximate=True) * up_in


def low(value):
    return value.astype(jnp.bfloat16)


def wide(value):
    return value.astype(jnp.float32)


def dot(left, right, contract):
    return lax.dot_general(
        left, right, ((contract[:1], contract[1:]), ((), ())), preferred_element_type=jnp.float32
    )


def traded(axes, step):
    count = math.prod(lax.axis_size(axis) for axis in axes)
    return [(source, source ^ step) for source in range(count)]


def swapped(value, axis):
    return lax.ppermute(value, axis, [(0, 1), (1, 0)])


def after(value, *others):
    return lax.optimization_barrier((value,) + others)[0]


def doubled(value, axis, step, place):
    other = lax.ppermute(value, axis, traded((axis,), step))
    first = (lax.axis_index(axis) & step) == 0
    return jnp.stack([jnp.where(first, value, other), jnp.where(first, other, value)], axis=place)


def next_plane(block):
    count = math.prod(lax.axis_size(axis) for axis in PLANES)
    return lax.ppermute(block, PLANES, [(one, (one + 1) % count) for one in range(count)])


def joined_planes(blocks):
    count, rows = len(blocks), blocks[0].shape[0]
    whole = jnp.zeros((count * rows, blocks[0].shape[1]), blocks[0].dtype)
    for step, block in enumerate(blocks):
        start = lax.rem(lax.axis_index(PLANES) + (count - step), count) * rows
        whole = lax.dynamic_update_slice_in_dim(whole, block, start, 0)
    return whole


def spread_ring(value):
    chips = math.prod(lax.axis_size(axis) for axis in RING)
    place = lax.axis_index(RING)
    whole = jnp.zeros((chips,) + value.shape, value.dtype)
    for step in range(chips):
        arrived = lax.ppermute(value, RING, traded(RING, step)) if step else value
        whole = lax.dynamic_update_index_in_dim(whole, arrived, place ^ step, 0)
    return whole


def ring_sum(terms):
    chips = terms.shape[0]
    place = lax.axis_index(CHIPS)
    total = 0.0
    for step in range(chips):
        term = lax.dynamic_index_in_dim(terms, place ^ step, 0, keepdims=False)
        if step:
            term = lax.ppermute(term, CHIPS, traded(CHIPS, step))
        total = total + wide(term)
    return total


def exchanged(value, axes):
    return lax.all_to_all(value, axes, split_axis=0, concat_axis=0, tiled=True)


def half_sum(terms, axis, place):
    here = lax.axis_index(axis)
    kept = lax.dynamic_index_in_dim(terms, here, place, keepdims=False)
    given = lax.dynamic_index_in_dim(terms, 1 - here, place, keepdims=False)
    return low(wide(kept) + wide(swapped(given, axis)))


def mlp_chunks_kernel(slices, side_ref, weight_ref, gain_ref, gate_up_ref, down_ref):
    per_piece = pl.num_programs(1)
    index = side_ref[0] * pl.num_programs(0) + pl.program_id(0)
    index = index * per_piece + pl.program_id(1)
    width = weight_ref.shape[2]
    lane = pl.program_id(1) * width
    gain = gain_ref[...]
    for part in range(3):
        weight = wide(low(weight_ref[part]))
        if part < 2:
            weight = weight * gain
        weight = low(jnp.where(index < slices, weight, 0.0))
        if part < 2:
            place = pl.multiple_of(part * per_piece * width + lane, width)
            gate_up_ref[0, :, pl.ds(place, width)] = weight
        else:
            down_ref[0, :, pl.ds(pl.multiple_of(lane, width), width)] = weight


def mlp_chunks(weight, gain, side, members, piece):
    parts, rows, ff_width = weight.shape
    slices = ff_width // LANES
    per_piece = piece // LANES

    def weight_block(m, b, side_ref):
        return (0, 0, jnp.minimum((side_ref[0] * members + m) * per_piece + b, slices - 1))

    def out_block(m, b, side_ref):
        return (m, 0, 0)

    return pl.pallas_call(
        lambda *refs: mlp_chunks_kernel(slices, *refs),
        grid_spec=pltpu.PrefetchScalarGridSpec(
            num_scalar_prefetch=1,
            grid=(members, per_piece),
            in_specs=[
                pl.BlockSpec((parts, rows, LANES), weight_block),
                pl.BlockSpec((rows, 1), lambda m, b, side_ref: (0, 0)),
            ],
            out_specs=[
                pl.BlockSpec((1, rows, 2 * piece), out_block),
                pl.BlockSpec((1, rows, piece), out_block),
            ],
        ),
        out_shape=[
            jax.ShapeDtypeStruct((members, rows, 2 * piece), jnp.bfloat16),
            jax.ShapeDtypeStruct((members, rows, piece), jnp.bfloat16),
        ],
        compiler_params=pltpu.CompilerParams(vmem_limit_bytes=48 * 1024 * 1024),
        cost_estimate=pl.CostEstimate(
            flops=weight.size, bytes_accessed=3 * weight.size, transcendentals=0
        ),
        name="mlp_chunks",
    )(jnp.full((1,), side, jnp.int32), weight, gain)


def mlp_adam_kernel(rate, per_side, scaled, side_ref, ours_ref, theirs_ref, weight_ref, first_ref,
                    second_ref, gain_ref, *refs):
    grad_out, second_out, weight_out, dot_out = refs[-4:]
    block = pl.program_id(0)
    ours = block // per_side == side_ref[0]
    grad = wide(jnp.where(ours, ours_ref[0], theirs_ref[0]))
    weight = weight_ref[0]
    dot_part = jnp.sum(wide(low(weight)) * grad, axis=1, keepdims=True)
    dot_out[...] = jnp.where(block == 0, dot_part, dot_out[...] + dot_part)
    if scaled:
        grad = grad * gain_ref[...]
    grad_out[0] = grad
    second_out[0], weight_out[0] = adam_step(weight, first_ref[0], second_ref[0], grad, rate)


def mlp_adam(part, side, pieces, states, gain, rate, outs):
    _, rows, ff_width = states[0].shape
    members, _, piece = pieces[0].shape
    per_piece = piece // LANES
    per_side = members * per_piece

    def grad_block(own):
        def place(b, side_ref):
            used = (b // per_side == side_ref[0]) == own
            inner = jnp.where(used, b % per_side, 0)
            return (inner // per_piece, 0, inner % per_piece)

        return pl.BlockSpec((1, rows, LANES), place)

    state = pl.BlockSpec((1, rows, LANES), lambda b, side_ref: (part, 0, b))
    gains = pl.BlockSpec((rows, 1), lambda b, side_ref: (0, 0))
    size = rows * ff_width
    return pl.pallas_call(
        lambda *refs: mlp_adam_kernel(rate, per_side, part < 2, *refs),
        grid_spec=pltpu.PrefetchScalarGridSpec(
            num_scalar_prefetch=1,
            grid=(ff_width // LANES,),
            in_specs=[grad_block(True), grad_block(False), state, state, state, gains]
            + [pl.BlockSpec(memory_space=pl.ANY)] * len(outs),
            out_specs=[state, state, state, gains],
        ),
        out_shape=[jax.ShapeDtypeStruct(states[0].shape, jnp.float32)] * 3
        + [jax.ShapeDtypeStruct((rows, 1), jnp.float32)],
        input_output_aliases={7 + index: index for index in range(len(outs))},
        compiler_params=pltpu.CompilerParams(vmem_limit_bytes=48 * 1024 * 1024),
        cost_estimate=pl.CostEstimate(
            flops=20 * size, bytes_accessed=26 * size, transcendentals=size
        ),
        name="mlp_adam",
    )(jnp.full((1,), side, jnp.int32), *pieces, *states, gain, *outs)


def stacked_heads(ref):
    return jnp.concatenate([ref[:, :HEAD_DIM], ref[:, HEAD_DIM:]], axis=0)


def attend_kernel(query_ref, key_ref, value_t_ref, bias_ref, out_ref, lse_ref, score_ref):
    rows = query_ref.shape[0]
    queries = stacked_heads(query_ref)
    blocks = key_ref.shape[0] // KEY_BLOCK

    def first(block, top):
        part = pl.ds(pl.multiple_of(block * KEY_BLOCK, KEY_BLOCK), KEY_BLOCK)
        scores = dot(key_ref[part, :], queries, (1, 1)) + bias_ref[part, :]
        score_ref[part, :] = scores
        return jnp.maximum(top, jnp.max(scores, axis=0, keepdims=True))

    top = jnp.full((1, 2 * rows), -jnp.inf, jnp.float32)
    top = lax.fori_loop(0, blocks, first, top, unroll=2)

    def second(block, carry):
        total, mixed = carry
        part = pl.ds(pl.multiple_of(block * KEY_BLOCK, KEY_BLOCK), KEY_BLOCK)
        exps = jnp.exp(score_ref[part, :] - top)
        total = total + jnp.sum(exps, axis=0, keepdims=True)
        return total, mixed + dot(value_t_ref[:, part], low(exps), (1, 0))

    total, mixed = lax.fori_loop(
        0,
        blocks,
        second,
        (jnp.zeros((1, 2 * rows), jnp.float32), jnp.zeros((HEAD_DIM, 2 * rows), jnp.float32)),
        unroll=2,
    )
    mixed = low((mixed / total).T)
    out_ref[:, :HEAD_DIM] = mixed[:rows]
    out_ref[:, HEAD_DIM:] = mixed[rows:]
    lse_ref[0] = top + jnp.log(total)


def attend(queries, keys, values, bias):
    rows, width = queries.shape
    pairs = width // (2 * HEAD_DIM)
    count = keys.shape[0]

    def whole(shape):
        return pl.BlockSpec(shape, lambda p: (0,) * len(shape))

    pair = pl.BlockSpec((rows, 2 * HEAD_DIM), lambda p: (0, p))
    return pl.pallas_call(
        attend_kernel,
        grid=(pairs,),
        in_specs=[pair, whole(keys.shape), whole((HEAD_DIM, count)), whole(bias.shape)],
        out_specs=[pair, pl.BlockSpec((1, 1, 2 * rows), lambda p: (p, 0, 0))],
        out_shape=[
            jax.ShapeDtypeStruct((rows, width), jnp.bfloat16),
            jax.ShapeDtypeStruct((pairs, 1, 2 * rows), jnp.float32),
        ],
        scratch_shapes=[pltpu.VMEM((count, 2 * rows), jnp.float32)],
        compiler_params=pltpu.CompilerParams(vmem_limit_bytes=48 * 1024 * 1024),
        cost_estimate=pl.CostEstimate(
            flops=4 * rows * width * count,
            bytes_accessed=8 * rows * width + 12 * bias.size,
            transcendentals=pairs * bias.size,
        ),
        name="attend",
    )(queries, keys, values.T, bias)


def attend_back_kernel(query_ref, grad_ref, key_ref, key_t_ref, value_ref, bias_ref, lse_ref,
                       delta_ref, grad_query_ref, grad_window_ref):
    rows = query_ref.shape[0]
    queries = stacked_heads(query_ref)
    grads = stacked_heads(grad_ref)
    blocks = key_ref.shape[0] // KEY_BLOCK

    @pl.when(pl.program_id(0) == 0)
    def _():
        grad_window_ref[...] = jnp.zeros_like(grad_window_ref)

    lse = lse_ref[0]
    delta = delta_ref[0]

    def body(block, grad_query):
        part = pl.ds(pl.multiple_of(block * KEY_BLOCK, KEY_BLOCK), KEY_BLOCK)
        probs = jnp.exp(dot(key_ref[part, :], queries, (1, 1)) + bias_ref[part, :] - lse)
        grad_probs = dot(value_ref[part, :], grads, (1, 1))
        grad_scores = low(probs * (grad_probs - delta))
        grad_window_ref[part, :HEAD_DIM] += dot(grad_scores, queries, (1, 0))
        grad_window_ref[part, HEAD_DIM:] += dot(low(probs), grads, (1, 0))
        return grad_query + dot(key_t_ref[:, part], grad_scores, (1, 0))

    grad_query = jnp.zeros((HEAD_DIM, 2 * rows), jnp.float32)
    grad_query = lax.fori_loop(0, blocks, body, grad_query, unroll=2).T
    grad_query_ref[:, :HEAD_DIM] = grad_query[:rows]
    grad_query_ref[:, HEAD_DIM:] = grad_query[rows:]


def attend_back(queries, grads, keys, values, bias, lse, delta):
    rows, width = queries.shape
    pairs = width // (2 * HEAD_DIM)
    count = keys.shape[0]

    def whole(shape):
        return pl.BlockSpec(shape, lambda p: (0,) * len(shape))

    pair = pl.BlockSpec((rows, 2 * HEAD_DIM), lambda p: (0, p))
    line = pl.BlockSpec((1, 1, 2 * rows), lambda p: (p, 0, 0))
    return pl.pallas_call(
        attend_back_kernel,
        grid=(pairs,),
        in_specs=[
            pair,
            pair,
            whole(keys.shape),
            whole((HEAD_DIM, count)),
            whole(values.shape),
            whole(bias.shape),
            line,
            line,
        ],
        out_specs=[pair, whole((count, 2 * HEAD_DIM))],
        out_shape=[
            jax.ShapeDtypeStruct((rows, width), jnp.float32),
            jax.ShapeDtypeStruct((count, 2 * HEAD_DIM), jnp.float32),
        ],
        compiler_params=pltpu.CompilerParams(vmem_limit_bytes=48 * 1024 * 1024),
        cost_estimate=pl.CostEstimate(
            flops=10 * rows * width * count,
            bytes_accessed=8 * rows * width + 16 * bias.size,
            transcendentals=pairs * bias.size,
        ),
        name="attend_back",
    )(queries, grads, keys, keys.T, values, bias, lse, delta)


def on_device(
    hidden_in,
    cotangent,
    lengths,
    weight_qkv,
    first_qkv,
    second_qkv,
    weight_out,
    first_out,
    second_out,
    weight_mlp,
    first_mlp,
    second_mlp,
    norm_gains,
    first_gains,
    second_gains,
):
    tok_rows = hidden_in.shape[2]
    width = hidden_in.shape[3]
    head_count = width // HEAD_DIM
    sides = lax.axis_size("seq")
    columns = lax.axis_size("k")
    members = columns * lax.axis_size("c")
    planes = lax.axis_size("g") * lax.axis_size("h")
    owner_count = planes * members
    blocks_in_side = lax.axis_size("h") * members
    side = lax.axis_index("seq")
    core = lax.axis_index("c")
    packed_index = lax.axis_index("g")
    place = lax.axis_index(("h", "k", "c"))
    own_rows = weight_mlp.shape[0]
    ff_width = weight_mlp.shape[2]
    piece = -(-ff_width // (sides * members * LANES)) * LANES

    gains_low = wide(low(norm_gains))
    gain_one = gains_low[:, :1]
    gain_two = gains_low[:, 1:]
    qkv_low = wide(low(weight_qkv))
    def regrouped(value, outer, inner):
        value = value.reshape(value.shape[0], outer, inner, own_rows).transpose(0, 2, 1, 3)
        return value.reshape(value.shape[0], outer * inner * own_rows)

    mlp_planes = weight_mlp.transpose(1, 0, 2)
    gate_up_chunks, down_chunks = mlp_chunks(mlp_planes, gain_two, side, members, piece)

    def to_members(chunks):
        return exchanged(chunks, ("k", "c")).reshape(members * own_rows, chunks.shape[2])

    incoming = cotangent.reshape(tok_rows, width)
    def own_half(weight):
        half = weight.shape[1] // sides
        return lax.dynamic_slice_in_dim(weight, side * half, half, 1)

    def gathered_group(weight):
        half = weight.shape[1]
        weight = lax.all_gather(weight, GROUP, axis=0, tiled=True)
        return weight.reshape(sides, owner_count * own_rows, half)

    gate_up_blocks = [to_members(gate_up_chunks)]
    qkv_rows = lax.all_gather(own_half(low(qkv_low * gain_one)), PLANES, axis=0, tiled=True)
    qkv_halves = gathered_group(after(qkv_rows, gate_up_blocks[0]))
    gate_up_blocks.append(next_plane(after(gate_up_blocks[0], qkv_rows)))
    down_blocks = [to_members(down_chunks)]
    down_blocks.append(next_plane(down_blocks[0]))
    incoming_columns = doubled(incoming, "k", 1, 0)

    tokens = wide(hidden_in.reshape(tok_rows, width))
    lengths_row = lax.dynamic_index_in_dim(lengths, packed_index, 0, keepdims=False)
    row_numbers = jnp.arange(tok_rows, dtype=jnp.int32)
    query_docs, query_places = doc_places(
        lengths_row, (place * sides + side) * tok_rows + row_numbers
    )
    blocks = jnp.arange(blocks_in_side, dtype=jnp.int32)[None, :] * sides
    blocks = blocks + jnp.arange(sides, dtype=jnp.int32)[:, None]
    key_offsets = (blocks[:, :, None] * tok_rows + row_numbers).reshape(-1)
    key_docs, key_places = doc_places(lengths_row, key_offsets)
    distance = query_places[:, None] - key_places[None, :]
    allowed = (query_docs[:, None] == key_docs[None, :]) & (distance >= 0) & (distance < WINDOW)
    cosine, sine = rope_angles(query_places, HEAD_DIM)
    query_scale = HEAD_DIM ** (-0.5)

    factor_one = lax.rsqrt(jnp.mean(tokens * tokens, axis=-1, keepdims=True) + NORM_EPS)
    normed_one = low(tokens * factor_one)
    normed_one = after(normed_one, incoming_columns, gate_up_blocks[1], down_blocks[1])
    rows = regrouped(normed_one, planes, members)
    projected = jnp.concatenate([dot(rows, half, (1, 0)) for half in qkv_halves], axis=1)
    out_rows = own_half(low(after(weight_out, projected)))
    out_halves = gathered_group(lax.all_gather(out_rows, PLANES, axis=0, tiled=True))
    key_pre = projected[:, width : width + HEAD_DIM]
    value_low = low(projected[:, width + HEAD_DIM :])
    key_low = low(rotate(key_pre, cosine, sine))
    window_kv = spread_ring(jnp.concatenate([key_low, value_low], axis=1))
    window_kv = doubled(window_kv, "c", 1, 1)
    window_kv = window_kv.reshape(SEQ_LEN, 2 * HEAD_DIM)
    gate_up_blocks.append(next_plane(after(gate_up_blocks[1], projected)))
    for _ in range(planes - 3):
        gate_up_blocks.append(next_plane(gate_up_blocks[-1]))
    down_blocks.append(next_plane(after(down_blocks[1], projected)))
    for _ in range(planes - 3):
        down_blocks.append(next_plane(down_blocks[-1]))
    gate_up_own = joined_planes(gate_up_blocks)
    down_own = joined_planes(down_blocks)
    incoming_sides = doubled(after(incoming_columns, window_kv), "seq", 1, 0)
    query_pre = projected[:, :width].reshape(tok_rows, head_count, HEAD_DIM)
    queries = low(rotate(query_pre, cosine[:, None, :], sine[:, None, :]) * query_scale)
    queries = after(queries.reshape(tok_rows, width), gate_up_blocks[2], down_blocks[2])
    incoming_all = doubled(incoming_sides, "c", 1, incoming_sides.ndim - 2)
    incoming_all = incoming_all.reshape(sides * members * tok_rows, width)
    keys_win = window_kv[:, :HEAD_DIM]
    values_win = window_kv[:, HEAD_DIM:]
    bias = jnp.where(allowed.T, 0.0, MASKED_SCORE)
    bias = jnp.concatenate([bias, bias], axis=1)
    attn_low, log_total = attend(queries, keys_win, values_win, bias)
    attn_low = after(attn_low, incoming_sides)
    rows = regrouped(attn_low, planes, members)
    branch = [dot(rows, half, (1, 0)) for half in out_halves]
    middle = tokens + jnp.concatenate(branch, axis=1)

    factor_two = lax.rsqrt(jnp.mean(middle * middle, axis=-1, keepdims=True) + NORM_EPS)
    normed_two = low(middle * factor_two)
    normed_two_all = lax.all_gather(normed_two, GROUP, axis=0, tiled=True)
    grad_act = low(dot(incoming_all, down_own, (1, 0)))
    gate_up = dot(after(normed_two_all, down_own, incoming_all), gate_up_own, (1, 0))
    activated, glu_back = jax.vjp(glu_values, gate_up[:, :piece], gate_up[:, piece:])
    activated_low = low(activated)
    def to_owners(term):
        return lax.psum_scatter(term, PLANES, scatter_dimension=0, tiled=True)

    down_term = low(dot(incoming_all, activated_low, (0, 0)))
    down_rows = to_owners(down_term)
    attn_all = lax.all_gather(after(attn_low, down_term), GROUP, axis=0, tiled=True)
    grad_gate, grad_up = glu_back(wide(after(grad_act, down_term)))
    grad_gate_up = low(jnp.concatenate([grad_gate, grad_up], axis=1))

    def in_plane(term, *others):
        term = term.reshape(members, own_rows, term.shape[1])
        ours = exchanged(after(term, *others), ("k", "c"))
        return (ours, swapped(ours, "seq"))

    def group_terms(hidden, weight):
        by_core = hidden.reshape(sides * columns, 2, tok_rows, hidden.shape[1])

        def one_core(which):
            rows = lax.dynamic_index_in_dim(by_core, which, 1, keepdims=False)
            return dot(rows.reshape(-1, hidden.shape[1]), weight, (1, 1))

        given = swapped(low(one_core(1 - core)), "c")
        return low(one_core(core) + wide(given)).reshape(sides * columns, tok_rows, width)

    terms = group_terms(grad_gate_up, gate_up_own)
    place = lax.axis_index(CHIPS)
    grad_normed_two = wide(lax.dynamic_index_in_dim(terms, place, 0, keepdims=False))
    arrived = []
    for step in range(1, sides * columns):
        term = lax.dynamic_index_in_dim(terms, place ^ step, 0, keepdims=False)
        if step == sides * columns - 1:
            term = after(term, *arrived)
        arrived.append(lax.ppermute(term, CHIPS, traded(CHIPS, step)))
    late = after(grad_gate_up, *arrived[:-1])
    gate_term = low(dot(normed_two_all, late[:, :piece], (0, 0)))
    up_term = low(dot(normed_two_all, late[:, piece:], (0, 0)))
    grad_normed_two = grad_normed_two + sum(wide(term) for term in arrived)
    grad_normed_two = after(grad_normed_two, gate_term, up_term)

    gate_rows = to_owners(gate_term)
    up_rows = to_owners(up_term)
    grad_middle = (
        wide(incoming)
        + factor_two * grad_normed_two
        - middle * factor_two**3 * jnp.mean(grad_normed_two * middle, axis=-1, keepdims=True)
    )

    shares = sides * members

    def by_column(*terms):
        terms = [term.reshape(tok_rows, shares, term.shape[1] // shares) for term in terms]
        terms = jnp.concatenate(terms, axis=2).transpose(1, 0, 2)
        return exchanged(terms, GROUP)

    def to_rows(total):
        total = exchanged(total.reshape(owner_count, own_rows, -1), OWNERS)
        return low(jnp.sum(wide(total.reshape(planes, members, own_rows, -1)), axis=0))

    def joined(total):
        return wide(total.transpose(1, 0, 2).reshape(own_rows, -1))

    grad_branch_low = low(grad_middle)
    half = width // sides
    grad_mixed = sum(
        dot(grad_branch_low[:, index * half : (index + 1) * half], out_halves[index], (1, 1))
        for index in range(sides)
    )
    grad_mixed_low = regrouped(low(grad_mixed), members, planes)
    delta = (wide(grad_mixed_low) * wide(attn_low)).reshape(tok_rows, head_count, HEAD_DIM)
    delta = jnp.sum(delta, axis=-1).T.reshape(log_total.shape)
    grad_query, grad_window = attend_back(
        queries, grad_mixed_low, keys_win, values_win, bias, log_total, delta
    )
    normed_one_columns = doubled(after(normed_one, grad_normed_two), "k", 1, 0)
    normed_one_sides = doubled(normed_one_columns, "seq", 1, 0)
    down_pieces = in_plane(down_rows)
    grad_window = after(low(grad_window), normed_one_sides, down_pieces[0])
    branch = low(dot(after(activated_low, grad_window), down_own, (1, 1)))
    normed_one_others = swapped(normed_one_sides, "c")
    grad_window = half_sum(grad_window.reshape(-1, 2, tok_rows, 2 * HEAD_DIM), "c", 1)
    grad_window = grad_window.reshape(sides, -1, columns, tok_rows, 2 * HEAD_DIM)
    grad_window = grad_window.swapaxes(1, 2).reshape(sides * columns, -1, tok_rows, 2 * HEAD_DIM)
    grad_local = wide(half_sum(low(ring_sum(grad_window)), "h", 0))

    mlp_states = (mlp_planes, first_mlp.transpose(1, 0, 2), second_mlp.transpose(1, 0, 2))
    rate_main = 2.0 * D ** (-0.5)

    def mlp_updated(part, pieces, outs):
        *outs, gain_dot = mlp_adam(part, side, pieces, mlp_states, gain_two, rate_main, outs)
        return outs, gain_dot

    mlp_outs, down_dot = mlp_updated(2, down_pieces, ())
    grad_local = after(grad_local, down_dot)
    grad_query = grad_query.reshape(tok_rows, head_count, HEAD_DIM)
    grad_query_pre = rotate(
        grad_query * query_scale, cosine[:, None, :], -sine[:, None, :]
    ).reshape(tok_rows, width)
    grad_key_pre = rotate(grad_local[:, :HEAD_DIM], cosine, -sine)
    grad_proj = low(
        jnp.concatenate([grad_query_pre, grad_key_pre, grad_local[:, HEAD_DIM:]], axis=1)
    )

    all_columns = by_column(after(grad_proj, normed_one_others), grad_branch_low)
    qkv_share = grad_proj.shape[1] // shares
    by_core = all_columns.reshape(sides * columns, 2, tok_rows, -1)[:, :, :, :qkv_share]

    def one_core_total(rows, which):
        columns_there = lax.dynamic_index_in_dim(by_core, which, 1, keepdims=False)
        return dot(rows.reshape(-1, width), columns_there.reshape(-1, qkv_share), (0, 0))

    qkv_total = one_core_total(normed_one_sides, core)
    qkv_total = low(qkv_total + one_core_total(normed_one_others, 1 - core))
    out_columns = all_columns.reshape(shares * tok_rows, -1)[:, qkv_share:]
    out_total = low(dot(attn_all, out_columns, (0, 0)))
    gate_pieces = in_plane(gate_rows, all_columns)
    up_pieces = in_plane(up_rows, gate_pieces[0])
    total = jnp.concatenate([qkv_total, out_total], axis=1)
    total = to_rows(after(total, up_pieces[0]))
    branch = lax.psum_scatter(
        after(branch, all_columns), GROUP, scatter_dimension=0, tiled=True
    )
    mlp_outs, gate_dot = mlp_updated(0, gate_pieces, mlp_outs)
    (grad_mlp, second_new_mlp, new_mlp), up_dot = mlp_updated(1, up_pieces, mlp_outs)
    grad_gain_two = gate_dot + up_dot
    total = doubled(total, "seq", 1, 0).reshape(shares, own_rows, -1)
    grad_qkv = joined(total[:, :, :qkv_share])
    grad_out = joined(total[:, :, qkv_share:])
    hidden_out = low(middle + wide(branch)).reshape(1, 1, tok_rows, width)

    half = grad_proj.shape[1] // sides
    grad_normed = sum(
        dot(grad_proj[:, index * half : (index + 1) * half], qkv_halves[index], (1, 1))
        for index in range(sides)
    )
    grad_normed = regrouped(grad_normed, members, planes)
    hidden_grad = (
        grad_middle
        + factor_one * grad_normed
        - tokens * factor_one**3 * jnp.mean(grad_normed * tokens, axis=-1, keepdims=True)
    ).reshape(1, 1, tok_rows, width)

    rate_out = 2.0 * max(1, 6 * D // WINDOW) ** (-0.5)
    rate_gains = 0.4
    grad_gain_one = jnp.sum(qkv_low * grad_qkv, axis=1, keepdims=True)
    grad_qkv = grad_qkv * gain_one
    second_new_qkv, new_qkv = adam_step(weight_qkv, first_qkv, second_qkv, grad_qkv, rate_main)
    second_new_out, new_out = adam_step(weight_out, first_out, second_out, grad_out, rate_out)
    grad_gains = jnp.concatenate([grad_gain_one, grad_gain_two], axis=1)
    second_new_gains, new_gains = adam_step(
        norm_gains, first_gains, second_gains, grad_gains, rate_gains
    )
    return (
        hidden_out,
        hidden_grad,
        grad_qkv,
        second_new_qkv,
        new_qkv,
        grad_out,
        second_new_out,
        new_out,
        grad_mlp.transpose(1, 0, 2),
        second_new_mlp.transpose(1, 0, 2),
        new_mlp.transpose(1, 0, 2),
        grad_gains,
        second_new_gains,
        new_gains,
    )


def solution(mesh):
    seq_count, owner_count = mesh.devices.shape

    def whole(*arguments):
        members = SEQ_LEN // (seq_count * arguments[0].shape[2])
        shape = (seq_count, owner_count // members, members // 4, 2, 2)
        split = Mesh(mesh.devices.reshape(shape), ("seq", "g", "h", "k", "c"))
        acts = P(OWNERS, "seq", None, None)
        flat = P(OWNERS, None)
        planes = P(OWNERS, None, None)
        return jax.shard_map(
            on_device,
            mesh=split,
            in_specs=(acts, acts, P()) + (flat,) * 6 + (planes,) * 3 + (flat,) * 3,
            out_specs=(acts, acts) + (flat,) * 6 + (planes,) * 3 + (flat,) * 3,
            check_vma=False,
        )(*arguments)

    return whole
```

```python
import math

import jax
import jax.numpy as jnp
from jax import lax
from jax.experimental import pallas as pl
from jax.experimental.pallas import tpu as pltpu
from jax.sharding import Mesh, PartitionSpec as P

D = 2560
HEAD_DIM = 256
WINDOW = 2048
STEP = 10
SEQ_LEN = 3072

NORM_EPS = 1e-06
BETA_ONE = 0.9
BETA_TWO = 0.95
ADAM_EPS = 1e-08
DECAY_RATE = 0.1
MASKED_SCORE = -1e30

LANES = 512
KEY_BLOCK = 768
PLANES = ("g", "h")
OWNERS = ("g", "h", "k", "c")
CHIPS = ("seq", "k")
GROUP = ("seq", "k", "c")
RING = ("seq", "h", "k")


def rotate(values, cosine, sine):
    half_dim = values.shape[-1] // 2
    first_half = values[..., :half_dim]
    second_half = values[..., half_dim:]
    return jnp.concatenate(
        [first_half * cosine - second_half * sine, second_half * cosine + first_half * sine],
        axis=-1,
    )


def doc_places(lengths_row, offsets):
    doc_ends = jnp.cumsum(lengths_row)
    passed = (doc_ends[None, :] <= offsets[:, None]).astype(jnp.int32)
    document = jnp.sum(passed, axis=1)
    starts = jnp.sum(passed * lengths_row[None, :], axis=1)
    return (document, offsets - starts)


def rope_angles(places, head_dim):
    freq_index = jnp.arange(head_dim // 2, dtype=jnp.float32)
    inverse = jnp.exp(freq_index * (-2.0 * math.log(10000.0) / head_dim))
    angles = places.astype(jnp.float32)[:, None] * inverse[None, :]
    return (jnp.cos(angles), jnp.sin(angles))


def adam_step(weight, first, second, grad, rate):
    first_new = BETA_ONE * first + (1.0 - BETA_ONE) * grad
    second_new = BETA_TWO * second + (1.0 - BETA_TWO) * grad * grad
    first_hat = first_new / (1.0 - BETA_ONE**STEP)
    second_hat = second_new / (1.0 - BETA_TWO**STEP)
    update = first_hat / (jnp.sqrt(second_hat) + ADAM_EPS)
    return (second_new, weight - rate * (update + DECAY_RATE * weight))


def glu_values(gate_in, up_in):
    return jax.nn.gelu(gate_in, approximate=True) * up_in


def low(value):
    return value.astype(jnp.bfloat16)


def wide(value):
    return value.astype(jnp.float32)


def dot(left, right, contract):
    return lax.dot_general(
        left, right, ((contract[:1], contract[1:]), ((), ())), preferred_element_type=jnp.float32
    )


def traded(axes, step):
    count = math.prod(lax.axis_size(axis) for axis in axes)
    return [(source, source ^ step) for source in range(count)]


def swapped(value, axis):
    return lax.ppermute(value, axis, [(0, 1), (1, 0)])


def after(value, *others):
    return lax.optimization_barrier((value,) + others)[0]


def doubled(value, axis, step, place):
    other = lax.ppermute(value, axis, traded((axis,), step))
    first = (lax.axis_index(axis) & step) == 0
    return jnp.stack([jnp.where(first, value, other), jnp.where(first, other, value)], axis=place)


def next_plane(block):
    count = math.prod(lax.axis_size(axis) for axis in PLANES)
    return lax.ppermute(block, PLANES, [(one, (one + 1) % count) for one in range(count)])


def joined_planes(blocks):
    count, (rows, width) = len(blocks), blocks[0].shape
    whole = jnp.zeros((count * rows, width), blocks[0].dtype)
    for step, block in enumerate(blocks):
        start = lax.rem(lax.axis_index(PLANES) + (count - step), count) * rows
        column = 0
        for part in block if isinstance(block, list) else [block]:
            whole = lax.dynamic_update_slice(whole, part, (start, column))
            column += part.shape[1]
    return whole


def spread_ring(value):
    chips = math.prod(lax.axis_size(axis) for axis in RING)
    place = lax.axis_index(RING)
    whole = jnp.zeros((chips,) + value.shape, value.dtype)
    for step in range(chips):
        arrived = lax.ppermute(value, RING, traded(RING, step)) if step else value
        whole = lax.dynamic_update_index_in_dim(whole, arrived, place ^ step, 0)
    return whole


def ring_sum(terms):
    chips = terms.shape[0]
    place = lax.axis_index(CHIPS)
    total = 0.0
    for step in range(chips):
        term = lax.dynamic_index_in_dim(terms, place ^ step, 0, keepdims=False)
        if step:
            term = lax.ppermute(term, CHIPS, traded(CHIPS, step))
        total = total + wide(term)
    return total


def exchanged(value, axes):
    return lax.all_to_all(value, axes, split_axis=0, concat_axis=0, tiled=True)


def half_sum(terms, axis, place):
    here = lax.axis_index(axis)
    kept = lax.dynamic_index_in_dim(terms, here, place, keepdims=False)
    given = lax.dynamic_index_in_dim(terms, 1 - here, place, keepdims=False)
    return low(wide(kept) + wide(swapped(given, axis)))


def mlp_chunks_kernel(slices, side_ref, weight_ref, gain_ref, gate_up_ref, down_ref):
    per_piece = pl.num_programs(1)
    index = side_ref[0] * pl.num_programs(0) + pl.program_id(0)
    index = index * per_piece + pl.program_id(1)
    width = weight_ref.shape[2]
    lane = pl.program_id(1) * width
    gain = gain_ref[...]
    for part in range(3):
        weight = wide(low(weight_ref[part]))
        if part < 2:
            weight = weight * gain
        weight = low(jnp.where(index < slices, weight, 0.0))
        if part < 2:
            place = pl.multiple_of(part * per_piece * width + lane, width)
            gate_up_ref[0, :, pl.ds(place, width)] = weight
        else:
            down_ref[0, :, pl.ds(pl.multiple_of(lane, width), width)] = weight


def mlp_chunks(weight, gain, side, members, piece):
    parts, rows, ff_width = weight.shape
    slices = ff_width // LANES
    per_piece = piece // LANES

    def weight_block(m, b, side_ref):
        return (0, 0, jnp.minimum((side_ref[0] * members + m) * per_piece + b, slices - 1))

    def out_block(m, b, side_ref):
        return (m, 0, 0)

    return pl.pallas_call(
        lambda *refs: mlp_chunks_kernel(slices, *refs),
        grid_spec=pltpu.PrefetchScalarGridSpec(
            num_scalar_prefetch=1,
            grid=(members, per_piece),
            in_specs=[
                pl.BlockSpec((parts, rows, LANES), weight_block),
                pl.BlockSpec((rows, 1), lambda m, b, side_ref: (0, 0)),
            ],
            out_specs=[
                pl.BlockSpec((1, rows, 2 * piece), out_block),
                pl.BlockSpec((1, rows, piece), out_block),
            ],
        ),
        out_shape=[
            jax.ShapeDtypeStruct((members, rows, 2 * piece), jnp.bfloat16),
            jax.ShapeDtypeStruct((members, rows, piece), jnp.bfloat16),
        ],
        compiler_params=pltpu.CompilerParams(vmem_limit_bytes=48 * 1024 * 1024),
        cost_estimate=pl.CostEstimate(
            flops=weight.size, bytes_accessed=3 * weight.size, transcendentals=0
        ),
        name="mlp_chunks",
    )(jnp.full((1,), side, jnp.int32), weight, gain)


def mlp_adam_kernel(rate, per_side, scaled, side_ref, ours_ref, theirs_ref, weight_ref, first_ref,
                    second_ref, gain_ref, *refs):
    grad_out, second_out, weight_out, dot_out = refs[-4:]
    block = pl.program_id(0)
    ours = block // per_side == side_ref[0]
    grad = wide(jnp.where(ours, ours_ref[0], theirs_ref[0]))
    weight = weight_ref[0]
    dot_part = jnp.sum(wide(low(weight)) * grad, axis=1, keepdims=True)
    dot_out[...] = jnp.where(block == 0, dot_part, dot_out[...] + dot_part)
    if scaled:
        grad = grad * gain_ref[...]
    grad_out[0] = grad
    second_out[0], weight_out[0] = adam_step(weight, first_ref[0], second_ref[0], grad, rate)


def mlp_adam(part, side, pieces, states, gain, rate, outs):
    _, rows, ff_width = states[0].shape
    members, _, piece = pieces[0].shape
    per_piece = piece // LANES
    per_side = members * per_piece

    def grad_block(own):
        def place(b, side_ref):
            used = (b // per_side == side_ref[0]) == own
            inner = jnp.where(used, b % per_side, 0)
            return (inner // per_piece, 0, inner % per_piece)

        return pl.BlockSpec((1, rows, LANES), place)

    state = pl.BlockSpec((1, rows, LANES), lambda b, side_ref: (part, 0, b))
    gains = pl.BlockSpec((rows, 1), lambda b, side_ref: (0, 0))
    size = rows * ff_width
    return pl.pallas_call(
        lambda *refs: mlp_adam_kernel(rate, per_side, part < 2, *refs),
        grid_spec=pltpu.PrefetchScalarGridSpec(
            num_scalar_prefetch=1,
            grid=(ff_width // LANES,),
            in_specs=[grad_block(True), grad_block(False), state, state, state, gains]
            + [pl.BlockSpec(memory_space=pl.ANY)] * len(outs),
            out_specs=[state, state, state, gains],
        ),
        out_shape=[jax.ShapeDtypeStruct(states[0].shape, jnp.float32)] * 3
        + [jax.ShapeDtypeStruct((rows, 1), jnp.float32)],
        input_output_aliases={7 + index: index for index in range(len(outs))},
        compiler_params=pltpu.CompilerParams(vmem_limit_bytes=48 * 1024 * 1024),
        cost_estimate=pl.CostEstimate(
            flops=20 * size, bytes_accessed=26 * size, transcendentals=size
        ),
        name="mlp_adam",
    )(jnp.full((1,), side, jnp.int32), *pieces, *states, gain, *outs)


def stacked_heads(ref):
    return jnp.concatenate([ref[:, :HEAD_DIM], ref[:, HEAD_DIM:]], axis=0)


def attend_kernel(query_ref, key_ref, value_t_ref, bias_ref, out_ref, lse_ref, score_ref):
    rows = query_ref.shape[0]
    queries = stacked_heads(query_ref)
    blocks = key_ref.shape[0] // KEY_BLOCK

    def first(block, top):
        part = pl.ds(pl.multiple_of(block * KEY_BLOCK, KEY_BLOCK), KEY_BLOCK)
        scores = dot(key_ref[part, :], queries, (1, 1)) + bias_ref[part, :]
        score_ref[part, :] = scores
        return jnp.maximum(top, jnp.max(scores, axis=0, keepdims=True))

    top = jnp.full((1, 2 * rows), -jnp.inf, jnp.float32)
    top = lax.fori_loop(0, blocks, first, top, unroll=2)

    def second(block, carry):
        total, mixed = carry
        part = pl.ds(pl.multiple_of(block * KEY_BLOCK, KEY_BLOCK), KEY_BLOCK)
        exps = jnp.exp(score_ref[part, :] - top)
        total = total + jnp.sum(exps, axis=0, keepdims=True)
        return total, mixed + dot(value_t_ref[:, part], low(exps), (1, 0))

    total, mixed = lax.fori_loop(
        0,
        blocks,
        second,
        (jnp.zeros((1, 2 * rows), jnp.float32), jnp.zeros((HEAD_DIM, 2 * rows), jnp.float32)),
        unroll=2,
    )
    mixed = low((mixed / total).T)
    out_ref[:, :HEAD_DIM] = mixed[:rows]
    out_ref[:, HEAD_DIM:] = mixed[rows:]
    lse_ref[0] = top + jnp.log(total)


def attend(queries, keys, values, bias):
    rows, width = queries.shape
    pairs = width // (2 * HEAD_DIM)
    count = keys.shape[0]

    def whole(shape):
        return pl.BlockSpec(shape, lambda p: (0,) * len(shape))

    pair = pl.BlockSpec((rows, 2 * HEAD_DIM), lambda p: (0, p))
    return pl.pallas_call(
        attend_kernel,
        grid=(pairs,),
        in_specs=[pair, whole(keys.shape), whole((HEAD_DIM, count)), whole(bias.shape)],
        out_specs=[pair, pl.BlockSpec((1, 1, 2 * rows), lambda p: (p, 0, 0))],
        out_shape=[
            jax.ShapeDtypeStruct((rows, width), jnp.bfloat16),
            jax.ShapeDtypeStruct((pairs, 1, 2 * rows), jnp.float32),
        ],
        scratch_shapes=[pltpu.VMEM((count, 2 * rows), jnp.float32)],
        compiler_params=pltpu.CompilerParams(vmem_limit_bytes=48 * 1024 * 1024),
        cost_estimate=pl.CostEstimate(
            flops=4 * rows * width * count,
            bytes_accessed=8 * rows * width + 12 * bias.size,
            transcendentals=pairs * bias.size,
        ),
        name="attend",
    )(queries, keys, values.T, bias)


def attend_back_kernel(query_ref, grad_ref, key_ref, key_t_ref, value_ref, bias_ref, lse_ref,
                       delta_ref, grad_query_ref, grad_window_ref):
    rows = query_ref.shape[0]
    queries = stacked_heads(query_ref)
    grads = stacked_heads(grad_ref)
    blocks = key_ref.shape[0] // KEY_BLOCK

    @pl.when(pl.program_id(0) == 0)
    def _():
        grad_window_ref[...] = jnp.zeros_like(grad_window_ref)

    lse = lse_ref[0]
    delta = delta_ref[0]

    def body(block, grad_query):
        part = pl.ds(pl.multiple_of(block * KEY_BLOCK, KEY_BLOCK), KEY_BLOCK)
        probs = jnp.exp(dot(key_ref[part, :], queries, (1, 1)) + bias_ref[part, :] - lse)
        grad_probs = dot(value_ref[part, :], grads, (1, 1))
        grad_scores = low(probs * (grad_probs - delta))
        grad_window_ref[part, :HEAD_DIM] += dot(grad_scores, queries, (1, 0))
        grad_window_ref[part, HEAD_DIM:] += dot(low(probs), grads, (1, 0))
        return grad_query + dot(key_t_ref[:, part], grad_scores, (1, 0))

    grad_query = jnp.zeros((HEAD_DIM, 2 * rows), jnp.float32)
    grad_query = lax.fori_loop(0, blocks, body, grad_query, unroll=2).T
    grad_query_ref[:, :HEAD_DIM] = grad_query[:rows]
    grad_query_ref[:, HEAD_DIM:] = grad_query[rows:]


def attend_back(queries, grads, keys, values, bias, lse, delta):
    rows, width = queries.shape
    pairs = width // (2 * HEAD_DIM)
    count = keys.shape[0]

    def whole(shape):
        return pl.BlockSpec(shape, lambda p: (0,) * len(shape))

    pair = pl.BlockSpec((rows, 2 * HEAD_DIM), lambda p: (0, p))
    line = pl.BlockSpec((1, 1, 2 * rows), lambda p: (p, 0, 0))
    return pl.pallas_call(
        attend_back_kernel,
        grid=(pairs,),
        in_specs=[
            pair,
            pair,
            whole(keys.shape),
            whole((HEAD_DIM, count)),
            whole(values.shape),
            whole(bias.shape),
            line,
            line,
        ],
        out_specs=[pair, whole((count, 2 * HEAD_DIM))],
        out_shape=[
            jax.ShapeDtypeStruct((rows, width), jnp.float32),
            jax.ShapeDtypeStruct((count, 2 * HEAD_DIM), jnp.float32),
        ],
        compiler_params=pltpu.CompilerParams(vmem_limit_bytes=48 * 1024 * 1024),
        cost_estimate=pl.CostEstimate(
            flops=10 * rows * width * count,
            bytes_accessed=8 * rows * width + 16 * bias.size,
            transcendentals=pairs * bias.size,
        ),
        name="attend_back",
    )(queries, grads, keys, keys.T, values, bias, lse, delta)


def on_device(
    hidden_in,
    cotangent,
    lengths,
    weight_qkv,
    first_qkv,
    second_qkv,
    weight_out,
    first_out,
    second_out,
    weight_mlp,
    first_mlp,
    second_mlp,
    norm_gains,
    first_gains,
    second_gains,
):
    tok_rows = hidden_in.shape[2]
    width = hidden_in.shape[3]
    head_count = width // HEAD_DIM
    sides = lax.axis_size("seq")
    columns = lax.axis_size("k")
    members = columns * lax.axis_size("c")
    planes = lax.axis_size("g") * lax.axis_size("h")
    owner_count = planes * members
    blocks_in_side = lax.axis_size("h") * members
    side = lax.axis_index("seq")
    core = lax.axis_index("c")
    packed_index = lax.axis_index("g")
    place = lax.axis_index(("h", "k", "c"))
    own_rows = weight_mlp.shape[0]
    ff_width = weight_mlp.shape[2]
    piece = -(-ff_width // (sides * members * LANES)) * LANES

    gains_low = wide(low(norm_gains))
    gain_one = gains_low[:, :1]
    gain_two = gains_low[:, 1:]
    qkv_low = wide(low(weight_qkv))
    def regrouped(value, outer, inner):
        value = value.reshape(value.shape[0], outer, inner, own_rows).transpose(0, 2, 1, 3)
        return value.reshape(value.shape[0], outer * inner * own_rows)

    mlp_planes = weight_mlp.transpose(1, 0, 2)
    gate_up_chunks, down_chunks = mlp_chunks(mlp_planes, gain_two, side, members, piece)

    def to_members(chunks):
        return exchanged(chunks, ("k", "c")).reshape(members * own_rows, chunks.shape[2])

    incoming = cotangent.reshape(tok_rows, width)
    def own_half(weight):
        half = weight.shape[1] // sides
        return lax.dynamic_slice_in_dim(weight, side * half, half, 1)

    def gathered_group(weight):
        half = weight.shape[1]
        weight = lax.all_gather(weight, GROUP, axis=0, tiled=True)
        return weight.reshape(sides, owner_count * own_rows, half)

    gate_up_blocks = [to_members(gate_up_chunks)]
    qkv_rows = lax.all_gather(own_half(low(qkv_low * gain_one)), PLANES, axis=0, tiled=True)
    qkv_halves = gathered_group(after(qkv_rows, gate_up_blocks[0]))
    gate_up_blocks.append(next_plane(after(gate_up_blocks[0], qkv_rows)))
    down_blocks = [to_members(down_chunks)]
    down_blocks.append(next_plane(down_blocks[0]))
    incoming_columns = doubled(incoming, "k", 1, 0)

    tokens = wide(hidden_in.reshape(tok_rows, width))
    lengths_row = lax.dynamic_index_in_dim(lengths, packed_index, 0, keepdims=False)
    row_numbers = jnp.arange(tok_rows, dtype=jnp.int32)
    query_docs, query_places = doc_places(
        lengths_row, (place * sides + side) * tok_rows + row_numbers
    )
    blocks = jnp.arange(blocks_in_side, dtype=jnp.int32)[None, :] * sides
    blocks = blocks + jnp.arange(sides, dtype=jnp.int32)[:, None]
    key_offsets = (blocks[:, :, None] * tok_rows + row_numbers).reshape(-1)
    key_docs, key_places = doc_places(lengths_row, key_offsets)
    distance = query_places[:, None] - key_places[None, :]
    allowed = (query_docs[:, None] == key_docs[None, :]) & (distance >= 0) & (distance < WINDOW)
    cosine, sine = rope_angles(query_places, HEAD_DIM)
    query_scale = HEAD_DIM ** (-0.5)

    factor_one = lax.rsqrt(jnp.mean(tokens * tokens, axis=-1, keepdims=True) + NORM_EPS)
    normed_one = low(tokens * factor_one)
    normed_one = after(normed_one, incoming_columns, gate_up_blocks[1], down_blocks[1])
    rows = regrouped(normed_one, planes, members)
    projected = jnp.concatenate([dot(rows, half, (1, 0)) for half in qkv_halves], axis=1)
    key_pre = projected[:, width : width + HEAD_DIM]
    value_low = low(projected[:, width + HEAD_DIM :])
    key_low = low(rotate(key_pre, cosine, sine))
    window_kv = spread_ring(jnp.concatenate([key_low, value_low], axis=1))
    window_kv = doubled(window_kv, "c", 1, 1)
    window_kv = window_kv.reshape(SEQ_LEN, 2 * HEAD_DIM)
    out_rows = own_half(low(after(weight_out, window_kv)))
    out_halves = gathered_group(lax.all_gather(out_rows, PLANES, axis=0, tiled=True))
    gate_up_blocks.append(next_plane(after(gate_up_blocks[1], projected)))
    for _ in range(planes - 4):
        gate_up_blocks.append(next_plane(gate_up_blocks[-1]))
    last = gate_up_blocks[-1]
    gate_up_blocks.append([next_plane(last[:, :piece]), next_plane(last[:, piece:])])
    down_blocks.append(next_plane(after(down_blocks[1], projected)))
    for _ in range(planes - 3):
        down_blocks.append(next_plane(down_blocks[-1]))
    gate_up_own = joined_planes(gate_up_blocks)
    down_own = joined_planes(down_blocks)
    incoming_sides = doubled(after(incoming_columns, projected), "seq", 1, 0)
    query_pre = projected[:, :width].reshape(tok_rows, head_count, HEAD_DIM)
    queries = low(rotate(query_pre, cosine[:, None, :], sine[:, None, :]) * query_scale)
    incoming_all = doubled(incoming_sides, "c", 1, incoming_sides.ndim - 2)
    incoming_all = incoming_all.reshape(sides * members * tok_rows, width)
    queries = after(queries.reshape(tok_rows, width), gate_up_blocks[2], down_blocks[2], incoming_all)
    keys_win = window_kv[:, :HEAD_DIM]
    values_win = window_kv[:, HEAD_DIM:]
    bias = jnp.where(allowed.T, 0.0, MASKED_SCORE)
    bias = jnp.concatenate([bias, bias], axis=1)
    attn_low, log_total = attend(queries, keys_win, values_win, bias)
    rows = regrouped(attn_low, planes, members)
    branch = [dot(rows, half, (1, 0)) for half in out_halves]
    middle = tokens + jnp.concatenate(branch, axis=1)

    factor_two = lax.rsqrt(jnp.mean(middle * middle, axis=-1, keepdims=True) + NORM_EPS)
    normed_two = after(low(middle * factor_two), gate_up_blocks[-1][0])
    normed_two_all = lax.all_gather(normed_two, GROUP, axis=0, tiled=True)
    grad_act = low(dot(incoming_all, down_own, (1, 0)))
    gate_up = dot(after(normed_two_all, down_own), gate_up_own, (1, 0))
    activated, glu_back = jax.vjp(glu_values, gate_up[:, :piece], gate_up[:, piece:])
    activated_low = low(activated)
    def to_owners(term):
        return lax.psum_scatter(term, PLANES, scatter_dimension=0, tiled=True)

    down_term = low(dot(incoming_all, activated_low, (0, 0)))
    down_rows = to_owners(down_term)
    attn_all = lax.all_gather(after(attn_low, down_term), GROUP, axis=0, tiled=True)
    grad_gate, grad_up = glu_back(wide(after(grad_act, down_term)))
    grad_gate_up = low(jnp.concatenate([grad_gate, grad_up], axis=1))

    def in_plane(term, *others):
        term = term.reshape(members, own_rows, term.shape[1])
        ours = exchanged(after(term, *others), ("k", "c"))
        return (ours, swapped(ours, "seq"))

    def group_terms(hidden, weight):
        by_core = hidden.reshape(sides * columns, 2, tok_rows, hidden.shape[1])

        def one_core(which):
            rows = lax.dynamic_index_in_dim(by_core, which, 1, keepdims=False)
            return dot(rows.reshape(-1, hidden.shape[1]), weight, (1, 1))

        given = swapped(low(one_core(1 - core)), "c")
        return low(one_core(core) + wide(given)).reshape(sides * columns, tok_rows, width)

    terms = group_terms(grad_gate_up, gate_up_own)
    place = lax.axis_index(CHIPS)
    grad_normed_two = wide(lax.dynamic_index_in_dim(terms, place, 0, keepdims=False))
    arrived = []
    for step in range(1, sides * columns):
        term = lax.dynamic_index_in_dim(terms, place ^ step, 0, keepdims=False)
        if step == sides * columns - 1:
            term = after(term, *arrived)
        arrived.append(lax.ppermute(term, CHIPS, traded(CHIPS, step)))
    late = after(grad_gate_up, *arrived[:-1])
    gate_term = low(dot(normed_two_all, late[:, :piece], (0, 0)))
    up_term = low(dot(normed_two_all, late[:, piece:], (0, 0)))
    grad_normed_two = grad_normed_two + sum(wide(term) for term in arrived)
    grad_normed_two = after(grad_normed_two, gate_term, up_term)

    gate_rows = to_owners(gate_term)
    up_rows = to_owners(up_term)
    grad_middle = (
        wide(incoming)
        + factor_two * grad_normed_two
        - middle * factor_two**3 * jnp.mean(grad_normed_two * middle, axis=-1, keepdims=True)
    )

    shares = sides * members

    def by_column(*terms):
        terms = [term.reshape(tok_rows, shares, term.shape[1] // shares) for term in terms]
        terms = jnp.concatenate(terms, axis=2).transpose(1, 0, 2)
        return exchanged(terms, GROUP)

    def to_rows(total):
        total = exchanged(total.reshape(owner_count, own_rows, -1), OWNERS)
        return low(jnp.sum(wide(total.reshape(planes, members, own_rows, -1)), axis=0))

    def joined(total):
        return wide(total.transpose(1, 0, 2).reshape(own_rows, -1))

    grad_branch_low = low(grad_middle)
    half = width // sides
    grad_mixed = sum(
        dot(grad_branch_low[:, index * half : (index + 1) * half], out_halves[index], (1, 1))
        for index in range(sides)
    )
    down_pieces = in_plane(down_rows)
    grad_mixed_low = regrouped(low(grad_mixed), members, planes)
    grad_mixed_low = after(grad_mixed_low, down_pieces[0])
    delta = (wide(grad_mixed_low) * wide(attn_low)).reshape(tok_rows, head_count, HEAD_DIM)
    delta = jnp.sum(delta, axis=-1).T.reshape(log_total.shape)
    grad_query, grad_window = attend_back(
        queries, grad_mixed_low, keys_win, values_win, bias, log_total, delta
    )
    normed_one_columns = doubled(after(normed_one, grad_normed_two), "k", 1, 0)
    normed_one_sides = doubled(normed_one_columns, "seq", 1, 0)
    grad_window = after(low(grad_window), normed_one_sides)
    branch = low(dot(after(activated_low, grad_window), down_own, (1, 1)))
    normed_one_others = swapped(normed_one_sides, "c")
    grad_window = half_sum(grad_window.reshape(-1, 2, tok_rows, 2 * HEAD_DIM), "c", 1)
    grad_window = grad_window.reshape(sides, -1, columns, tok_rows, 2 * HEAD_DIM)
    grad_window = grad_window.swapaxes(1, 2).reshape(sides * columns, -1, tok_rows, 2 * HEAD_DIM)
    grad_local = wide(half_sum(low(ring_sum(grad_window)), "h", 0))

    mlp_states = (mlp_planes, first_mlp.transpose(1, 0, 2), second_mlp.transpose(1, 0, 2))
    rate_main = 2.0 * D ** (-0.5)

    def mlp_updated(part, pieces, outs):
        *outs, gain_dot = mlp_adam(part, side, pieces, mlp_states, gain_two, rate_main, outs)
        return outs, gain_dot

    mlp_outs, down_dot = mlp_updated(2, down_pieces, ())
    grad_local = after(grad_local, down_dot)
    grad_query = grad_query.reshape(tok_rows, head_count, HEAD_DIM)
    grad_query_pre = rotate(
        grad_query * query_scale, cosine[:, None, :], -sine[:, None, :]
    ).reshape(tok_rows, width)
    grad_key_pre = rotate(grad_local[:, :HEAD_DIM], cosine, -sine)
    grad_proj = low(
        jnp.concatenate([grad_query_pre, grad_key_pre, grad_local[:, HEAD_DIM:]], axis=1)
    )

    all_columns = by_column(after(grad_proj, normed_one_others), grad_branch_low)
    qkv_share = grad_proj.shape[1] // shares
    by_core = all_columns.reshape(sides * columns, 2, tok_rows, -1)[:, :, :, :qkv_share]

    def one_core_total(rows, which):
        columns_there = lax.dynamic_index_in_dim(by_core, which, 1, keepdims=False)
        return dot(rows.reshape(-1, width), columns_there.reshape(-1, qkv_share), (0, 0))

    qkv_total = one_core_total(normed_one_sides, core)
    qkv_total = low(qkv_total + one_core_total(normed_one_others, 1 - core))
    out_columns = all_columns.reshape(shares * tok_rows, -1)[:, qkv_share:]
    out_total = low(dot(attn_all, out_columns, (0, 0)))
    gate_pieces = in_plane(gate_rows, all_columns)
    total = jnp.concatenate([qkv_total, out_total], axis=1)
    total = to_rows(after(total, gate_pieces[0]))
    up_pieces = in_plane(up_rows, total)
    branch = lax.psum_scatter(
        after(branch, all_columns), GROUP, scatter_dimension=0, tiled=True
    )
    mlp_outs, gate_dot = mlp_updated(0, gate_pieces, mlp_outs)
    (grad_mlp, second_new_mlp, new_mlp), up_dot = mlp_updated(1, up_pieces, mlp_outs)
    grad_gain_two = gate_dot + up_dot
    total = doubled(total, "seq", 1, 0).reshape(shares, own_rows, -1)
    grad_qkv = joined(total[:, :, :qkv_share])
    grad_out = joined(total[:, :, qkv_share:])
    hidden_out = low(middle + wide(branch)).reshape(1, 1, tok_rows, width)

    half = grad_proj.shape[1] // sides
    grad_normed = sum(
        dot(grad_proj[:, index * half : (index + 1) * half], qkv_halves[index], (1, 1))
        for index in range(sides)
    )
    grad_normed = regrouped(grad_normed, members, planes)
    hidden_grad = (
        grad_middle
        + factor_one * grad_normed
        - tokens * factor_one**3 * jnp.mean(grad_normed * tokens, axis=-1, keepdims=True)
    ).reshape(1, 1, tok_rows, width)

    rate_out = 2.0 * max(1, 6 * D // WINDOW) ** (-0.5)
    rate_gains = 0.4
    grad_gain_one = jnp.sum(qkv_low * grad_qkv, axis=1, keepdims=True)
    grad_qkv = grad_qkv * gain_one
    second_new_qkv, new_qkv = adam_step(weight_qkv, first_qkv, second_qkv, grad_qkv, rate_main)
    second_new_out, new_out = adam_step(weight_out, first_out, second_out, grad_out, rate_out)
    grad_gains = jnp.concatenate([grad_gain_one, grad_gain_two], axis=1)
    second_new_gains, new_gains = adam_step(
        norm_gains, first_gains, second_gains, grad_gains, rate_gains
    )
    return (
        hidden_out,
        hidden_grad,
        grad_qkv,
        second_new_qkv,
        new_qkv,
        grad_out,
        second_new_out,
        new_out,
        grad_mlp.transpose(1, 0, 2),
        second_new_mlp.transpose(1, 0, 2),
        new_mlp.transpose(1, 0, 2),
        grad_gains,
        second_new_gains,
        new_gains,
    )


def solution(mesh):
    seq_count, owner_count = mesh.devices.shape

    def whole(*arguments):
        members = SEQ_LEN // (seq_count * arguments[0].shape[2])
        shape = (seq_count, owner_count // members, members // 4, 2, 2)
        split = Mesh(mesh.devices.reshape(shape), ("seq", "g", "h", "k", "c"))
        acts = P(OWNERS, "seq", None, None)
        flat = P(OWNERS, None)
        planes = P(OWNERS, None, None)
        return jax.shard_map(
            on_device,
            mesh=split,
            in_specs=(acts, acts, P()) + (flat,) * 6 + (planes,) * 3 + (flat,) * 3,
            out_specs=(acts, acts) + (flat,) * 6 + (planes,) * 3 + (flat,) * 3,
            check_vma=False,
        )(*arguments)

    return whole
```

```python
import math

import jax
import jax.numpy as jnp
from jax import lax
from jax.experimental import pallas as pl
from jax.experimental.pallas import tpu as pltpu
from jax.sharding import Mesh, PartitionSpec as P

D = 2560
HEAD_DIM = 256
WINDOW = 2048
STEP = 10
SEQ_LEN = 3072

NORM_EPS = 1e-06
BETA_ONE = 0.9
BETA_TWO = 0.95
ADAM_EPS = 1e-08
DECAY_RATE = 0.1
MASKED_SCORE = -1e30

LANES = 512
KEY_BLOCK = 768
PLANES = ("g", "h")
OWNERS = ("g", "h", "k", "c")
CHIPS = ("seq", "k")
GROUP = ("seq", "k", "c")
RING = ("seq", "h", "k")


def rotate(values, cosine, sine):
    half_dim = values.shape[-1] // 2
    first_half = values[..., :half_dim]
    second_half = values[..., half_dim:]
    return jnp.concatenate(
        [first_half * cosine - second_half * sine, second_half * cosine + first_half * sine],
        axis=-1,
    )


def doc_places(lengths_row, offsets):
    doc_ends = jnp.cumsum(lengths_row)
    passed = (doc_ends[None, :] <= offsets[:, None]).astype(jnp.int32)
    document = jnp.sum(passed, axis=1)
    starts = jnp.sum(passed * lengths_row[None, :], axis=1)
    return (document, offsets - starts)


def rope_angles(places, head_dim):
    freq_index = jnp.arange(head_dim // 2, dtype=jnp.float32)
    inverse = jnp.exp(freq_index * (-2.0 * math.log(10000.0) / head_dim))
    angles = places.astype(jnp.float32)[:, None] * inverse[None, :]
    return (jnp.cos(angles), jnp.sin(angles))


def adam_step(weight, first, second, grad, rate):
    first_new = BETA_ONE * first + (1.0 - BETA_ONE) * grad
    second_new = BETA_TWO * second + (1.0 - BETA_TWO) * grad * grad
    first_hat = first_new / (1.0 - BETA_ONE**STEP)
    second_hat = second_new / (1.0 - BETA_TWO**STEP)
    update = first_hat / (jnp.sqrt(second_hat) + ADAM_EPS)
    return (second_new, weight - rate * (update + DECAY_RATE * weight))


def glu_values(gate_in, up_in):
    return jax.nn.gelu(gate_in, approximate=True) * up_in


def low(value):
    return value.astype(jnp.bfloat16)


def wide(value):
    return value.astype(jnp.float32)


def dot(left, right, contract):
    return lax.dot_general(
        left, right, ((contract[:1], contract[1:]), ((), ())), preferred_element_type=jnp.float32
    )


def traded(axes, step):
    count = math.prod(lax.axis_size(axis) for axis in axes)
    return [(source, source ^ step) for source in range(count)]


def swapped(value, axis):
    return lax.ppermute(value, axis, [(0, 1), (1, 0)])


def after(value, *others):
    return lax.optimization_barrier((value,) + others)[0]


def doubled(value, axis, step, place):
    other = lax.ppermute(value, axis, traded((axis,), step))
    first = (lax.axis_index(axis) & step) == 0
    return jnp.stack([jnp.where(first, value, other), jnp.where(first, other, value)], axis=place)


def next_plane(block):
    count = math.prod(lax.axis_size(axis) for axis in PLANES)
    return lax.ppermute(block, PLANES, [(one, (one + 1) % count) for one in range(count)])


def joined_planes(blocks):
    count, (rows, width) = len(blocks), blocks[0].shape
    whole = jnp.zeros((count * rows, width), blocks[0].dtype)
    for step, block in enumerate(blocks):
        start = lax.rem(lax.axis_index(PLANES) + (count - step), count) * rows
        column = 0
        for part in block if isinstance(block, list) else [block]:
            whole = lax.dynamic_update_slice(whole, part, (start, column))
            column += part.shape[1]
    return whole


def spread_ring(value):
    chips = math.prod(lax.axis_size(axis) for axis in RING)
    place = lax.axis_index(RING)
    whole = jnp.zeros((chips,) + value.shape, value.dtype)
    for step in range(chips):
        arrived = lax.ppermute(value, RING, traded(RING, step)) if step else value
        whole = lax.dynamic_update_index_in_dim(whole, arrived, place ^ step, 0)
    return whole


def ring_sum(terms):
    chips = terms.shape[0]
    place = lax.axis_index(CHIPS)
    total = 0.0
    for step in range(chips):
        term = lax.dynamic_index_in_dim(terms, place ^ step, 0, keepdims=False)
        if step:
            term = lax.ppermute(term, CHIPS, traded(CHIPS, step))
        total = total + wide(term)
    return total


def exchanged(value, axes):
    return lax.all_to_all(value, axes, split_axis=0, concat_axis=0, tiled=True)


def half_sum(terms, axis, place):
    here = lax.axis_index(axis)
    kept = lax.dynamic_index_in_dim(terms, here, place, keepdims=False)
    given = lax.dynamic_index_in_dim(terms, 1 - here, place, keepdims=False)
    return low(wide(kept) + wide(swapped(given, axis)))


def mlp_chunks_kernel(slices, side_ref, weight_ref, gain_ref, gate_up_ref, down_ref):
    per_piece = pl.num_programs(1)
    index = side_ref[0] * pl.num_programs(0) + pl.program_id(0)
    index = index * per_piece + pl.program_id(1)
    width = weight_ref.shape[2]
    lane = pl.program_id(1) * width
    gain = gain_ref[...]
    for part in range(3):
        weight = wide(low(weight_ref[part]))
        if part < 2:
            weight = weight * gain
        weight = low(jnp.where(index < slices, weight, 0.0))
        if part < 2:
            place = pl.multiple_of(part * per_piece * width + lane, width)
            gate_up_ref[0, :, pl.ds(place, width)] = weight
        else:
            down_ref[0, :, pl.ds(pl.multiple_of(lane, width), width)] = weight


def mlp_chunks(weight, gain, side, members, piece):
    parts, rows, ff_width = weight.shape
    slices = ff_width // LANES
    per_piece = piece // LANES

    def weight_block(m, b, side_ref):
        return (0, 0, jnp.minimum((side_ref[0] * members + m) * per_piece + b, slices - 1))

    def out_block(m, b, side_ref):
        return (m, 0, 0)

    return pl.pallas_call(
        lambda *refs: mlp_chunks_kernel(slices, *refs),
        grid_spec=pltpu.PrefetchScalarGridSpec(
            num_scalar_prefetch=1,
            grid=(members, per_piece),
            in_specs=[
                pl.BlockSpec((parts, rows, LANES), weight_block),
                pl.BlockSpec((rows, 1), lambda m, b, side_ref: (0, 0)),
            ],
            out_specs=[
                pl.BlockSpec((1, rows, 2 * piece), out_block),
                pl.BlockSpec((1, rows, piece), out_block),
            ],
        ),
        out_shape=[
            jax.ShapeDtypeStruct((members, rows, 2 * piece), jnp.bfloat16),
            jax.ShapeDtypeStruct((members, rows, piece), jnp.bfloat16),
        ],
        compiler_params=pltpu.CompilerParams(vmem_limit_bytes=48 * 1024 * 1024),
        cost_estimate=pl.CostEstimate(
            flops=weight.size, bytes_accessed=3 * weight.size, transcendentals=0
        ),
        name="mlp_chunks",
    )(jnp.full((1,), side, jnp.int32), weight, gain)


def mlp_adam_kernel(rate, per_side, scaled, side_ref, ours_ref, theirs_ref, weight_ref, first_ref,
                    second_ref, gain_ref, *refs):
    grad_out, second_out, weight_out, dot_out = refs[-4:]
    block = pl.program_id(0)
    ours = block // per_side == side_ref[0]
    grad = wide(jnp.where(ours, ours_ref[0], theirs_ref[0]))
    weight = weight_ref[0]
    dot_part = jnp.sum(wide(low(weight)) * grad, axis=1, keepdims=True)
    dot_out[...] = jnp.where(block == 0, dot_part, dot_out[...] + dot_part)
    if scaled:
        grad = grad * gain_ref[...]
    grad_out[0] = grad
    second_out[0], weight_out[0] = adam_step(weight, first_ref[0], second_ref[0], grad, rate)


def mlp_adam(part, side, pieces, states, gain, rate, outs):
    _, rows, ff_width = states[0].shape
    members, _, piece = pieces[0].shape
    per_piece = piece // LANES
    per_side = members * per_piece

    def grad_block(own):
        def place(b, side_ref):
            used = (b // per_side == side_ref[0]) == own
            inner = jnp.where(used, b % per_side, 0)
            return (inner // per_piece, 0, inner % per_piece)

        return pl.BlockSpec((1, rows, LANES), place)

    state = pl.BlockSpec((1, rows, LANES), lambda b, side_ref: (part, 0, b))
    gains = pl.BlockSpec((rows, 1), lambda b, side_ref: (0, 0))
    size = rows * ff_width
    return pl.pallas_call(
        lambda *refs: mlp_adam_kernel(rate, per_side, part < 2, *refs),
        grid_spec=pltpu.PrefetchScalarGridSpec(
            num_scalar_prefetch=1,
            grid=(ff_width // LANES,),
            in_specs=[grad_block(True), grad_block(False), state, state, state, gains]
            + [pl.BlockSpec(memory_space=pl.ANY)] * len(outs),
            out_specs=[state, state, state, gains],
        ),
        out_shape=[jax.ShapeDtypeStruct(states[0].shape, jnp.float32)] * 3
        + [jax.ShapeDtypeStruct((rows, 1), jnp.float32)],
        input_output_aliases={7 + index: index for index in range(len(outs))},
        compiler_params=pltpu.CompilerParams(vmem_limit_bytes=48 * 1024 * 1024),
        cost_estimate=pl.CostEstimate(
            flops=20 * size, bytes_accessed=26 * size, transcendentals=size
        ),
        name="mlp_adam",
    )(jnp.full((1,), side, jnp.int32), *pieces, *states, gain, *outs)


def stacked_heads(ref):
    return jnp.concatenate([ref[:, :HEAD_DIM], ref[:, HEAD_DIM:]], axis=0)


def attend_kernel(query_ref, key_ref, value_t_ref, bias_ref, out_ref, lse_ref, score_ref):
    rows = query_ref.shape[0]
    queries = stacked_heads(query_ref)
    blocks = key_ref.shape[0] // KEY_BLOCK

    def first(block, top):
        part = pl.ds(pl.multiple_of(block * KEY_BLOCK, KEY_BLOCK), KEY_BLOCK)
        scores = dot(key_ref[part, :], queries, (1, 1)) + bias_ref[part, :]
        score_ref[part, :] = scores
        return jnp.maximum(top, jnp.max(scores, axis=0, keepdims=True))

    top = jnp.full((1, 2 * rows), -jnp.inf, jnp.float32)
    top = lax.fori_loop(0, blocks, first, top, unroll=2)

    def second(block, carry):
        total, mixed = carry
        part = pl.ds(pl.multiple_of(block * KEY_BLOCK, KEY_BLOCK), KEY_BLOCK)
        exps = jnp.exp(score_ref[part, :] - top)
        total = total + jnp.sum(exps, axis=0, keepdims=True)
        return total, mixed + dot(value_t_ref[:, part], low(exps), (1, 0))

    total, mixed = lax.fori_loop(
        0,
        blocks,
        second,
        (jnp.zeros((1, 2 * rows), jnp.float32), jnp.zeros((HEAD_DIM, 2 * rows), jnp.float32)),
        unroll=2,
    )
    mixed = low((mixed / total).T)
    out_ref[:, :HEAD_DIM] = mixed[:rows]
    out_ref[:, HEAD_DIM:] = mixed[rows:]
    lse_ref[0] = top + jnp.log(total)


def attend(queries, keys, values, bias):
    rows, width = queries.shape
    pairs = width // (2 * HEAD_DIM)
    count = keys.shape[0]

    def whole(shape):
        return pl.BlockSpec(shape, lambda p: (0,) * len(shape))

    pair = pl.BlockSpec((rows, 2 * HEAD_DIM), lambda p: (0, p))
    return pl.pallas_call(
        attend_kernel,
        grid=(pairs,),
        in_specs=[pair, whole(keys.shape), whole((HEAD_DIM, count)), whole(bias.shape)],
        out_specs=[pair, pl.BlockSpec((1, 1, 2 * rows), lambda p: (p, 0, 0))],
        out_shape=[
            jax.ShapeDtypeStruct((rows, width), jnp.bfloat16),
            jax.ShapeDtypeStruct((pairs, 1, 2 * rows), jnp.float32),
        ],
        scratch_shapes=[pltpu.VMEM((count, 2 * rows), jnp.float32)],
        compiler_params=pltpu.CompilerParams(vmem_limit_bytes=48 * 1024 * 1024),
        cost_estimate=pl.CostEstimate(
            flops=4 * rows * width * count,
            bytes_accessed=8 * rows * width + 12 * bias.size,
            transcendentals=pairs * bias.size,
        ),
        name="attend",
    )(queries, keys, values.T, bias)


def attend_back_kernel(query_ref, grad_ref, key_ref, key_t_ref, value_ref, bias_ref, lse_ref,
                       delta_ref, grad_query_ref, grad_window_ref):
    rows = query_ref.shape[0]
    queries = stacked_heads(query_ref)
    grads = stacked_heads(grad_ref)
    blocks = key_ref.shape[0] // KEY_BLOCK

    @pl.when(pl.program_id(0) == 0)
    def _():
        grad_window_ref[...] = jnp.zeros_like(grad_window_ref)

    lse = lse_ref[0]
    delta = delta_ref[0]

    def body(block, grad_query):
        part = pl.ds(pl.multiple_of(block * KEY_BLOCK, KEY_BLOCK), KEY_BLOCK)
        probs = jnp.exp(dot(key_ref[part, :], queries, (1, 1)) + bias_ref[part, :] - lse)
        grad_probs = dot(value_ref[part, :], grads, (1, 1))
        grad_scores = low(probs * (grad_probs - delta))
        grad_window_ref[part, :HEAD_DIM] += dot(grad_scores, queries, (1, 0))
        grad_window_ref[part, HEAD_DIM:] += dot(low(probs), grads, (1, 0))
        return grad_query + dot(key_t_ref[:, part], grad_scores, (1, 0))

    grad_query = jnp.zeros((HEAD_DIM, 2 * rows), jnp.float32)
    grad_query = lax.fori_loop(0, blocks, body, grad_query, unroll=2).T
    grad_query_ref[:, :HEAD_DIM] = grad_query[:rows]
    grad_query_ref[:, HEAD_DIM:] = grad_query[rows:]


def attend_back(queries, grads, keys, values, bias, lse, delta):
    rows, width = queries.shape
    pairs = width // (2 * HEAD_DIM)
    count = keys.shape[0]

    def whole(shape):
        return pl.BlockSpec(shape, lambda p: (0,) * len(shape))

    pair = pl.BlockSpec((rows, 2 * HEAD_DIM), lambda p: (0, p))
    line = pl.BlockSpec((1, 1, 2 * rows), lambda p: (p, 0, 0))
    return pl.pallas_call(
        attend_back_kernel,
        grid=(pairs,),
        in_specs=[
            pair,
            pair,
            whole(keys.shape),
            whole((HEAD_DIM, count)),
            whole(values.shape),
            whole(bias.shape),
            line,
            line,
        ],
        out_specs=[pair, whole((count, 2 * HEAD_DIM))],
        out_shape=[
            jax.ShapeDtypeStruct((rows, width), jnp.float32),
            jax.ShapeDtypeStruct((count, 2 * HEAD_DIM), jnp.float32),
        ],
        compiler_params=pltpu.CompilerParams(vmem_limit_bytes=48 * 1024 * 1024),
        cost_estimate=pl.CostEstimate(
            flops=10 * rows * width * count,
            bytes_accessed=8 * rows * width + 16 * bias.size,
            transcendentals=pairs * bias.size,
        ),
        name="attend_back",
    )(queries, grads, keys, keys.T, values, bias, lse, delta)


def on_device(
    hidden_in,
    cotangent,
    lengths,
    weight_qkv,
    first_qkv,
    second_qkv,
    weight_out,
    first_out,
    second_out,
    weight_mlp,
    first_mlp,
    second_mlp,
    norm_gains,
    first_gains,
    second_gains,
):
    tok_rows = hidden_in.shape[2]
    width = hidden_in.shape[3]
    head_count = width // HEAD_DIM
    sides = lax.axis_size("seq")
    columns = lax.axis_size("k")
    members = columns * lax.axis_size("c")
    planes = lax.axis_size("g") * lax.axis_size("h")
    owner_count = planes * members
    blocks_in_side = lax.axis_size("h") * members
    side = lax.axis_index("seq")
    core = lax.axis_index("c")
    packed_index = lax.axis_index("g")
    place = lax.axis_index(("h", "k", "c"))
    own_rows = weight_mlp.shape[0]
    ff_width = weight_mlp.shape[2]
    piece = -(-ff_width // (sides * members * LANES)) * LANES

    gains_low = wide(low(norm_gains))
    gain_one = gains_low[:, :1]
    gain_two = gains_low[:, 1:]
    qkv_low = wide(low(weight_qkv))
    def regrouped(value, outer, inner):
        value = value.reshape(value.shape[0], outer, inner, own_rows).transpose(0, 2, 1, 3)
        return value.reshape(value.shape[0], outer * inner * own_rows)

    mlp_planes = weight_mlp.transpose(1, 0, 2)
    gate_up_chunks, down_chunks = mlp_chunks(mlp_planes, gain_two, side, members, piece)

    def to_members(chunks):
        return exchanged(chunks, ("k", "c")).reshape(members * own_rows, chunks.shape[2])

    incoming = cotangent.reshape(tok_rows, width)
    def own_half(weight):
        half = weight.shape[1] // sides
        return lax.dynamic_slice_in_dim(weight, side * half, half, 1)

    def gathered_group(weight):
        half = weight.shape[1]
        weight = lax.all_gather(weight, GROUP, axis=0, tiled=True)
        return weight.reshape(sides, owner_count * own_rows, half)

    gate_up_blocks = [to_members(gate_up_chunks)]
    plane_rows = [own_half(low(qkv_low * gain_one)), own_half(low(weight_out))]
    split = plane_rows[0].shape[1]
    plane_rows = jnp.concatenate(plane_rows, axis=1)
    plane_rows = lax.all_gather(plane_rows, PLANES, axis=0, tiled=True)
    plane_rows = after(plane_rows, gate_up_blocks[0])
    qkv_halves = gathered_group(plane_rows[:, :split])
    out_halves = gathered_group(plane_rows[:, split:])
    gate_up_blocks.append(next_plane(after(gate_up_blocks[0], plane_rows)))
    down_blocks = [to_members(down_chunks)]
    down_blocks.append(next_plane(down_blocks[0]))
    incoming_columns = doubled(incoming, "k", 1, 0)

    tokens = wide(hidden_in.reshape(tok_rows, width))
    lengths_row = lax.dynamic_index_in_dim(lengths, packed_index, 0, keepdims=False)
    row_numbers = jnp.arange(tok_rows, dtype=jnp.int32)
    query_docs, query_places = doc_places(
        lengths_row, (place * sides + side) * tok_rows + row_numbers
    )
    blocks = jnp.arange(blocks_in_side, dtype=jnp.int32)[None, :] * sides
    blocks = blocks + jnp.arange(sides, dtype=jnp.int32)[:, None]
    key_offsets = (blocks[:, :, None] * tok_rows + row_numbers).reshape(-1)
    key_docs, key_places = doc_places(lengths_row, key_offsets)
    distance = query_places[:, None] - key_places[None, :]
    allowed = (query_docs[:, None] == key_docs[None, :]) & (distance >= 0) & (distance < WINDOW)
    cosine, sine = rope_angles(query_places, HEAD_DIM)
    query_scale = HEAD_DIM ** (-0.5)

    factor_one = lax.rsqrt(jnp.mean(tokens * tokens, axis=-1, keepdims=True) + NORM_EPS)
    normed_one = low(tokens * factor_one)
    normed_one = after(normed_one, incoming_columns, gate_up_blocks[1], down_blocks[1])
    rows = regrouped(normed_one, planes, members)
    projected = jnp.concatenate([dot(rows, half, (1, 0)) for half in qkv_halves], axis=1)
    key_pre = projected[:, width : width + HEAD_DIM]
    value_low = low(projected[:, width + HEAD_DIM :])
    key_low = low(rotate(key_pre, cosine, sine))
    window_kv = spread_ring(jnp.concatenate([key_low, value_low], axis=1))
    window_kv = doubled(window_kv, "c", 1, 1)
    window_kv = window_kv.reshape(SEQ_LEN, 2 * HEAD_DIM)
    gate_up_blocks.append(next_plane(after(gate_up_blocks[1], projected)))
    for _ in range(planes - 4):
        gate_up_blocks.append(next_plane(gate_up_blocks[-1]))
    last = gate_up_blocks[-1]
    gate_up_blocks.append([next_plane(last[:, :piece]), next_plane(last[:, piece:])])
    down_blocks.append(next_plane(after(down_blocks[1], projected)))
    for _ in range(planes - 3):
        down_blocks.append(next_plane(down_blocks[-1]))
    gate_up_own = joined_planes(gate_up_blocks)
    down_own = joined_planes(down_blocks)
    incoming_sides = doubled(after(incoming_columns, window_kv), "seq", 1, 0)
    query_pre = projected[:, :width].reshape(tok_rows, head_count, HEAD_DIM)
    queries = low(rotate(query_pre, cosine[:, None, :], sine[:, None, :]) * query_scale)
    incoming_all = doubled(incoming_sides, "c", 1, incoming_sides.ndim - 2)
    incoming_all = incoming_all.reshape(sides * members * tok_rows, width)
    queries = after(queries.reshape(tok_rows, width), gate_up_blocks[2], down_blocks[2])
    keys_win = window_kv[:, :HEAD_DIM]
    values_win = window_kv[:, HEAD_DIM:]
    bias = jnp.where(allowed.T, 0.0, MASKED_SCORE)
    bias = jnp.concatenate([bias, bias], axis=1)
    attn_low, log_total = attend(queries, keys_win, values_win, bias)
    attn_low = after(attn_low, incoming_sides)
    rows = regrouped(attn_low, planes, members)
    branch = [dot(rows, half, (1, 0)) for half in out_halves]
    middle = tokens + jnp.concatenate(branch, axis=1)

    factor_two = lax.rsqrt(jnp.mean(middle * middle, axis=-1, keepdims=True) + NORM_EPS)
    normed_two = after(low(middle * factor_two), gate_up_blocks[-1][0])
    normed_two_all = lax.all_gather(normed_two, GROUP, axis=0, tiled=True)
    grad_act = low(dot(incoming_all, down_own, (1, 0)))
    gate_up = dot(after(normed_two_all, down_own, incoming_all), gate_up_own, (1, 0))
    activated, glu_back = jax.vjp(glu_values, gate_up[:, :piece], gate_up[:, piece:])
    activated_low = low(activated)
    def to_owners(term):
        return lax.psum_scatter(term, PLANES, scatter_dimension=0, tiled=True)

    down_term = low(dot(incoming_all, activated_low, (0, 0)))
    down_rows = to_owners(down_term)
    attn_all = lax.all_gather(after(attn_low, down_term), GROUP, axis=0, tiled=True)
    grad_gate, grad_up = glu_back(wide(after(grad_act, down_term)))
    grad_gate_up = low(jnp.concatenate([grad_gate, grad_up], axis=1))

    def in_plane(term, *others):
        term = term.reshape(members, own_rows, term.shape[1])
        ours = exchanged(after(term, *others), ("k", "c"))
        return (ours, swapped(ours, "seq"))

    def group_terms(hidden, weight):
        by_core = hidden.reshape(sides * columns, 2, tok_rows, hidden.shape[1])

        def one_core(which):
            rows = lax.dynamic_index_in_dim(by_core, which, 1, keepdims=False)
            return dot(rows.reshape(-1, hidden.shape[1]), weight, (1, 1))

        given = swapped(low(one_core(1 - core)), "c")
        return low(one_core(core) + wide(given)).reshape(sides * columns, tok_rows, width)

    terms = group_terms(grad_gate_up, gate_up_own)
    place = lax.axis_index(CHIPS)
    grad_normed_two = wide(lax.dynamic_index_in_dim(terms, place, 0, keepdims=False))
    arrived = []
    for step in range(1, sides * columns):
        term = lax.dynamic_index_in_dim(terms, place ^ step, 0, keepdims=False)
        if step == sides * columns - 1:
            term = after(term, *arrived)
        arrived.append(lax.ppermute(term, CHIPS, traded(CHIPS, step)))
    late = after(grad_gate_up, *arrived[:-1])
    gate_term = low(dot(normed_two_all, late[:, :piece], (0, 0)))
    up_term = low(dot(normed_two_all, late[:, piece:], (0, 0)))
    grad_normed_two = grad_normed_two + sum(wide(term) for term in arrived)
    grad_normed_two = after(grad_normed_two, gate_term, up_term)

    gate_rows = to_owners(gate_term)
    up_rows = to_owners(up_term)
    grad_middle = (
        wide(incoming)
        + factor_two * grad_normed_two
        - middle * factor_two**3 * jnp.mean(grad_normed_two * middle, axis=-1, keepdims=True)
    )

    shares = sides * members

    def by_column(*terms):
        terms = [term.reshape(tok_rows, shares, term.shape[1] // shares) for term in terms]
        terms = jnp.concatenate(terms, axis=2).transpose(1, 0, 2)
        return exchanged(terms, GROUP)

    def to_rows(total):
        total = exchanged(total.reshape(owner_count, own_rows, -1), OWNERS)
        return low(jnp.sum(wide(total.reshape(planes, members, own_rows, -1)), axis=0))

    def joined(total):
        return wide(total.transpose(1, 0, 2).reshape(own_rows, -1))

    grad_branch_low = low(grad_middle)
    half = width // sides
    grad_mixed = sum(
        dot(grad_branch_low[:, index * half : (index + 1) * half], out_halves[index], (1, 1))
        for index in range(sides)
    )
    down_pieces = in_plane(down_rows)
    grad_mixed_low = regrouped(low(grad_mixed), members, planes)
    delta = (wide(grad_mixed_low) * wide(attn_low)).reshape(tok_rows, head_count, HEAD_DIM)
    delta = jnp.sum(delta, axis=-1).T.reshape(log_total.shape)
    grad_query, grad_window = attend_back(
        queries, grad_mixed_low, keys_win, values_win, bias, log_total, delta
    )
    normed_one_columns = doubled(after(normed_one, grad_normed_two), "k", 1, 0)
    normed_one_sides = doubled(normed_one_columns, "seq", 1, 0)
    grad_window = after(low(grad_window), normed_one_sides)
    branch = low(dot(after(activated_low, grad_window), down_own, (1, 1)))
    normed_one_others = swapped(normed_one_sides, "c")
    grad_window = half_sum(grad_window.reshape(-1, 2, tok_rows, 2 * HEAD_DIM), "c", 1)
    grad_window = grad_window.reshape(sides, -1, columns, tok_rows, 2 * HEAD_DIM)
    grad_window = grad_window.swapaxes(1, 2).reshape(sides * columns, -1, tok_rows, 2 * HEAD_DIM)
    grad_local = wide(half_sum(low(ring_sum(grad_window)), "h", 0))

    mlp_states = (mlp_planes, first_mlp.transpose(1, 0, 2), second_mlp.transpose(1, 0, 2))
    rate_main = 2.0 * D ** (-0.5)

    def mlp_updated(part, pieces, outs):
        *outs, gain_dot = mlp_adam(part, side, pieces, mlp_states, gain_two, rate_main, outs)
        return outs, gain_dot

    mlp_outs, down_dot = mlp_updated(2, down_pieces, ())
    grad_local = after(grad_local, down_dot)
    grad_query = grad_query.reshape(tok_rows, head_count, HEAD_DIM)
    grad_query_pre = rotate(
        grad_query * query_scale, cosine[:, None, :], -sine[:, None, :]
    ).reshape(tok_rows, width)
    grad_key_pre = rotate(grad_local[:, :HEAD_DIM], cosine, -sine)
    grad_proj = low(
        jnp.concatenate([grad_query_pre, grad_key_pre, grad_local[:, HEAD_DIM:]], axis=1)
    )

    all_columns = by_column(after(grad_proj, normed_one_others, down_pieces[0]), grad_branch_low)
    qkv_share = grad_proj.shape[1] // shares
    by_core = all_columns.reshape(sides * columns, 2, tok_rows, -1)[:, :, :, :qkv_share]

    def one_core_total(rows, which):
        columns_there = lax.dynamic_index_in_dim(by_core, which, 1, keepdims=False)
        return dot(rows.reshape(-1, width), columns_there.reshape(-1, qkv_share), (0, 0))

    qkv_total = one_core_total(normed_one_sides, core)
    qkv_total = low(qkv_total + one_core_total(normed_one_others, 1 - core))
    out_columns = all_columns.reshape(shares * tok_rows, -1)[:, qkv_share:]
    out_total = low(dot(attn_all, out_columns, (0, 0)))
    gate_pieces = in_plane(gate_rows, all_columns)
    total = jnp.concatenate([qkv_total, out_total], axis=1)
    up_pieces = in_plane(up_rows, gate_pieces[0])
    total = to_rows(after(total, up_pieces[0]))
    branch = lax.psum_scatter(
        after(branch, all_columns), GROUP, scatter_dimension=0, tiled=True
    )
    mlp_outs, gate_dot = mlp_updated(0, gate_pieces, mlp_outs)
    (grad_mlp, second_new_mlp, new_mlp), up_dot = mlp_updated(1, up_pieces, mlp_outs)
    grad_gain_two = gate_dot + up_dot
    total = doubled(total, "seq", 1, 0).reshape(shares, own_rows, -1)
    grad_qkv = joined(total[:, :, :qkv_share])
    grad_out = joined(total[:, :, qkv_share:])
    hidden_out = low(middle + wide(branch)).reshape(1, 1, tok_rows, width)

    half = grad_proj.shape[1] // sides
    grad_normed = sum(
        dot(grad_proj[:, index * half : (index + 1) * half], qkv_halves[index], (1, 1))
        for index in range(sides)
    )
    grad_normed = regrouped(grad_normed, members, planes)
    hidden_grad = (
        grad_middle
        + factor_one * grad_normed
        - tokens * factor_one**3 * jnp.mean(grad_normed * tokens, axis=-1, keepdims=True)
    ).reshape(1, 1, tok_rows, width)

    rate_out = 2.0 * max(1, 6 * D // WINDOW) ** (-0.5)
    rate_gains = 0.4
    grad_gain_one = jnp.sum(qkv_low * grad_qkv, axis=1, keepdims=True)
    grad_qkv = grad_qkv * gain_one
    second_new_qkv, new_qkv = adam_step(weight_qkv, first_qkv, second_qkv, grad_qkv, rate_main)
    second_new_out, new_out = adam_step(weight_out, first_out, second_out, grad_out, rate_out)
    grad_gains = jnp.concatenate([grad_gain_one, grad_gain_two], axis=1)
    second_new_gains, new_gains = adam_step(
        norm_gains, first_gains, second_gains, grad_gains, rate_gains
    )
    return (
        hidden_out,
        hidden_grad,
        grad_qkv,
        second_new_qkv,
        new_qkv,
        grad_out,
        second_new_out,
        new_out,
        grad_mlp.transpose(1, 0, 2),
        second_new_mlp.transpose(1, 0, 2),
        new_mlp.transpose(1, 0, 2),
        grad_gains,
        second_new_gains,
        new_gains,
    )


def solution(mesh):
    seq_count, owner_count = mesh.devices.shape

    def whole(*arguments):
        members = SEQ_LEN // (seq_count * arguments[0].shape[2])
        shape = (seq_count, owner_count // members, members // 4, 2, 2)
        split = Mesh(mesh.devices.reshape(shape), ("seq", "g", "h", "k", "c"))
        acts = P(OWNERS, "seq", None, None)
        flat = P(OWNERS, None)
        planes = P(OWNERS, None, None)
        return jax.shard_map(
            on_device,
            mesh=split,
            in_specs=(acts, acts, P()) + (flat,) * 6 + (planes,) * 3 + (flat,) * 3,
            out_specs=(acts, acts) + (flat,) * 6 + (planes,) * 3 + (flat,) * 3,
            check_vma=False,
        )(*arguments)

    return whole
```

```python
import math

import jax
import jax.numpy as jnp
from jax import lax
from jax.experimental import pallas as pl
from jax.experimental.pallas import tpu as pltpu
from jax.sharding import Mesh, PartitionSpec as P

D = 2560
HEAD_DIM = 256
WINDOW = 2048
STEP = 10
SEQ_LEN = 3072

NORM_EPS = 1e-06
BETA_ONE = 0.9
BETA_TWO = 0.95
ADAM_EPS = 1e-08
DECAY_RATE = 0.1
MASKED_SCORE = -1e30

LANES = 512
KEY_BLOCK = 768
PLANES = ("g", "h")
OWNERS = ("g", "h", "k", "c")
CHIPS = ("seq", "k")
GROUP = ("seq", "k", "c")
RING = ("seq", "h", "k")


def rotate(values, cosine, sine):
    half_dim = values.shape[-1] // 2
    first_half = values[..., :half_dim]
    second_half = values[..., half_dim:]
    return jnp.concatenate(
        [first_half * cosine - second_half * sine, second_half * cosine + first_half * sine],
        axis=-1,
    )


def doc_places(lengths_row, offsets):
    doc_ends = jnp.cumsum(lengths_row)
    passed = (doc_ends[None, :] <= offsets[:, None]).astype(jnp.int32)
    document = jnp.sum(passed, axis=1)
    starts = jnp.sum(passed * lengths_row[None, :], axis=1)
    return (document, offsets - starts)


def rope_angles(places, head_dim):
    freq_index = jnp.arange(head_dim // 2, dtype=jnp.float32)
    inverse = jnp.exp(freq_index * (-2.0 * math.log(10000.0) / head_dim))
    angles = places.astype(jnp.float32)[:, None] * inverse[None, :]
    return (jnp.cos(angles), jnp.sin(angles))


def adam_step(weight, first, second, grad, rate):
    first_new = BETA_ONE * first + (1.0 - BETA_ONE) * grad
    second_new = BETA_TWO * second + (1.0 - BETA_TWO) * grad * grad
    first_hat = first_new / (1.0 - BETA_ONE**STEP)
    second_hat = second_new / (1.0 - BETA_TWO**STEP)
    update = first_hat / (jnp.sqrt(second_hat) + ADAM_EPS)
    return (second_new, weight - rate * (update + DECAY_RATE * weight))


def glu_values(gate_in, up_in):
    return jax.nn.gelu(gate_in, approximate=True) * up_in


def low(value):
    return value.astype(jnp.bfloat16)


def wide(value):
    return value.astype(jnp.float32)


def dot(left, right, contract):
    return lax.dot_general(
        left, right, ((contract[:1], contract[1:]), ((), ())), preferred_element_type=jnp.float32
    )


def traded(axes, step):
    count = math.prod(lax.axis_size(axis) for axis in axes)
    return [(source, source ^ step) for source in range(count)]


def swapped(value, axis):
    return lax.ppermute(value, axis, [(0, 1), (1, 0)])


def after(value, *others):
    return lax.optimization_barrier((value,) + others)[0]


def doubled(value, axis, step, place):
    other = lax.ppermute(value, axis, traded((axis,), step))
    first = (lax.axis_index(axis) & step) == 0
    return jnp.stack([jnp.where(first, value, other), jnp.where(first, other, value)], axis=place)


def next_plane(block):
    count = math.prod(lax.axis_size(axis) for axis in PLANES)
    return lax.ppermute(block, PLANES, [(one, (one + 1) % count) for one in range(count)])


def joined_planes(blocks):
    count, (rows, width) = len(blocks), blocks[0].shape
    whole = jnp.zeros((count * rows, width), blocks[0].dtype)
    for step, block in enumerate(blocks):
        start = lax.rem(lax.axis_index(PLANES) + (count - step), count) * rows
        column = 0
        for part in block if isinstance(block, list) else [block]:
            whole = lax.dynamic_update_slice(whole, part, (start, column))
            column += part.shape[1]
    return whole


def spread_ring(value):
    chips = math.prod(lax.axis_size(axis) for axis in RING)
    place = lax.axis_index(RING)
    whole = jnp.zeros((chips,) + value.shape, value.dtype)
    for step in range(chips):
        arrived = lax.ppermute(value, RING, traded(RING, step)) if step else value
        whole = lax.dynamic_update_index_in_dim(whole, arrived, place ^ step, 0)
    return whole


def ring_sum(terms):
    chips = terms.shape[0]
    place = lax.axis_index(CHIPS)
    total = 0.0
    for step in range(chips):
        term = lax.dynamic_index_in_dim(terms, place ^ step, 0, keepdims=False)
        if step:
            term = lax.ppermute(term, CHIPS, traded(CHIPS, step))
        total = total + wide(term)
    return total


def exchanged(value, axes):
    return lax.all_to_all(value, axes, split_axis=0, concat_axis=0, tiled=True)


def half_sum(terms, axis, place):
    here = lax.axis_index(axis)
    kept = lax.dynamic_index_in_dim(terms, here, place, keepdims=False)
    given = lax.dynamic_index_in_dim(terms, 1 - here, place, keepdims=False)
    return low(wide(kept) + wide(swapped(given, axis)))


def mlp_chunks_kernel(slices, side_ref, weight_ref, gain_ref, gate_up_ref, down_ref):
    per_piece = pl.num_programs(1)
    index = side_ref[0] * pl.num_programs(0) + pl.program_id(0)
    index = index * per_piece + pl.program_id(1)
    width = weight_ref.shape[2]
    lane = pl.program_id(1) * width
    gain = gain_ref[...]
    for part in range(3):
        weight = wide(low(weight_ref[part]))
        if part < 2:
            weight = weight * gain
        weight = low(jnp.where(index < slices, weight, 0.0))
        if part < 2:
            place = pl.multiple_of(part * per_piece * width + lane, width)
            gate_up_ref[0, :, pl.ds(place, width)] = weight
        else:
            down_ref[0, :, pl.ds(pl.multiple_of(lane, width), width)] = weight


def mlp_chunks(weight, gain, side, members, piece):
    parts, rows, ff_width = weight.shape
    slices = ff_width // LANES
    per_piece = piece // LANES

    def weight_block(m, b, side_ref):
        return (0, 0, jnp.minimum((side_ref[0] * members + m) * per_piece + b, slices - 1))

    def out_block(m, b, side_ref):
        return (m, 0, 0)

    return pl.pallas_call(
        lambda *refs: mlp_chunks_kernel(slices, *refs),
        grid_spec=pltpu.PrefetchScalarGridSpec(
            num_scalar_prefetch=1,
            grid=(members, per_piece),
            in_specs=[
                pl.BlockSpec((parts, rows, LANES), weight_block),
                pl.BlockSpec((rows, 1), lambda m, b, side_ref: (0, 0)),
            ],
            out_specs=[
                pl.BlockSpec((1, rows, 2 * piece), out_block),
                pl.BlockSpec((1, rows, piece), out_block),
            ],
        ),
        out_shape=[
            jax.ShapeDtypeStruct((members, rows, 2 * piece), jnp.bfloat16),
            jax.ShapeDtypeStruct((members, rows, piece), jnp.bfloat16),
        ],
        compiler_params=pltpu.CompilerParams(vmem_limit_bytes=48 * 1024 * 1024),
        cost_estimate=pl.CostEstimate(
            flops=weight.size, bytes_accessed=3 * weight.size, transcendentals=0
        ),
        name="mlp_chunks",
    )(jnp.full((1,), side, jnp.int32), weight, gain)


def mlp_adam_kernel(rate, per_side, scaled, side_ref, ours_ref, theirs_ref, weight_ref, first_ref,
                    second_ref, gain_ref, *refs):
    grad_out, second_out, weight_out, dot_out = refs[-4:]
    block = pl.program_id(0)
    ours = block // per_side == side_ref[0]
    grad = wide(jnp.where(ours, ours_ref[0], theirs_ref[0]))
    weight = weight_ref[0]
    dot_part = jnp.sum(wide(low(weight)) * grad, axis=1, keepdims=True)
    dot_out[...] = jnp.where(block == 0, dot_part, dot_out[...] + dot_part)
    if scaled:
        grad = grad * gain_ref[...]
    grad_out[0] = grad
    second_out[0], weight_out[0] = adam_step(weight, first_ref[0], second_ref[0], grad, rate)


def mlp_adam(part, side, pieces, column, piece, states, gain, rate, outs):
    _, rows, ff_width = states[0].shape
    members = pieces[0].shape[0]
    per_piece = piece // LANES
    per_side = members * per_piece

    def grad_block(own):
        def place(b, side_ref):
            used = (b // per_side == side_ref[0]) == own
            inner = jnp.where(used, b % per_side, 0)
            return (inner // per_piece, 0, column // LANES + inner % per_piece)

        return pl.BlockSpec((1, rows, LANES), place)

    state = pl.BlockSpec((1, rows, LANES), lambda b, side_ref: (part, 0, b))
    gains = pl.BlockSpec((rows, 1), lambda b, side_ref: (0, 0))
    size = rows * ff_width
    return pl.pallas_call(
        lambda *refs: mlp_adam_kernel(rate, per_side, part < 2, *refs),
        grid_spec=pltpu.PrefetchScalarGridSpec(
            num_scalar_prefetch=1,
            grid=(ff_width // LANES,),
            in_specs=[grad_block(True), grad_block(False), state, state, state, gains]
            + [pl.BlockSpec(memory_space=pl.ANY)] * len(outs),
            out_specs=[state, state, state, gains],
        ),
        out_shape=[jax.ShapeDtypeStruct(states[0].shape, jnp.float32)] * 3
        + [jax.ShapeDtypeStruct((rows, 1), jnp.float32)],
        input_output_aliases={7 + index: index for index in range(len(outs))},
        compiler_params=pltpu.CompilerParams(vmem_limit_bytes=48 * 1024 * 1024),
        cost_estimate=pl.CostEstimate(
            flops=20 * size, bytes_accessed=26 * size, transcendentals=size
        ),
        name="mlp_adam",
    )(jnp.full((1,), side, jnp.int32), *pieces, *states, gain, *outs)


def stacked_heads(ref):
    return jnp.concatenate([ref[:, :HEAD_DIM], ref[:, HEAD_DIM:]], axis=0)


def attend_kernel(query_ref, key_ref, value_t_ref, bias_ref, out_ref, lse_ref, score_ref):
    rows = query_ref.shape[0]
    queries = stacked_heads(query_ref)
    blocks = key_ref.shape[0] // KEY_BLOCK

    def first(block, top):
        part = pl.ds(pl.multiple_of(block * KEY_BLOCK, KEY_BLOCK), KEY_BLOCK)
        scores = dot(key_ref[part, :], queries, (1, 1)) + bias_ref[part, :]
        score_ref[part, :] = scores
        return jnp.maximum(top, jnp.max(scores, axis=0, keepdims=True))

    top = jnp.full((1, 2 * rows), -jnp.inf, jnp.float32)
    top = lax.fori_loop(0, blocks, first, top, unroll=2)

    def second(block, carry):
        total, mixed = carry
        part = pl.ds(pl.multiple_of(block * KEY_BLOCK, KEY_BLOCK), KEY_BLOCK)
        exps = jnp.exp(score_ref[part, :] - top)
        total = total + jnp.sum(exps, axis=0, keepdims=True)
        return total, mixed + dot(value_t_ref[:, part], low(exps), (1, 0))

    total, mixed = lax.fori_loop(
        0,
        blocks,
        second,
        (jnp.zeros((1, 2 * rows), jnp.float32), jnp.zeros((HEAD_DIM, 2 * rows), jnp.float32)),
        unroll=2,
    )
    mixed = low((mixed / total).T)
    out_ref[:, :HEAD_DIM] = mixed[:rows]
    out_ref[:, HEAD_DIM:] = mixed[rows:]
    lse_ref[0] = top + jnp.log(total)


def attend(queries, keys, values, bias):
    rows, width = queries.shape
    pairs = width // (2 * HEAD_DIM)
    count = keys.shape[0]

    def whole(shape):
        return pl.BlockSpec(shape, lambda p: (0,) * len(shape))

    pair = pl.BlockSpec((rows, 2 * HEAD_DIM), lambda p: (0, p))
    return pl.pallas_call(
        attend_kernel,
        grid=(pairs,),
        in_specs=[pair, whole(keys.shape), whole((HEAD_DIM, count)), whole(bias.shape)],
        out_specs=[pair, pl.BlockSpec((1, 1, 2 * rows), lambda p: (p, 0, 0))],
        out_shape=[
            jax.ShapeDtypeStruct((rows, width), jnp.bfloat16),
            jax.ShapeDtypeStruct((pairs, 1, 2 * rows), jnp.float32),
        ],
        scratch_shapes=[pltpu.VMEM((count, 2 * rows), jnp.float32)],
        compiler_params=pltpu.CompilerParams(vmem_limit_bytes=48 * 1024 * 1024),
        cost_estimate=pl.CostEstimate(
            flops=4 * rows * width * count,
            bytes_accessed=8 * rows * width + 12 * bias.size,
            transcendentals=pairs * bias.size,
        ),
        name="attend",
    )(queries, keys, values.T, bias)


def attend_back_kernel(query_ref, grad_ref, key_ref, key_t_ref, value_ref, bias_ref, lse_ref,
                       delta_ref, grad_query_ref, grad_window_ref):
    rows = query_ref.shape[0]
    queries = stacked_heads(query_ref)
    grads = stacked_heads(grad_ref)
    blocks = key_ref.shape[0] // KEY_BLOCK

    @pl.when(pl.program_id(0) == 0)
    def _():
        grad_window_ref[...] = jnp.zeros_like(grad_window_ref)

    lse = lse_ref[0]
    delta = delta_ref[0]

    def body(block, grad_query):
        part = pl.ds(pl.multiple_of(block * KEY_BLOCK, KEY_BLOCK), KEY_BLOCK)
        probs = jnp.exp(dot(key_ref[part, :], queries, (1, 1)) + bias_ref[part, :] - lse)
        grad_probs = dot(value_ref[part, :], grads, (1, 1))
        grad_scores = low(probs * (grad_probs - delta))
        grad_window_ref[part, :HEAD_DIM] += dot(grad_scores, queries, (1, 0))
        grad_window_ref[part, HEAD_DIM:] += dot(low(probs), grads, (1, 0))
        return grad_query + dot(key_t_ref[:, part], grad_scores, (1, 0))

    grad_query = jnp.zeros((HEAD_DIM, 2 * rows), jnp.float32)
    grad_query = lax.fori_loop(0, blocks, body, grad_query, unroll=2).T
    grad_query_ref[:, :HEAD_DIM] = grad_query[:rows]
    grad_query_ref[:, HEAD_DIM:] = grad_query[rows:]


def attend_back(queries, grads, keys, values, bias, lse, delta):
    rows, width = queries.shape
    pairs = width // (2 * HEAD_DIM)
    count = keys.shape[0]

    def whole(shape):
        return pl.BlockSpec(shape, lambda p: (0,) * len(shape))

    pair = pl.BlockSpec((rows, 2 * HEAD_DIM), lambda p: (0, p))
    line = pl.BlockSpec((1, 1, 2 * rows), lambda p: (p, 0, 0))
    return pl.pallas_call(
        attend_back_kernel,
        grid=(pairs,),
        in_specs=[
            pair,
            pair,
            whole(keys.shape),
            whole((HEAD_DIM, count)),
            whole(values.shape),
            whole(bias.shape),
            line,
            line,
        ],
        out_specs=[pair, whole((count, 2 * HEAD_DIM))],
        out_shape=[
            jax.ShapeDtypeStruct((rows, width), jnp.float32),
            jax.ShapeDtypeStruct((count, 2 * HEAD_DIM), jnp.float32),
        ],
        compiler_params=pltpu.CompilerParams(vmem_limit_bytes=48 * 1024 * 1024),
        cost_estimate=pl.CostEstimate(
            flops=10 * rows * width * count,
            bytes_accessed=8 * rows * width + 16 * bias.size,
            transcendentals=pairs * bias.size,
        ),
        name="attend_back",
    )(queries, grads, keys, keys.T, values, bias, lse, delta)


def on_device(
    hidden_in,
    cotangent,
    lengths,
    weight_qkv,
    first_qkv,
    second_qkv,
    weight_out,
    first_out,
    second_out,
    weight_mlp,
    first_mlp,
    second_mlp,
    norm_gains,
    first_gains,
    second_gains,
):
    tok_rows = hidden_in.shape[2]
    width = hidden_in.shape[3]
    head_count = width // HEAD_DIM
    sides = lax.axis_size("seq")
    columns = lax.axis_size("k")
    members = columns * lax.axis_size("c")
    planes = lax.axis_size("g") * lax.axis_size("h")
    owner_count = planes * members
    blocks_in_side = lax.axis_size("h") * members
    side = lax.axis_index("seq")
    core = lax.axis_index("c")
    packed_index = lax.axis_index("g")
    place = lax.axis_index(("h", "k", "c"))
    own_rows = weight_mlp.shape[0]
    ff_width = weight_mlp.shape[2]
    piece = -(-ff_width // (sides * members * LANES)) * LANES

    gains_low = wide(low(norm_gains))
    gain_one = gains_low[:, :1]
    gain_two = gains_low[:, 1:]
    qkv_low = wide(low(weight_qkv))
    def regrouped(value, outer, inner):
        value = value.reshape(value.shape[0], outer, inner, own_rows).transpose(0, 2, 1, 3)
        return value.reshape(value.shape[0], outer * inner * own_rows)

    mlp_planes = weight_mlp.transpose(1, 0, 2)
    gate_up_chunks, down_chunks = mlp_chunks(mlp_planes, gain_two, side, members, piece)

    def to_members(chunks):
        return exchanged(chunks, ("k", "c")).reshape(members * own_rows, chunks.shape[2])

    incoming = cotangent.reshape(tok_rows, width)
    def own_half(weight):
        half = weight.shape[1] // sides
        return lax.dynamic_slice_in_dim(weight, side * half, half, 1)

    def gathered_group(weight):
        half = weight.shape[1]
        weight = lax.all_gather(weight, GROUP, axis=0, tiled=True)
        return weight.reshape(sides, owner_count * own_rows, half)

    gate_up_blocks = [to_members(gate_up_chunks)]
    plane_rows = [own_half(low(qkv_low * gain_one)), own_half(low(weight_out))]
    split = plane_rows[0].shape[1]
    plane_rows = jnp.concatenate(plane_rows, axis=1)
    plane_rows = lax.all_gather(plane_rows, PLANES, axis=0, tiled=True)
    plane_rows = after(plane_rows, gate_up_blocks[0])
    qkv_halves = gathered_group(plane_rows[:, :split])
    out_halves = gathered_group(plane_rows[:, split:])
    gate_up_blocks.append(next_plane(after(gate_up_blocks[0], plane_rows)))
    down_blocks = [to_members(down_chunks)]
    down_blocks.append(next_plane(down_blocks[0]))
    incoming_columns = doubled(incoming, "k", 1, 0)

    tokens = wide(hidden_in.reshape(tok_rows, width))
    lengths_row = lax.dynamic_index_in_dim(lengths, packed_index, 0, keepdims=False)
    row_numbers = jnp.arange(tok_rows, dtype=jnp.int32)
    query_docs, query_places = doc_places(
        lengths_row, (place * sides + side) * tok_rows + row_numbers
    )
    blocks = jnp.arange(blocks_in_side, dtype=jnp.int32)[None, :] * sides
    blocks = blocks + jnp.arange(sides, dtype=jnp.int32)[:, None]
    key_offsets = (blocks[:, :, None] * tok_rows + row_numbers).reshape(-1)
    key_docs, key_places = doc_places(lengths_row, key_offsets)
    distance = query_places[:, None] - key_places[None, :]
    allowed = (query_docs[:, None] == key_docs[None, :]) & (distance >= 0) & (distance < WINDOW)
    cosine, sine = rope_angles(query_places, HEAD_DIM)
    query_scale = HEAD_DIM ** (-0.5)

    factor_one = lax.rsqrt(jnp.mean(tokens * tokens, axis=-1, keepdims=True) + NORM_EPS)
    normed_one = low(tokens * factor_one)
    normed_one = after(normed_one, incoming_columns, gate_up_blocks[1], down_blocks[1])
    rows = regrouped(normed_one, planes, members)
    projected = jnp.concatenate([dot(rows, half, (1, 0)) for half in qkv_halves], axis=1)
    key_pre = projected[:, width : width + HEAD_DIM]
    value_low = low(projected[:, width + HEAD_DIM :])
    key_low = low(rotate(key_pre, cosine, sine))
    window_kv = spread_ring(jnp.concatenate([key_low, value_low], axis=1))
    window_kv = doubled(window_kv, "c", 1, 1)
    window_kv = window_kv.reshape(SEQ_LEN, 2 * HEAD_DIM)
    gate_up_blocks.append(next_plane(after(gate_up_blocks[1], projected)))
    for _ in range(planes - 4):
        gate_up_blocks.append(next_plane(gate_up_blocks[-1]))
    last = gate_up_blocks[-1]
    gate_up_blocks.append([next_plane(last[:, :piece]), next_plane(last[:, piece:])])
    down_blocks.append(next_plane(after(down_blocks[1], projected)))
    for _ in range(planes - 3):
        down_blocks.append(next_plane(down_blocks[-1]))
    gate_up_own = joined_planes(gate_up_blocks)
    down_own = joined_planes(down_blocks)
    incoming_sides = doubled(after(incoming_columns, window_kv), "seq", 1, 0)
    query_pre = projected[:, :width].reshape(tok_rows, head_count, HEAD_DIM)
    queries = low(rotate(query_pre, cosine[:, None, :], sine[:, None, :]) * query_scale)
    incoming_all = doubled(incoming_sides, "c", 1, incoming_sides.ndim - 2)
    incoming_all = incoming_all.reshape(sides * members * tok_rows, width)
    queries = after(queries.reshape(tok_rows, width), gate_up_blocks[2], down_blocks[2])
    keys_win = window_kv[:, :HEAD_DIM]
    values_win = window_kv[:, HEAD_DIM:]
    bias = jnp.where(allowed.T, 0.0, MASKED_SCORE)
    bias = jnp.concatenate([bias, bias], axis=1)
    attn_low, log_total = attend(queries, keys_win, values_win, bias)
    attn_low = after(attn_low, incoming_sides)
    rows = regrouped(attn_low, planes, members)
    branch = [dot(rows, half, (1, 0)) for half in out_halves]
    middle = tokens + jnp.concatenate(branch, axis=1)

    factor_two = lax.rsqrt(jnp.mean(middle * middle, axis=-1, keepdims=True) + NORM_EPS)
    normed_two = after(low(middle * factor_two), gate_up_blocks[-1][0])
    normed_two_all = lax.all_gather(normed_two, GROUP, axis=0, tiled=True)
    grad_act = low(dot(incoming_all, down_own, (1, 0)))
    gate_up = dot(after(normed_two_all, down_own, incoming_all), gate_up_own, (1, 0))
    activated, glu_back = jax.vjp(glu_values, gate_up[:, :piece], gate_up[:, piece:])
    activated_low = low(activated)
    def to_owners(term):
        return lax.psum_scatter(term, PLANES, scatter_dimension=0, tiled=True)

    down_term = low(dot(incoming_all, activated_low, (0, 0)))
    down_rows = to_owners(down_term)
    attn_all = lax.all_gather(after(attn_low, down_term), GROUP, axis=0, tiled=True)
    grad_gate, grad_up = glu_back(wide(after(grad_act, down_term)))
    grad_gate_up = low(jnp.concatenate([grad_gate, grad_up], axis=1))

    def in_plane(term, *others):
        term = term.reshape(members, own_rows, term.shape[1])
        ours = exchanged(after(term, *others), ("k", "c"))
        return (ours, swapped(ours, "seq"))

    def group_terms(hidden, weight):
        by_core = hidden.reshape(sides * columns, 2, tok_rows, hidden.shape[1])

        def one_core(which):
            rows = lax.dynamic_index_in_dim(by_core, which, 1, keepdims=False)
            return dot(rows.reshape(-1, hidden.shape[1]), weight, (1, 1))

        given = swapped(low(one_core(1 - core)), "c")
        return low(one_core(core) + wide(given)).reshape(sides * columns, tok_rows, width)

    terms = group_terms(grad_gate_up, gate_up_own)
    place = lax.axis_index(CHIPS)
    grad_normed_two = wide(lax.dynamic_index_in_dim(terms, place, 0, keepdims=False))
    arrived = []
    for step in range(1, sides * columns):
        term = lax.dynamic_index_in_dim(terms, place ^ step, 0, keepdims=False)
        if step == sides * columns - 1:
            term = after(term, *arrived)
        arrived.append(lax.ppermute(term, CHIPS, traded(CHIPS, step)))
    late = after(grad_gate_up, *arrived[:-1])
    gate_term = low(dot(normed_two_all, late[:, :piece], (0, 0)))
    up_term = low(dot(normed_two_all, late[:, piece:], (0, 0)))
    grad_normed_two = grad_normed_two + sum(wide(term) for term in arrived)
    grad_normed_two = after(grad_normed_two, gate_term, up_term)

    gate_rows = to_owners(gate_term)
    up_rows = to_owners(up_term)
    grad_middle = (
        wide(incoming)
        + factor_two * grad_normed_two
        - middle * factor_two**3 * jnp.mean(grad_normed_two * middle, axis=-1, keepdims=True)
    )

    shares = sides * members

    def by_column(*terms):
        terms = [term.reshape(tok_rows, shares, term.shape[1] // shares) for term in terms]
        terms = jnp.concatenate(terms, axis=2).transpose(1, 0, 2)
        return exchanged(terms, GROUP)

    def to_rows(total):
        total = exchanged(total.reshape(owner_count, own_rows, -1), OWNERS)
        return low(jnp.sum(wide(total.reshape(planes, members, own_rows, -1)), axis=0))

    def joined(total):
        return wide(total.transpose(1, 0, 2).reshape(own_rows, -1))

    grad_branch_low = low(grad_middle)
    half = width // sides
    grad_mixed = sum(
        dot(grad_branch_low[:, index * half : (index + 1) * half], out_halves[index], (1, 1))
        for index in range(sides)
    )
    grad_mixed_low = regrouped(low(grad_mixed), members, planes)
    delta = (wide(grad_mixed_low) * wide(attn_low)).reshape(tok_rows, head_count, HEAD_DIM)
    delta = jnp.sum(delta, axis=-1).T.reshape(log_total.shape)
    grad_query, grad_window = attend_back(
        queries, grad_mixed_low, keys_win, values_win, bias, log_total, delta
    )
    normed_one_columns = doubled(after(normed_one, grad_normed_two), "k", 1, 0)
    normed_one_sides = doubled(normed_one_columns, "seq", 1, 0)
    grad_window = after(low(grad_window), normed_one_sides)
    branch = low(dot(after(activated_low, grad_window), down_own, (1, 1)))
    normed_one_others = swapped(normed_one_sides, "c")
    grad_window = half_sum(grad_window.reshape(-1, 2, tok_rows, 2 * HEAD_DIM), "c", 1)
    grad_window = grad_window.reshape(sides, -1, columns, tok_rows, 2 * HEAD_DIM)
    grad_window = grad_window.swapaxes(1, 2).reshape(sides * columns, -1, tok_rows, 2 * HEAD_DIM)
    grad_local = wide(half_sum(low(ring_sum(grad_window)), "h", 0))

    mlp_states = (mlp_planes, first_mlp.transpose(1, 0, 2), second_mlp.transpose(1, 0, 2))
    rate_main = 2.0 * D ** (-0.5)

    def mlp_updated(part, pieces, column, outs):
        *outs, gain_dot = mlp_adam(
            part, side, pieces, column, piece, mlp_states, gain_two, rate_main, outs
        )
        return outs, gain_dot

    grad_query = grad_query.reshape(tok_rows, head_count, HEAD_DIM)
    grad_query_pre = rotate(
        grad_query * query_scale, cosine[:, None, :], -sine[:, None, :]
    ).reshape(tok_rows, width)
    grad_key_pre = rotate(grad_local[:, :HEAD_DIM], cosine, -sine)
    grad_proj = low(
        jnp.concatenate([grad_query_pre, grad_key_pre, grad_local[:, HEAD_DIM:]], axis=1)
    )

    all_columns = by_column(after(grad_proj, normed_one_others), grad_branch_low)
    qkv_share = grad_proj.shape[1] // shares
    by_core = all_columns.reshape(sides * columns, 2, tok_rows, -1)[:, :, :, :qkv_share]

    def one_core_total(rows, which):
        columns_there = lax.dynamic_index_in_dim(by_core, which, 1, keepdims=False)
        return dot(rows.reshape(-1, width), columns_there.reshape(-1, qkv_share), (0, 0))

    qkv_total = one_core_total(normed_one_sides, core)
    qkv_total = low(qkv_total + one_core_total(normed_one_others, 1 - core))
    out_columns = all_columns.reshape(shares * tok_rows, -1)[:, qkv_share:]
    out_total = low(dot(attn_all, out_columns, (0, 0)))
    first_pieces = in_plane(jnp.concatenate([down_rows, gate_rows], axis=1), all_columns)
    total = jnp.concatenate([qkv_total, out_total], axis=1)
    total = to_rows(after(total, first_pieces[0]))
    up_pieces = in_plane(up_rows, total)
    branch = lax.psum_scatter(
        after(branch, all_columns), GROUP, scatter_dimension=0, tiled=True
    )
    mlp_outs, _ = mlp_updated(2, first_pieces, 0, ())
    mlp_outs, gate_dot = mlp_updated(0, first_pieces, piece, mlp_outs)
    (grad_mlp, second_new_mlp, new_mlp), up_dot = mlp_updated(1, up_pieces, 0, mlp_outs)
    grad_gain_two = gate_dot + up_dot
    total = doubled(total, "seq", 1, 0).reshape(shares, own_rows, -1)
    grad_qkv = joined(total[:, :, :qkv_share])
    grad_out = joined(total[:, :, qkv_share:])
    hidden_out = low(middle + wide(branch)).reshape(1, 1, tok_rows, width)

    half = grad_proj.shape[1] // sides
    grad_normed = sum(
        dot(grad_proj[:, index * half : (index + 1) * half], qkv_halves[index], (1, 1))
        for index in range(sides)
    )
    grad_normed = regrouped(grad_normed, members, planes)
    hidden_grad = (
        grad_middle
        + factor_one * grad_normed
        - tokens * factor_one**3 * jnp.mean(grad_normed * tokens, axis=-1, keepdims=True)
    ).reshape(1, 1, tok_rows, width)

    rate_out = 2.0 * max(1, 6 * D // WINDOW) ** (-0.5)
    rate_gains = 0.4
    grad_gain_one = jnp.sum(qkv_low * grad_qkv, axis=1, keepdims=True)
    grad_qkv = grad_qkv * gain_one
    second_new_qkv, new_qkv = adam_step(weight_qkv, first_qkv, second_qkv, grad_qkv, rate_main)
    second_new_out, new_out = adam_step(weight_out, first_out, second_out, grad_out, rate_out)
    grad_gains = jnp.concatenate([grad_gain_one, grad_gain_two], axis=1)
    second_new_gains, new_gains = adam_step(
        norm_gains, first_gains, second_gains, grad_gains, rate_gains
    )
    return (
        hidden_out,
        hidden_grad,
        grad_qkv,
        second_new_qkv,
        new_qkv,
        grad_out,
        second_new_out,
        new_out,
        grad_mlp.transpose(1, 0, 2),
        second_new_mlp.transpose(1, 0, 2),
        new_mlp.transpose(1, 0, 2),
        grad_gains,
        second_new_gains,
        new_gains,
    )


def solution(mesh):
    seq_count, owner_count = mesh.devices.shape

    def whole(*arguments):
        members = SEQ_LEN // (seq_count * arguments[0].shape[2])
        shape = (seq_count, owner_count // members, members // 4, 2, 2)
        split = Mesh(mesh.devices.reshape(shape), ("seq", "g", "h", "k", "c"))
        acts = P(OWNERS, "seq", None, None)
        flat = P(OWNERS, None)
        planes = P(OWNERS, None, None)
        return jax.shard_map(
            on_device,
            mesh=split,
            in_specs=(acts, acts, P()) + (flat,) * 6 + (planes,) * 3 + (flat,) * 3,
            out_specs=(acts, acts) + (flat,) * 6 + (planes,) * 3 + (flat,) * 3,
            check_vma=False,
        )(*arguments)

    return whole
```

```python
import math

import jax
import jax.numpy as jnp
from jax import lax
from jax.experimental import pallas as pl
from jax.experimental.pallas import tpu as pltpu
from jax.sharding import Mesh, PartitionSpec as P

D = 2560
HEAD_DIM = 256
WINDOW = 2048
STEP = 10
SEQ_LEN = 3072

NORM_EPS = 1e-06
BETA_ONE = 0.9
BETA_TWO = 0.95
ADAM_EPS = 1e-08
DECAY_RATE = 0.1
MASKED_SCORE = -1e30

LANES = 512
KEY_BLOCK = 768
PLANES = ("g", "h")
OWNERS = ("g", "h", "k", "c")
CHIPS = ("seq", "k")
GROUP = ("seq", "k", "c")
RING = ("seq", "h", "k")


def rotate(values, cosine, sine):
    half_dim = values.shape[-1] // 2
    first_half = values[..., :half_dim]
    second_half = values[..., half_dim:]
    return jnp.concatenate(
        [first_half * cosine - second_half * sine, second_half * cosine + first_half * sine],
        axis=-1,
    )


def doc_places(lengths_row, offsets):
    doc_ends = jnp.cumsum(lengths_row)
    passed = (doc_ends[None, :] <= offsets[:, None]).astype(jnp.int32)
    document = jnp.sum(passed, axis=1)
    starts = jnp.sum(passed * lengths_row[None, :], axis=1)
    return (document, offsets - starts)


def rope_angles(places, head_dim):
    freq_index = jnp.arange(head_dim // 2, dtype=jnp.float32)
    inverse = jnp.exp(freq_index * (-2.0 * math.log(10000.0) / head_dim))
    angles = places.astype(jnp.float32)[:, None] * inverse[None, :]
    return (jnp.cos(angles), jnp.sin(angles))


def adam_step(weight, first, second, grad, rate):
    first_new = BETA_ONE * first + (1.0 - BETA_ONE) * grad
    second_new = BETA_TWO * second + (1.0 - BETA_TWO) * grad * grad
    first_hat = first_new / (1.0 - BETA_ONE**STEP)
    second_hat = second_new / (1.0 - BETA_TWO**STEP)
    update = first_hat / (jnp.sqrt(second_hat) + ADAM_EPS)
    return (second_new, weight - rate * (update + DECAY_RATE * weight))


def glu_values(gate_in, up_in):
    return jax.nn.gelu(gate_in, approximate=True) * up_in


def low(value):
    return value.astype(jnp.bfloat16)


def wide(value):
    return value.astype(jnp.float32)


def dot(left, right, contract):
    return lax.dot_general(
        left, right, ((contract[:1], contract[1:]), ((), ())), preferred_element_type=jnp.float32
    )


def traded(axes, step):
    count = math.prod(lax.axis_size(axis) for axis in axes)
    return [(source, source ^ step) for source in range(count)]


def swapped(value, axis):
    return lax.ppermute(value, axis, [(0, 1), (1, 0)])


def after(value, *others):
    return lax.optimization_barrier((value,) + others)[0]


def doubled(value, axis, step, place):
    other = lax.ppermute(value, axis, traded((axis,), step))
    first = (lax.axis_index(axis) & step) == 0
    return jnp.stack([jnp.where(first, value, other), jnp.where(first, other, value)], axis=place)


def next_plane(block):
    count = math.prod(lax.axis_size(axis) for axis in PLANES)
    return lax.ppermute(block, PLANES, [(one, (one + 1) % count) for one in range(count)])


def joined_planes(blocks):
    count, (rows, width) = len(blocks), blocks[0].shape
    whole = jnp.zeros((count * rows, width), blocks[0].dtype)
    for step, block in enumerate(blocks):
        start = lax.rem(lax.axis_index(PLANES) + (count - step), count) * rows
        column = 0
        for part in block if isinstance(block, list) else [block]:
            whole = lax.dynamic_update_slice(whole, part, (start, column))
            column += part.shape[1]
    return whole


def spread_ring(value):
    chips = math.prod(lax.axis_size(axis) for axis in RING)
    place = lax.axis_index(RING)
    whole = jnp.zeros((chips,) + value.shape, value.dtype)
    for step in range(chips):
        arrived = lax.ppermute(value, RING, traded(RING, step)) if step else value
        whole = lax.dynamic_update_index_in_dim(whole, arrived, place ^ step, 0)
    return whole


def ring_sum(terms):
    chips = terms.shape[0]
    place = lax.axis_index(CHIPS)
    total = 0.0
    for step in range(chips):
        term = lax.dynamic_index_in_dim(terms, place ^ step, 0, keepdims=False)
        if step:
            term = lax.ppermute(term, CHIPS, traded(CHIPS, step))
        total = total + wide(term)
    return total


def exchanged(value, axes):
    return lax.all_to_all(value, axes, split_axis=0, concat_axis=0, tiled=True)


def half_sum(terms, axis, place):
    here = lax.axis_index(axis)
    kept = lax.dynamic_index_in_dim(terms, here, place, keepdims=False)
    given = lax.dynamic_index_in_dim(terms, 1 - here, place, keepdims=False)
    return low(wide(kept) + wide(swapped(given, axis)))


def mlp_chunks_kernel(slices, side_ref, weight_ref, gain_ref, gate_up_ref, down_ref):
    per_piece = pl.num_programs(1)
    index = side_ref[0] * pl.num_programs(0) + pl.program_id(0)
    index = index * per_piece + pl.program_id(1)
    width = weight_ref.shape[2]
    lane = pl.program_id(1) * width
    gain = gain_ref[...]
    for part in range(3):
        weight = wide(low(weight_ref[part]))
        if part < 2:
            weight = weight * gain
        weight = low(jnp.where(index < slices, weight, 0.0))
        if part < 2:
            place = pl.multiple_of(part * per_piece * width + lane, width)
            gate_up_ref[0, :, pl.ds(place, width)] = weight
        else:
            down_ref[0, :, pl.ds(pl.multiple_of(lane, width), width)] = weight


def mlp_chunks(weight, gain, side, members, piece):
    parts, rows, ff_width = weight.shape
    slices = ff_width // LANES
    per_piece = piece // LANES

    def weight_block(m, b, side_ref):
        return (0, 0, jnp.minimum((side_ref[0] * members + m) * per_piece + b, slices - 1))

    def out_block(m, b, side_ref):
        return (m, 0, 0)

    return pl.pallas_call(
        lambda *refs: mlp_chunks_kernel(slices, *refs),
        grid_spec=pltpu.PrefetchScalarGridSpec(
            num_scalar_prefetch=1,
            grid=(members, per_piece),
            in_specs=[
                pl.BlockSpec((parts, rows, LANES), weight_block),
                pl.BlockSpec((rows, 1), lambda m, b, side_ref: (0, 0)),
            ],
            out_specs=[
                pl.BlockSpec((1, rows, 2 * piece), out_block),
                pl.BlockSpec((1, rows, piece), out_block),
            ],
        ),
        out_shape=[
            jax.ShapeDtypeStruct((members, rows, 2 * piece), jnp.bfloat16),
            jax.ShapeDtypeStruct((members, rows, piece), jnp.bfloat16),
        ],
        compiler_params=pltpu.CompilerParams(vmem_limit_bytes=48 * 1024 * 1024),
        cost_estimate=pl.CostEstimate(
            flops=weight.size, bytes_accessed=3 * weight.size, transcendentals=0
        ),
        name="mlp_chunks",
    )(jnp.full((1,), side, jnp.int32), weight, gain)


def mlp_adam_kernel(rate, per_side, scaled, side_ref, ours_ref, theirs_ref, weight_ref, first_ref,
                    second_ref, gain_ref, *refs):
    grad_out, second_out, weight_out, dot_out = refs[-4:]
    block = pl.program_id(0)
    ours = block // per_side == side_ref[0]
    grad = wide(jnp.where(ours, ours_ref[0], theirs_ref[0]))
    weight = weight_ref[0]
    dot_part = jnp.sum(wide(low(weight)) * grad, axis=1, keepdims=True)
    dot_out[...] = jnp.where(block == 0, dot_part, dot_out[...] + dot_part)
    if scaled:
        grad = grad * gain_ref[...]
    grad_out[0] = grad
    second_out[0], weight_out[0] = adam_step(weight, first_ref[0], second_ref[0], grad, rate)


def mlp_adam(part, side, pieces, column, piece, states, gain, rate, outs):
    _, rows, ff_width = states[0].shape
    members = pieces[0].shape[0]
    per_piece = piece // LANES
    per_side = members * per_piece

    def grad_block(own):
        def place(b, side_ref):
            used = (b // per_side == side_ref[0]) == own
            inner = jnp.where(used, b % per_side, 0)
            return (inner // per_piece, 0, column // LANES + inner % per_piece)

        return pl.BlockSpec((1, rows, LANES), place)

    state = pl.BlockSpec((1, rows, LANES), lambda b, side_ref: (part, 0, b))
    gains = pl.BlockSpec((rows, 1), lambda b, side_ref: (0, 0))
    size = rows * ff_width
    return pl.pallas_call(
        lambda *refs: mlp_adam_kernel(rate, per_side, part < 2, *refs),
        grid_spec=pltpu.PrefetchScalarGridSpec(
            num_scalar_prefetch=1,
            grid=(ff_width // LANES,),
            in_specs=[grad_block(True), grad_block(False), state, state, state, gains]
            + [pl.BlockSpec(memory_space=pl.ANY)] * len(outs),
            out_specs=[state, state, state, gains],
        ),
        out_shape=[jax.ShapeDtypeStruct(states[0].shape, jnp.float32)] * 3
        + [jax.ShapeDtypeStruct((rows, 1), jnp.float32)],
        input_output_aliases={7 + index: index for index in range(len(outs))},
        compiler_params=pltpu.CompilerParams(vmem_limit_bytes=48 * 1024 * 1024),
        cost_estimate=pl.CostEstimate(
            flops=20 * size, bytes_accessed=26 * size, transcendentals=size
        ),
        name="mlp_adam",
    )(jnp.full((1,), side, jnp.int32), *pieces, *states, gain, *outs)


def stacked_heads(ref):
    return jnp.concatenate([ref[:, :HEAD_DIM], ref[:, HEAD_DIM:]], axis=0)


def attend_kernel(query_ref, key_ref, value_t_ref, bias_ref, out_ref, lse_ref, score_ref):
    rows = query_ref.shape[0]
    queries = stacked_heads(query_ref)
    blocks = key_ref.shape[0] // KEY_BLOCK

    def first(block, top):
        part = pl.ds(pl.multiple_of(block * KEY_BLOCK, KEY_BLOCK), KEY_BLOCK)
        scores = dot(key_ref[part, :], queries, (1, 1)) + bias_ref[part, :]
        score_ref[part, :] = scores
        return jnp.maximum(top, jnp.max(scores, axis=0, keepdims=True))

    top = jnp.full((1, 2 * rows), -jnp.inf, jnp.float32)
    top = lax.fori_loop(0, blocks, first, top, unroll=2)

    def second(block, carry):
        total, mixed = carry
        part = pl.ds(pl.multiple_of(block * KEY_BLOCK, KEY_BLOCK), KEY_BLOCK)
        exps = jnp.exp(score_ref[part, :] - top)
        total = total + jnp.sum(exps, axis=0, keepdims=True)
        return total, mixed + dot(value_t_ref[:, part], low(exps), (1, 0))

    total, mixed = lax.fori_loop(
        0,
        blocks,
        second,
        (jnp.zeros((1, 2 * rows), jnp.float32), jnp.zeros((HEAD_DIM, 2 * rows), jnp.float32)),
        unroll=2,
    )
    mixed = low((mixed / total).T)
    out_ref[:, :HEAD_DIM] = mixed[:rows]
    out_ref[:, HEAD_DIM:] = mixed[rows:]
    lse_ref[0] = top + jnp.log(total)


def attend(queries, keys, values, bias):
    rows, width = queries.shape
    pairs = width // (2 * HEAD_DIM)
    count = keys.shape[0]

    def whole(shape):
        return pl.BlockSpec(shape, lambda p: (0,) * len(shape))

    pair = pl.BlockSpec((rows, 2 * HEAD_DIM), lambda p: (0, p))
    return pl.pallas_call(
        attend_kernel,
        grid=(pairs,),
        in_specs=[pair, whole(keys.shape), whole((HEAD_DIM, count)), whole(bias.shape)],
        out_specs=[pair, pl.BlockSpec((1, 1, 2 * rows), lambda p: (p, 0, 0))],
        out_shape=[
            jax.ShapeDtypeStruct((rows, width), jnp.bfloat16),
            jax.ShapeDtypeStruct((pairs, 1, 2 * rows), jnp.float32),
        ],
        scratch_shapes=[pltpu.VMEM((count, 2 * rows), jnp.float32)],
        compiler_params=pltpu.CompilerParams(vmem_limit_bytes=48 * 1024 * 1024),
        cost_estimate=pl.CostEstimate(
            flops=4 * rows * width * count,
            bytes_accessed=8 * rows * width + 12 * bias.size,
            transcendentals=pairs * bias.size,
        ),
        name="attend",
    )(queries, keys, values.T, bias)


def attend_back_kernel(query_ref, grad_ref, key_ref, key_t_ref, value_ref, bias_ref, lse_ref,
                       delta_ref, grad_query_ref, grad_window_ref):
    rows = query_ref.shape[0]
    queries = stacked_heads(query_ref)
    grads = stacked_heads(grad_ref)
    blocks = key_ref.shape[0] // KEY_BLOCK

    @pl.when(pl.program_id(0) == 0)
    def _():
        grad_window_ref[...] = jnp.zeros_like(grad_window_ref)

    lse = lse_ref[0]
    delta = delta_ref[0]

    def body(block, grad_query):
        part = pl.ds(pl.multiple_of(block * KEY_BLOCK, KEY_BLOCK), KEY_BLOCK)
        probs = jnp.exp(dot(key_ref[part, :], queries, (1, 1)) + bias_ref[part, :] - lse)
        grad_probs = dot(value_ref[part, :], grads, (1, 1))
        grad_scores = low(probs * (grad_probs - delta))
        grad_window_ref[part, :HEAD_DIM] += dot(grad_scores, queries, (1, 0))
        grad_window_ref[part, HEAD_DIM:] += dot(low(probs), grads, (1, 0))
        return grad_query + dot(key_t_ref[:, part], grad_scores, (1, 0))

    grad_query = jnp.zeros((HEAD_DIM, 2 * rows), jnp.float32)
    grad_query = lax.fori_loop(0, blocks, body, grad_query, unroll=2).T
    grad_query_ref[:, :HEAD_DIM] = grad_query[:rows]
    grad_query_ref[:, HEAD_DIM:] = grad_query[rows:]


def attend_back(queries, grads, keys, values, bias, lse, delta):
    rows, width = queries.shape
    pairs = width // (2 * HEAD_DIM)
    count = keys.shape[0]

    def whole(shape):
        return pl.BlockSpec(shape, lambda p: (0,) * len(shape))

    pair = pl.BlockSpec((rows, 2 * HEAD_DIM), lambda p: (0, p))
    line = pl.BlockSpec((1, 1, 2 * rows), lambda p: (p, 0, 0))
    return pl.pallas_call(
        attend_back_kernel,
        grid=(pairs,),
        in_specs=[
            pair,
            pair,
            whole(keys.shape),
            whole((HEAD_DIM, count)),
            whole(values.shape),
            whole(bias.shape),
            line,
            line,
        ],
        out_specs=[pair, whole((count, 2 * HEAD_DIM))],
        out_shape=[
            jax.ShapeDtypeStruct((rows, width), jnp.float32),
            jax.ShapeDtypeStruct((count, 2 * HEAD_DIM), jnp.float32),
        ],
        compiler_params=pltpu.CompilerParams(vmem_limit_bytes=48 * 1024 * 1024),
        cost_estimate=pl.CostEstimate(
            flops=10 * rows * width * count,
            bytes_accessed=8 * rows * width + 16 * bias.size,
            transcendentals=pairs * bias.size,
        ),
        name="attend_back",
    )(queries, grads, keys, keys.T, values, bias, lse, delta)


def on_device(
    hidden_in,
    cotangent,
    lengths,
    weight_qkv,
    first_qkv,
    second_qkv,
    weight_out,
    first_out,
    second_out,
    weight_mlp,
    first_mlp,
    second_mlp,
    norm_gains,
    first_gains,
    second_gains,
):
    tok_rows = hidden_in.shape[2]
    width = hidden_in.shape[3]
    head_count = width // HEAD_DIM
    sides = lax.axis_size("seq")
    columns = lax.axis_size("k")
    members = columns * lax.axis_size("c")
    planes = lax.axis_size("g") * lax.axis_size("h")
    owner_count = planes * members
    blocks_in_side = lax.axis_size("h") * members
    side = lax.axis_index("seq")
    core = lax.axis_index("c")
    packed_index = lax.axis_index("g")
    place = lax.axis_index(("h", "k", "c"))
    own_rows = weight_mlp.shape[0]
    ff_width = weight_mlp.shape[2]
    piece = -(-ff_width // (sides * members * LANES)) * LANES

    gains_low = wide(low(norm_gains))
    gain_one = gains_low[:, :1]
    gain_two = gains_low[:, 1:]
    qkv_low = wide(low(weight_qkv))
    def regrouped(value, outer, inner):
        value = value.reshape(value.shape[0], outer, inner, own_rows).transpose(0, 2, 1, 3)
        return value.reshape(value.shape[0], outer * inner * own_rows)

    mlp_planes = weight_mlp.transpose(1, 0, 2)
    gate_up_chunks, down_chunks = mlp_chunks(mlp_planes, gain_two, side, members, piece)

    def to_members(chunks):
        return exchanged(chunks, ("k", "c")).reshape(members * own_rows, chunks.shape[2])

    incoming = cotangent.reshape(tok_rows, width)
    def own_half(weight):
        half = weight.shape[1] // sides
        return lax.dynamic_slice_in_dim(weight, side * half, half, 1)

    def gathered_group(weight):
        half = weight.shape[1]
        weight = lax.all_gather(weight, GROUP, axis=0, tiled=True)
        return weight.reshape(sides, owner_count * own_rows, half)

    gate_up_blocks = [to_members(gate_up_chunks)]
    plane_rows = [own_half(low(qkv_low * gain_one)), own_half(low(weight_out))]
    split = plane_rows[0].shape[1]
    plane_rows = jnp.concatenate(plane_rows, axis=1)
    plane_rows = lax.all_gather(plane_rows, PLANES, axis=0, tiled=True)
    plane_rows = after(plane_rows, gate_up_blocks[0])
    qkv_halves = gathered_group(plane_rows[:, :split])
    out_halves = gathered_group(plane_rows[:, split:])
    gate_up_blocks.append(next_plane(after(gate_up_blocks[0], plane_rows)))
    down_blocks = [to_members(down_chunks)]
    down_blocks.append(next_plane(down_blocks[0]))
    incoming_columns = doubled(incoming, "k", 1, 0)

    tokens = wide(hidden_in.reshape(tok_rows, width))
    lengths_row = lax.dynamic_index_in_dim(lengths, packed_index, 0, keepdims=False)
    row_numbers = jnp.arange(tok_rows, dtype=jnp.int32)
    query_docs, query_places = doc_places(
        lengths_row, (place * sides + side) * tok_rows + row_numbers
    )
    blocks = jnp.arange(blocks_in_side, dtype=jnp.int32)[None, :] * sides
    blocks = blocks + jnp.arange(sides, dtype=jnp.int32)[:, None]
    key_offsets = (blocks[:, :, None] * tok_rows + row_numbers).reshape(-1)
    key_docs, key_places = doc_places(lengths_row, key_offsets)
    distance = query_places[:, None] - key_places[None, :]
    allowed = (query_docs[:, None] == key_docs[None, :]) & (distance >= 0) & (distance < WINDOW)
    cosine, sine = rope_angles(query_places, HEAD_DIM)
    query_scale = HEAD_DIM ** (-0.5)

    factor_one = lax.rsqrt(jnp.mean(tokens * tokens, axis=-1, keepdims=True) + NORM_EPS)
    normed_one = low(tokens * factor_one)
    normed_one = after(normed_one, incoming_columns, gate_up_blocks[1], down_blocks[1])
    rows = regrouped(normed_one, planes, members)
    projected = jnp.concatenate([dot(rows, half, (1, 0)) for half in qkv_halves], axis=1)
    key_pre = projected[:, width : width + HEAD_DIM]
    value_low = low(projected[:, width + HEAD_DIM :])
    key_low = low(rotate(key_pre, cosine, sine))
    window_kv = spread_ring(jnp.concatenate([key_low, value_low], axis=1))
    window_kv = doubled(window_kv, "c", 1, 1)
    window_kv = window_kv.reshape(SEQ_LEN, 2 * HEAD_DIM)
    gate_up_blocks.append(next_plane(after(gate_up_blocks[1], projected)))
    for _ in range(planes - 4):
        gate_up_blocks.append(next_plane(gate_up_blocks[-1]))
    last = gate_up_blocks[-1]
    gate_up_blocks.append([next_plane(last[:, :piece]), next_plane(last[:, piece:])])
    down_blocks.append(next_plane(after(down_blocks[1], projected)))
    for _ in range(planes - 3):
        down_blocks.append(next_plane(down_blocks[-1]))
    gate_up_own = joined_planes(gate_up_blocks)
    down_own = joined_planes(down_blocks)
    incoming_sides = doubled(after(incoming_columns, window_kv), "seq", 1, 0)
    query_pre = projected[:, :width].reshape(tok_rows, head_count, HEAD_DIM)
    queries = low(rotate(query_pre, cosine[:, None, :], sine[:, None, :]) * query_scale)
    incoming_all = doubled(incoming_sides, "c", 1, incoming_sides.ndim - 2)
    incoming_all = incoming_all.reshape(sides * members * tok_rows, width)
    queries = after(queries.reshape(tok_rows, width), gate_up_blocks[2], down_blocks[2])
    keys_win = window_kv[:, :HEAD_DIM]
    values_win = window_kv[:, HEAD_DIM:]
    bias = jnp.where(allowed.T, 0.0, MASKED_SCORE)
    bias = jnp.concatenate([bias, bias], axis=1)
    attn_low, log_total = attend(queries, keys_win, values_win, bias)
    attn_low = after(attn_low, incoming_sides)
    rows = regrouped(attn_low, planes, members)
    branch = [dot(rows, half, (1, 0)) for half in out_halves]
    middle = tokens + jnp.concatenate(branch, axis=1)

    factor_two = lax.rsqrt(jnp.mean(middle * middle, axis=-1, keepdims=True) + NORM_EPS)
    normed_two = after(low(middle * factor_two), gate_up_blocks[-1][0])
    normed_two_all = lax.all_gather(normed_two, GROUP, axis=0, tiled=True)
    grad_act = low(dot(incoming_all, down_own, (1, 0)))
    gate_up = dot(after(normed_two_all, down_own, incoming_all), gate_up_own, (1, 0))
    activated, glu_back = jax.vjp(glu_values, gate_up[:, :piece], gate_up[:, piece:])
    activated_low = low(activated)
    def to_owners(term):
        return lax.psum_scatter(term, PLANES, scatter_dimension=0, tiled=True)

    down_term = low(dot(incoming_all, activated_low, (0, 0)))
    down_rows = to_owners(down_term)
    grad_gate, grad_up = glu_back(wide(after(grad_act, down_term)))
    grad_gate_up = low(jnp.concatenate([grad_gate, grad_up], axis=1))

    def in_plane(term, *others):
        term = term.reshape(members, own_rows, term.shape[1])
        ours = exchanged(after(term, *others), ("k", "c"))
        return (ours, swapped(ours, "seq"))

    def group_terms(hidden, weight):
        by_core = hidden.reshape(sides * columns, 2, tok_rows, hidden.shape[1])

        def one_core(which):
            rows = lax.dynamic_index_in_dim(by_core, which, 1, keepdims=False)
            return dot(rows.reshape(-1, hidden.shape[1]), weight, (1, 1))

        given = swapped(low(one_core(1 - core)), "c")
        return low(one_core(core) + wide(given)).reshape(sides * columns, tok_rows, width)

    terms = group_terms(grad_gate_up, gate_up_own)
    place = lax.axis_index(CHIPS)
    grad_normed_two = wide(lax.dynamic_index_in_dim(terms, place, 0, keepdims=False))
    arrived = []
    for step in range(1, sides * columns):
        term = lax.dynamic_index_in_dim(terms, place ^ step, 0, keepdims=False)
        if step == sides * columns - 1:
            term = after(term, *arrived)
        arrived.append(lax.ppermute(term, CHIPS, traded(CHIPS, step)))
    late = after(grad_gate_up, *arrived[:-1])
    gate_term = low(dot(normed_two_all, late[:, :piece], (0, 0)))
    up_term = low(dot(normed_two_all, late[:, piece:], (0, 0)))
    grad_normed_two = grad_normed_two + sum(wide(term) for term in arrived)
    grad_normed_two = after(grad_normed_two, gate_term, up_term)

    gate_rows = to_owners(gate_term)
    up_rows = to_owners(up_term)
    attn_all = lax.all_gather(after(attn_low, up_term), GROUP, axis=0, tiled=True)
    grad_middle = (
        wide(incoming)
        + factor_two * grad_normed_two
        - middle * factor_two**3 * jnp.mean(grad_normed_two * middle, axis=-1, keepdims=True)
    )

    shares = sides * members

    def by_column(*terms):
        terms = [term.reshape(tok_rows, shares, term.shape[1] // shares) for term in terms]
        terms = jnp.concatenate(terms, axis=2).transpose(1, 0, 2)
        return exchanged(terms, GROUP)

    def to_rows(total):
        total = exchanged(total.reshape(owner_count, own_rows, -1), OWNERS)
        return low(jnp.sum(wide(total.reshape(planes, members, own_rows, -1)), axis=0))

    def joined(total):
        return wide(total.transpose(1, 0, 2).reshape(own_rows, -1))

    grad_branch_low = low(grad_middle)
    half = width // sides
    grad_mixed = sum(
        dot(grad_branch_low[:, index * half : (index + 1) * half], out_halves[index], (1, 1))
        for index in range(sides)
    )
    grad_mixed_low = regrouped(low(grad_mixed), members, planes)
    delta = (wide(grad_mixed_low) * wide(attn_low)).reshape(tok_rows, head_count, HEAD_DIM)
    delta = jnp.sum(delta, axis=-1).T.reshape(log_total.shape)
    grad_query, grad_window = attend_back(
        queries, grad_mixed_low, keys_win, values_win, bias, log_total, delta
    )
    normed_one_columns = doubled(after(normed_one, grad_normed_two), "k", 1, 0)
    normed_one_sides = doubled(normed_one_columns, "seq", 1, 0)
    grad_window = after(low(grad_window), normed_one_sides)
    branch = low(dot(after(activated_low, grad_window), down_own, (1, 1)))
    normed_one_others = swapped(normed_one_sides, "c")
    grad_window = half_sum(grad_window.reshape(-1, 2, tok_rows, 2 * HEAD_DIM), "c", 1)
    grad_window = grad_window.reshape(sides, -1, columns, tok_rows, 2 * HEAD_DIM)
    grad_window = grad_window.swapaxes(1, 2).reshape(sides * columns, -1, tok_rows, 2 * HEAD_DIM)
    grad_local = wide(half_sum(low(ring_sum(grad_window)), "h", 0))

    mlp_states = (mlp_planes, first_mlp.transpose(1, 0, 2), second_mlp.transpose(1, 0, 2))
    rate_main = 2.0 * D ** (-0.5)

    def mlp_updated(part, pieces, column, outs):
        *outs, gain_dot = mlp_adam(
            part, side, pieces, column, piece, mlp_states, gain_two, rate_main, outs
        )
        return outs, gain_dot

    grad_query = grad_query.reshape(tok_rows, head_count, HEAD_DIM)
    grad_query_pre = rotate(
        grad_query * query_scale, cosine[:, None, :], -sine[:, None, :]
    ).reshape(tok_rows, width)
    grad_key_pre = rotate(grad_local[:, :HEAD_DIM], cosine, -sine)
    grad_proj = low(
        jnp.concatenate([grad_query_pre, grad_key_pre, grad_local[:, HEAD_DIM:]], axis=1)
    )

    all_columns = by_column(after(grad_proj, normed_one_others), grad_branch_low)
    qkv_share = grad_proj.shape[1] // shares
    by_core = all_columns.reshape(sides * columns, 2, tok_rows, -1)[:, :, :, :qkv_share]

    def one_core_total(rows, which):
        columns_there = lax.dynamic_index_in_dim(by_core, which, 1, keepdims=False)
        return dot(rows.reshape(-1, width), columns_there.reshape(-1, qkv_share), (0, 0))

    qkv_total = one_core_total(normed_one_sides, core)
    qkv_total = low(qkv_total + one_core_total(normed_one_others, 1 - core))
    out_columns = all_columns.reshape(shares * tok_rows, -1)[:, qkv_share:]
    out_total = low(dot(attn_all, out_columns, (0, 0)))
    first_pieces = in_plane(jnp.concatenate([down_rows, gate_rows], axis=1), all_columns)
    total = jnp.concatenate([qkv_total, out_total], axis=1)
    up_pieces = in_plane(up_rows, first_pieces[0])
    total = to_rows(after(total, up_pieces[0]))
    branch = lax.psum_scatter(
        after(branch, all_columns), GROUP, scatter_dimension=0, tiled=True
    )
    mlp_outs, _ = mlp_updated(2, first_pieces, 0, ())
    mlp_outs, gate_dot = mlp_updated(0, first_pieces, piece, mlp_outs)
    (grad_mlp, second_new_mlp, new_mlp), up_dot = mlp_updated(1, up_pieces, 0, mlp_outs)
    grad_gain_two = gate_dot + up_dot
    total = doubled(after(total, gate_dot), "seq", 1, 0).reshape(shares, own_rows, -1)
    grad_qkv = joined(total[:, :, :qkv_share])
    grad_out = joined(total[:, :, qkv_share:])
    hidden_out = low(middle + wide(branch)).reshape(1, 1, tok_rows, width)

    half = grad_proj.shape[1] // sides
    grad_normed = sum(
        dot(grad_proj[:, index * half : (index + 1) * half], qkv_halves[index], (1, 1))
        for index in range(sides)
    )
    grad_normed = regrouped(grad_normed, members, planes)
    hidden_grad = (
        grad_middle
        + factor_one * grad_normed
        - tokens * factor_one**3 * jnp.mean(grad_normed * tokens, axis=-1, keepdims=True)
    ).reshape(1, 1, tok_rows, width)

    rate_out = 2.0 * max(1, 6 * D // WINDOW) ** (-0.5)
    rate_gains = 0.4
    grad_gain_one = jnp.sum(qkv_low * grad_qkv, axis=1, keepdims=True)
    grad_qkv = grad_qkv * gain_one
    second_new_qkv, new_qkv = adam_step(weight_qkv, first_qkv, second_qkv, grad_qkv, rate_main)
    second_new_out, new_out = adam_step(weight_out, first_out, second_out, grad_out, rate_out)
    grad_gains = jnp.concatenate([grad_gain_one, grad_gain_two], axis=1)
    second_new_gains, new_gains = adam_step(
        norm_gains, first_gains, second_gains, grad_gains, rate_gains
    )
    return (
        hidden_out,
        hidden_grad,
        grad_qkv,
        second_new_qkv,
        new_qkv,
        grad_out,
        second_new_out,
        new_out,
        grad_mlp.transpose(1, 0, 2),
        second_new_mlp.transpose(1, 0, 2),
        new_mlp.transpose(1, 0, 2),
        grad_gains,
        second_new_gains,
        new_gains,
    )


def solution(mesh):
    seq_count, owner_count = mesh.devices.shape

    def whole(*arguments):
        members = SEQ_LEN // (seq_count * arguments[0].shape[2])
        shape = (seq_count, owner_count // members, members // 4, 2, 2)
        split = Mesh(mesh.devices.reshape(shape), ("seq", "g", "h", "k", "c"))
        acts = P(OWNERS, "seq", None, None)
        flat = P(OWNERS, None)
        planes = P(OWNERS, None, None)
        return jax.shard_map(
            on_device,
            mesh=split,
            in_specs=(acts, acts, P()) + (flat,) * 6 + (planes,) * 3 + (flat,) * 3,
            out_specs=(acts, acts) + (flat,) * 6 + (planes,) * 3 + (flat,) * 3,
            check_vma=False,
        )(*arguments)

    return whole
```
